32 devices in a mesh: dp: 16 (over z, y, x), tensor: 2 (over core).
Axes of the slice: x: 2, y: 2, z: 4, core: 2. Of those that a mesh axis runs over, the one named last changes fastest.
Arguments:
- tokens: bfloat16 [32768, 768], P('dp'), may hold values from -6 to 6
- cotangent: bfloat16 [32768, 768], P('dp'), may hold values from -6 to 6
- long_lengths: int32 [32], P('dp'), may hold values from 129 to 512, as said below
- short_lengths: int32 [128], P('dp'), may hold values from 1 to 128, as said below
- live_counts: int32 [16, 2], P('dp'), may hold values from 1 to 8, as said below
- query_weight: bfloat16 [768, 768], P(None, 'tensor'), may hold values from -0.21875 to 0.21875
- query_bias: float32 [768], P('tensor'), may hold values from -3 to 3
- key_weight: bfloat16 [768, 768], P(None, 'tensor'), may hold values from -0.21875 to 0.21875
- value_weight: bfloat16 [768, 768], P(None, 'tensor'), may hold values from -0.21875 to 0.21875
- value_bias: float32 [768], P('tensor'), may hold values from -3 to 3
- output_weight: bfloat16 [768, 768], P('tensor'), may hold values from -3.5 to 3.5
- output_bias: float32 [768], replicated, may hold values from -3 to 3
- attn_gain: float32 [768], replicated, may hold values from 0.1 to 1.9
- attn_shift: float32 [768], replicated, may hold values from -3 to 3
- inner_weight: bfloat16 [768, 3072], P(None, 'tensor'), may hold values from -0.21875 to 0.21875
- inner_bias: float32 [3072], P('tensor'), may hold values from -3 to 3
- outer_weight: bfloat16 [3072, 768], P('tensor'), may hold values from -0.109375 to 0.109375
- outer_bias: float32 [768], replicated, may hold values from -3 to 3
- ffn_gain: float32 [768], replicated, may hold values from 0.1 to 1.9
- ffn_shift: float32 [768], replicated, may hold values from -3 to 3
Outputs:
- result: bfloat16 [32768, 768], P('dp')
- pooled: float32 [160, 768], P('dp')
- input_grad: float32 [32768, 768], P('dp')
- query_weight_grad: float32 [768, 768], P('dp', 'tensor')
- query_bias_grad: float32 [768], P('tensor')
- key_weight_grad: float32 [768, 768], P('dp', 'tensor')
- value_weight_grad: float32 [768, 768], P('dp', 'tensor')
- value_bias_grad: float32 [768], P('tensor')
- output_weight_grad: float32 [768, 768], P('tensor', 'dp')
- output_bias_grad: float32 [768], P('dp')
- attn_gain_grad: float32 [768], P('dp')
- attn_shift_grad: float32 [768], P('dp')
- inner_weight_grad: float32 [768, 3072], P('dp', 'tensor')
- inner_bias_grad: float32 [3072], P('tensor')
- outer_weight_grad: float32 [3072, 768], P('tensor', 'dp')
- outer_bias_grad: float32 [768], P('dp')
- ffn_gain_grad: float32 [768], P('dp')
- ffn_shift_grad: float32 [768], P('dp')
The draws below stay inside these ranges and needn't reach their ends.
Inputs may be any that keep to these rules, and one draw needn't show every extreme that they name: `long_lengths`: each long slot's length is over 128; slot 0 of some device has exactly 512. `short_lengths`: slot 0 of some device has exactly 128. `live_counts`: row i gives device i's live long slots (column 0, at most 2) and live short slots (column 1, at most 8); the slots below a count are live; some device has all its slots live.
All inputs are finite; a program needn't handle non-finite values.
Results may differ from the reference program's by a relative error of at most 0.02.
Values may be sent and summed in bfloat16 or wider, within the bound.
A program may use at most 192 MiB of HBM per device.

```python
import jax
import jax.numpy as jnp
from jax import lax

D = 768
HEAD_DIM = 64
FF = 3072
LONG = 512
SHORT = 128
NL = 2
NS = 8
TOK_DEV = 2048
TOKENS = 32768
SEQS = 160
N_DP = 16
N_TENSOR = 2


def draw_long_lengths(key, part):
    key = jax.random.fold_in(key, 11)
    first_key, second_key = jax.random.split(key)
    values = jax.random.randint(first_key, (N_DP * NL,), SHORT + 1, LONG + 1)
    chosen = jax.random.randint(second_key, (), 0, N_DP) * NL
    return jnp.where(jnp.arange(N_DP * NL) == chosen, LONG, values).astype(jnp.int32)


def draw_short_lengths(key, part):
    key = jax.random.fold_in(key, 12)
    first_key, second_key = jax.random.split(key)
    values = jax.random.randint(first_key, (N_DP * NS,), 1, SHORT + 1)
    chosen = jax.random.randint(second_key, (), 0, N_DP) * NS
    return jnp.where(jnp.arange(N_DP * NS) == chosen, SHORT, values).astype(jnp.int32)


def draw_live_counts(key, part):
    key = jax.random.fold_in(key, 13)
    first_key, second_key, third_key = jax.random.split(key, 3)
    long_count = jax.random.randint(first_key, (N_DP,), 1, NL + 1)
    short_count = jax.random.randint(second_key, (N_DP,), 1, NS + 1)
    full_device = jax.random.randint(third_key, (), 0, N_DP)
    full_row = jnp.arange(N_DP) == full_device
    long_count = jnp.where(full_row, NL, long_count)
    short_count = jnp.where(full_row, NS, short_count)
    return jnp.stack([long_count, short_count], axis=1).astype(jnp.int32)


def spiked(array, own_key, source, target, shards_of, factor):
    def block_of(position):
        return (jnp.arange(array.shape[position]) // (array.shape[position] // shards_of)).reshape((-1,) + (1,) * (array.ndim - 1 - position))

    one_side = jax.random.permutation(own_key, shards_of)[block_of(target)]
    other_side = (block_of(target) + shards_of // 2) % shards_of
    return jnp.where((block_of(source) == one_side) | (block_of(source) == other_side), factor * array, array)


def levels(rng, dims, shards, smallest, largest):
    loudness = 1.0
    for dim, parts in shards:
        draws = jax.random.uniform(jax.random.fold_in(jax.random.fold_in(rng, 6), dim), (parts,), jnp.float32, smallest / len(shards), largest / len(shards))
        loudness = loudness * jnp.repeat(jnp.exp(draws), dims[dim] // parts).reshape((-1,) + (1,) * (len(dims) - 1 - dim))
    return loudness


def gaussian(stream_key, extent, width, limit, cuts=(), kind=jnp.bfloat16):
    gain = levels(stream_key, extent, cuts, -0.22, 0.18) if cuts else 1.0
    values = jax.random.normal(stream_key, extent, jnp.float32) * width * gain
    return jnp.minimum(jnp.maximum(values, -limit), limit).astype(kind)


def bell_draw_with(own_key, shape, width, most, pieces, heavy, held_as=jnp.bfloat16):
    entries = width * jax.random.normal(own_key, shape, jnp.float32)
    if pieces:
        entries = entries * levels(own_key, shape, pieces, -0.22, 0.18)
    return jnp.clip(spiked(entries, jax.random.fold_in(own_key, 3), *heavy), -most, most).astype(held_as)


def setup_inputs(seed: int = 0) -> dict:
    splits = jax.random.split(jax.random.key(seed), 21)
    tokens = bell_draw_with(splits[0], (TOKENS, D), 1.0, 6.0, ((0, 16),), (0, 1, 16, 2.0))
    cotangent = bell_draw_with(splits[1], (TOKENS, D), 1.0, 6.0, ((0, 16),), (0, 1, 16, 2.0))
    long_lengths = draw_long_lengths(jax.random.fold_in(splits[20], 71), 0)
    short_lengths = draw_short_lengths(jax.random.fold_in(splits[20], 71), 0)
    live_counts = draw_live_counts(jax.random.fold_in(splits[20], 71), 0)
    query_weight = gaussian(splits[5], (D, D), D ** -0.5, 0.21875, ((1, 2),))
    query_bias = gaussian(splits[6], (D,), 0.5, 3.0, ((0, 2),), jnp.float32)
    key_weight = gaussian(splits[7], (D, D), D ** -0.5, 0.21875, ((1, 2),))
    value_weight = gaussian(splits[8], (D, D), D ** -0.5, 0.21875, ((1, 2),))
    value_bias = gaussian(splits[9], (D,), 0.5, 3.0, ((0, 2),), jnp.float32)
    output_weight = gaussian(splits[10], (D, D), (D * 2 // LONG) ** -0.5, 3.5, ((0, 2),))
    output_bias = gaussian(splits[11], (D,), 0.5, 3.0, (), jnp.float32)
    attn_gain = jnp.clip(1.0 + 0.18 * jax.random.normal(splits[12], (D,), jnp.float32), 0.1, 1.9)
    attn_shift = gaussian(splits[13], (D,), 0.5, 3.0, (), jnp.float32)
    inner_weight = gaussian(splits[14], (D, FF), D ** -0.5, 0.21875, ((1, 2),))
    inner_bias = gaussian(splits[15], (FF,), 0.5, 3.0, ((0, 2),), jnp.float32)
    outer_weight = gaussian(splits[16], (FF, D), FF ** -0.5, 0.109375, ((0, 2),))
    outer_bias = gaussian(splits[17], (D,), 0.5, 3.0, (), jnp.float32)
    ffn_gain = jnp.clip(1.0 + 0.18 * jax.random.normal(splits[18], (D,), jnp.float32), 0.1, 1.9)
    ffn_shift = gaussian(splits[19], (D,), 0.5, 3.0, (), jnp.float32)
    return {"tokens": tokens, "cotangent": cotangent, "long_lengths": long_lengths, "short_lengths": short_lengths, "live_counts": live_counts, "query_weight": query_weight, "query_bias": query_bias, "key_weight": key_weight, "value_weight": value_weight, "value_bias": value_bias, "output_weight": output_weight, "output_bias": output_bias, "attn_gain": attn_gain, "attn_shift": attn_shift, "inner_weight": inner_weight, "inner_bias": inner_bias, "outer_weight": outer_weight, "outer_bias": outer_bias, "ffn_gain": ffn_gain, "ffn_shift": ffn_shift}


NORM_EPS = 1e-12
MASKED = -1000000000.0
SCORE_SCALE = 0.125
HIGH = lax.Precision.HIGHEST

@jax.custom_vjp
def low(v):
    return lax.optimization_barrier(v.astype(jnp.bfloat16)).astype(jnp.float32)

@jax.custom_vjp
def low_back(v):
    return v

def low_keep(v):
    return (low(v), None)

def low_pass(kept, grad):
    return (grad,)

def back_keep(v):
    return (v, None)

def back_low(kept, grad):
    return (low(grad),)
low.defvjp(low_keep, low_pass)
low_back.defvjp(back_keep, back_low)

def product(left_side, right_side):
    return jnp.dot(left_side, right_side, precision=HIGH)

def normalize(values, norm_gain, norm_shift):
    centre = values - lax.optimization_barrier(jnp.mean(values, axis=-1, keepdims=True))
    inverse = lax.rsqrt(lax.optimization_barrier(jnp.mean(centre * centre, axis=-1, keepdims=True)) + NORM_EPS)
    return centre * inverse * norm_gain + norm_shift

def attend_bucket(queries, keys_in, values_in, lengths, slot_count, length):
    layout = (slot_count, length, -1, HEAD_DIM)
    scores = jnp.einsum('bqhd,bkhd->bhqk', queries.reshape(layout), keys_in.reshape(layout), precision=HIGH) * SCORE_SCALE
    scores = low_back(scores)
    key_valid = jnp.arange(length)[None, :] < lengths[:, None]
    scores = jnp.where(key_valid[:, None, None, :], scores, MASKED)
    probs_low = low(jax.nn.softmax(scores, axis=-1))
    mixed_heads = jnp.einsum('bhqk,bkhd->bqhd', probs_low, values_in.reshape(layout), precision=HIGH)
    return mixed_heads.reshape(slot_count * length, -1)

def pool_rows(row_values, lengths, slot_count, length):
    blocks = row_values.reshape(slot_count, length, -1)
    key_valid = (jnp.arange(length)[None, :] < lengths[:, None]).astype(row_values.dtype)
    sums = lax.optimization_barrier(jnp.sum(blocks * key_valid[:, :, None], axis=1))
    return sums / jnp.maximum(lengths, 1).astype(row_values.dtype)[:, None]

def forward(token_block, params, long_live, short_live):
    query_weight, query_bias, key_weight, value_weight, value_bias, output_weight, output_bias, attn_gain, attn_shift, inner_weight, inner_bias, outer_weight, outer_bias, ffn_gain, ffn_shift = params
    head_width = D // N_TENSOR
    ffn_width = FF // N_TENSOR
    split_at = NL * LONG
    attn_out = output_bias
    for group_index in range(N_TENSOR):
        head_cols = slice(group_index * head_width, (group_index + 1) * head_width)
        shared = low_back(token_block)
        queries = low(low_back(product(shared, query_weight[:, head_cols]) + query_bias[head_cols]))
        keys_in = low(low_back(product(shared, key_weight[:, head_cols])))
        values_in = low(low_back(product(shared, value_weight[:, head_cols]) + value_bias[head_cols]))
        long_rows = attend_bucket(queries[:split_at], keys_in[:split_at], values_in[:split_at], long_live, NL, LONG)
        short_rows = attend_bucket(queries[split_at:], keys_in[split_at:], values_in[split_at:], short_live, NS, SHORT)
        head_rows = low(low_back(jnp.concatenate([long_rows, short_rows], axis=0)))
        attn_out = attn_out + low(product(head_rows, output_weight[head_cols, :]))
    attn_out = low_back(attn_out)
    hidden_one = normalize(token_block + attn_out, attn_gain, attn_shift)
    hidden_low = low(hidden_one)
    ffn_out = outer_bias
    for group_index in range(N_TENSOR):
        ffn_cols = slice(group_index * ffn_width, (group_index + 1) * ffn_width)
        inner_pre = low_back(product(low_back(hidden_low), inner_weight[:, ffn_cols]) + inner_bias[ffn_cols])
        act_low = low(jax.nn.gelu(inner_pre, approximate=False))
        ffn_out = ffn_out + low(product(act_low, outer_weight[ffn_cols, :]))
    ffn_out = low_back(ffn_out)
    output_full = normalize(hidden_one + ffn_out, ffn_gain, ffn_shift)
    pooled = jnp.concatenate([pool_rows(output_full[:split_at], long_live, NL, LONG), pool_rows(output_full[split_at:], short_live, NS, SHORT)], axis=0)
    return (output_full, pooled)

def reference(tokens, cotangent, long_lengths, short_lengths, live_counts, query_weight, query_bias, key_weight, value_weight, value_bias, output_weight, output_bias, attn_gain, attn_shift, inner_weight, inner_bias, outer_weight, outer_bias, ffn_gain, ffn_shift):
    weights = jax.tree.map(lambda member: member.astype(jnp.float32), (query_weight, query_bias, key_weight, value_weight, value_bias, output_weight, output_bias, attn_gain, attn_shift, inner_weight, inner_bias, outer_weight, outer_bias, ffn_gain, ffn_shift))
    token_blocks = tokens.astype(jnp.float32).reshape(N_DP, TOK_DEV, D)
    cot_blocks = cotangent.astype(jnp.float32).reshape(N_DP, TOK_DEV, D)
    long_blocks = long_lengths.reshape(N_DP, NL)
    short_blocks = short_lengths.reshape(N_DP, NS)

    def scan_step(grad_totals, scan_items):
        token_block, cot_block, long_len, short_len, counts = scan_items
        long_live = jnp.where(jnp.arange(NL) < counts[0], long_len, 0)
        short_live = jnp.where(jnp.arange(NS) < counts[1], short_len, 0)
        output_full, pullback, pooled = jax.vjp(lambda inputs, params: forward(inputs, params, long_live, short_live), token_block, weights, has_aux=True)
        input_grad, weight_grads = pullback(cot_block)
        grad_totals = jax.tree.map(jnp.add, grad_totals, weight_grads)
        return (grad_totals, (output_full, pooled, input_grad))
    zeros = jax.tree.map(jnp.zeros_like, weights)
    totals, (outputs, pooled, input_grads) = lax.scan(scan_step, zeros, (token_blocks, cot_blocks, long_blocks, short_blocks, live_counts))
    return (outputs.reshape(TOKENS, D).astype(jnp.bfloat16), pooled.reshape(SEQS, D), input_grads.reshape(TOKENS, D), totals[0], totals[1], totals[2], totals[3], totals[4], totals[5], totals[6], totals[7], totals[8], totals[9], totals[10], totals[11], totals[12], totals[13], totals[14])
```

```python
import functools

import jax
import jax.numpy as jnp
from jax import lax
from jax.experimental import pallas as pl
from jax.experimental.pallas import tpu as pltpu
from jax.sharding import PartitionSpec as P

HEAD_DIM = 64
LONG = 512
SHORT = 128
PAIR = 128
NORM_EPS = 1e-12
MASKED = -1000000000.0
SCORE_SCALE = 0.125
INV_ROOT_TAU = 0.3989422804014327
ROOT_HALF = 0.7071067811865476
BF = jnp.bfloat16
F32 = jnp.float32
MESH = pl.DeviceIdType.MESH
UNIT = 384
BITS = 4
GROUPS = 1 << BITS

VM = pl.BlockSpec(memory_space=pltpu.VMEM)
SM = pl.BlockSpec(memory_space=pltpu.SMEM)
ANY = pl.BlockSpec(memory_space=pl.ANY)


def params(**more):
    return pltpu.CompilerParams(vmem_limit_bytes=58 << 20, **more)


def dot(a, b):
    return jnp.dot(a, b, preferred_element_type=F32)


def dot_nt(a, b):
    return lax.dot_general(a, b, (((1,), (1,)), ((), ())), preferred_element_type=F32)


def dot_tn(a, b):
    return lax.dot_general(a, b, (((0,), (0,)), ((), ())), preferred_element_type=F32)


def spans(start, unit, size=None):
    return pl.ds(pl.multiple_of(start, unit), unit if size is None else size)


def my_slots(long_ref, short_ref, count_ref):
    tensor = lax.axis_index("tensor")
    n_long, n_short = long_ref.shape[0] // 2, short_ref.shape[0] // 2
    lengths = []
    for ref, n, column in ((long_ref, n_long, 0), (short_ref, n_short, 1)):
        for j in range(n):
            slot = tensor * n + j
            lengths.append(jnp.where(slot < count_ref[0, column], ref[slot], 0))
    return lengths


def my_rows(whole_ref, mine_ref, sem):
    tensor = lax.axis_index("tensor")
    half = mine_ref.shape[0] // 2
    return [
        pltpu.make_async_copy(
            whole_ref.at[pl.ds(pl.multiple_of((2 * k + tensor) * half, half), half)],
            mine_ref.at[pl.ds(k * half, half)], sem.at[k])
        for k in range(2)
    ]


def key_terms(length, count):
    keys = lax.broadcasted_iota(jnp.int32, (1, count), 1)
    scale = jnp.where(length > 0, SCORE_SCALE, 0.0).astype(BF)
    bias = jnp.where((keys < length) | (length <= 0), 0.0, MASKED)
    return scale, bias


def halves():
    return lax.broadcasted_iota(jnp.int32, (1, PAIR), 1) // HEAD_DIM


def attend_kernel(
    long_ref, short_ref, count_ref, tok_ref, wq_ref, wk_ref, wv_ref, bias_ref, qkv_ref, a_ref, lse_ref, wc_ref,
    x_ref, sem,
):
    loads = my_rows(tok_ref, x_ref, sem)
    for load in loads:
        load.start()
    lengths = my_slots(long_ref, short_ref, count_ref)
    rows_all, width = qkv_ref.shape
    pairs = width // (3 * PAIR)
    inner = pairs * PAIR
    for p in range(pairs):
        cols = slice(p * PAIR, (p + 1) * PAIR)
        for k, w_ref in enumerate((wq_ref, wk_ref, wv_ref)):
            wc_ref[:, (3 * p + k) * PAIR:(3 * p + k + 1) * PAIR] = w_ref[:, cols]
    for load in loads:
        load.wait()
    for p in range(pairs):
        cols = slice(p * 384, (p + 1) * 384)
        value = dot(x_ref[...], wc_ref[:, cols])
        bq = bias_ref[0:1, p * PAIR:(p + 1) * PAIR]
        bv = bias_ref[0:1, inner + p * PAIR:inner + (p + 1) * PAIR]
        qkv_ref[:, cols] = (value + jnp.concatenate([bq, jnp.zeros_like(bq), bv], axis=1)).astype(BF)
    half = halves()
    lane = lax.broadcasted_iota(jnp.int32, (1, PAIR), 1)
    lse_ref[...] = jnp.zeros_like(lse_ref)

    def block(row0, count, length, p):
        rows = slice(row0, row0 + count)
        scale, bias = key_terms(length, count)
        qp = qkv_ref[rows, spans(p * 384, 128)] * scale
        kp = qkv_ref[rows, spans(p * 384 + 128, 128)]
        vp = qkv_ref[rows, spans(p * 384 + 256, 128)]
        out = None
        stat = lse_ref[rows, :]
        for h in range(2):
            own = half == h
            s = dot_nt(jnp.where(own, qp, jnp.zeros_like(qp)), kp) + bias
            high = jnp.max(s, axis=1, keepdims=True)
            e = jnp.exp(s - high)
            total = jnp.sum(e, axis=1, keepdims=True)
            o = dot(e.astype(BF), jnp.where(own, vp, jnp.zeros_like(vp))) * (1.0 / total)
            out = o if out is None else out + o
            stat = jnp.where(lane == p * 2 + h, high + jnp.log(total), stat)
        a_ref[rows, spans(p * 128, 128)] = out.astype(BF)
        lse_ref[rows, :] = stat

    def pair(p, _):
        block(0, LONG, lengths[0], p)
        for s in range((rows_all - LONG) // SHORT):
            block(LONG + SHORT * s, SHORT, lengths[1 + s], p)
        return 0

    lax.fori_loop(0, pairs, pair, 0)


def attend(slots, tokens, weights, bias):
    rows, d = tokens.shape[0] // 2, tokens.shape[1]
    inner = weights[0].shape[1]
    shape = jax.ShapeDtypeStruct
    return pl.pallas_call(
        attend_kernel,
        out_shape=(
            shape((rows, 3 * inner), BF), shape((rows, inner), BF), shape((rows, 128), F32), shape((d, 3 * inner), BF),
        ),
        in_specs=[SM, SM, SM, ANY, VM, VM, VM, VM],
        out_specs=(VM,) * 4,
        scratch_shapes=[pltpu.VMEM((rows, d), BF), pltpu.SemaphoreType.DMA((2,))],
        compiler_params=params(),
        cost_estimate=pl.CostEstimate(
            flops=6 * rows * d * inner + 8 * rows * 512 * inner, bytes_accessed=8 << 20, transcendentals=rows * 512 * 6),
        name="attend",
    )(*slots, tokens, *weights, bias)


def norm(v, gain, shift):
    centre = v - jnp.mean(v, axis=-1, keepdims=True)
    inverse = lax.rsqrt(jnp.mean(centre * centre, axis=-1, keepdims=True) + NORM_EPS)
    normed = centre * inverse
    return normed * gain + shift, normed, inverse


def norm_back(e, normed, inverse, gain):
    scaled = e * gain
    plain = jnp.mean(scaled, axis=-1, keepdims=True)
    cross = jnp.mean(scaled * normed, axis=-1, keepdims=True)
    return inverse * (scaled - plain - normed * cross)


def gelu_terms(u):
    t = 1.0 / (1.0 + (0.3275911 * ROOT_HALF) * jnp.abs(u))
    bell = jnp.exp(-0.5 * u * u)
    poly = t * (0.127414796 + t * (-0.142248368 + t * (0.7107068705 + t * (-0.7265760135 + t * 0.5307027145))))
    tail = poly * bell
    cdf = jnp.where(u >= 0.0, 1.0 - tail, tail)
    return u * cdf, cdf + u * bell * INV_ROOT_TAU


def forward_kernel(
    long_ref, short_ref, count_ref, x_ref, cot_ref, ao_ref, ap_ref, woo_ref, wop_ref,
    w1o_hbm, w1p_hbm, w2o_hbm, w2p_hbm, bo_ref, bp_ref,
    attn_bias_ref, a1_ref, s1_ref, ffn_bias_ref, a2_ref, s2_ref,
    result_ref, pooled_ref, n1_ref, r1_ref, h_ref, go_ref, gp_ref, do_ref, dp_ref, df_ref, dr_ref, grad_ref,
    w1o_ref, w1p_ref, w2o_ref, w2p_ref, sem,
):
    step = pl.program_id(0)
    loads = [
        pltpu.make_async_copy(src, dst, sem.at[k]) for k, (src, dst) in enumerate(
            ((w1o_hbm, w1o_ref), (w1p_hbm, w1p_ref), (w2o_hbm, w2o_ref), (w2p_hbm, w2p_ref)))]

    @pl.when(step == 0)
    def _():
        for load in loads:
            load.start()

    lengths = my_slots(long_ref, short_ref, count_ref)
    rows_all = x_ref.shape[0]
    skip = bo_ref.shape[1] - w1o_ref.shape[1]
    width = w1o_ref.shape[1]
    tile = 256
    chunk = 512
    attn_bias, a1, s1, ffn_bias, a2, s2 = (
        ref[...] for ref in (attn_bias_ref, a1_ref, s1_ref, ffn_bias_ref, a2_ref, s2_ref))

    @pl.when(step == 0)
    def _():
        grad_ref[...] = jnp.zeros_like(grad_ref)

    pooled_ref[...] = jnp.zeros_like(pooled_ref)

    def head(i, _):
        rows = spans(i * tile, tile)
        attn = dot(ao_ref[rows, :], woo_ref[...]) + dot(ap_ref[rows, :], wop_ref[...]) + attn_bias
        h1, normed, inverse = norm(x_ref[rows, :].astype(F32) + attn, a1, s1)
        n1_ref[rows, :] = normed
        r1_ref[rows, :] = jnp.broadcast_to(inverse, (tile, 128))
        h_ref[rows, :] = h1.astype(BF)
        return 0

    lax.fori_loop(0, rows_all // tile, head, 0)

    for k, (w1_ref, b1_ref, g_ref, d_ref) in enumerate(
            ((w1o_ref, bo_ref, go_ref, do_ref), (w1p_ref, bp_ref, gp_ref, dp_ref))):
        pl.when(step == 0)(loads[k].wait)

        def inner(c, _, w1_ref=w1_ref, b1_ref=b1_ref, g_ref=g_ref, d_ref=d_ref):
            cols = spans(c * chunk, chunk)
            for i in range(rows_all // tile):
                rows = slice(i * tile, (i + 1) * tile)
                u = dot(h_ref[rows, :], w1_ref[:, cols]) + b1_ref[:, spans(skip + c * chunk, 128, chunk)]
                g, slope = gelu_terms(u)
                g_ref[rows, cols] = g.astype(BF)
                d_ref[rows, cols] = slope.astype(BF)
            return 0

        lax.fori_loop(0, width // chunk, inner, 0)

    @pl.when(step == 0)
    def _():
        loads[2].wait()
        loads[3].wait()

    def tail(i, _):
        rows = spans(i * tile, tile)
        ffn = dot(go_ref[rows, :], w2o_ref[...]) + dot(gp_ref[rows, :], w2p_ref[...]) + ffn_bias
        h1 = n1_ref[rows, :] * a1 + s1
        y, normed, inverse = norm(h1 + ffn, a2, s2)
        result_ref[rows, :] = y.astype(BF)
        place = i * tile + lax.broadcasted_iota(jnp.int32, (tile, 1), 0)

        @pl.when(step == 0)
        def _():
            pooled_ref[0:1, :] += jnp.sum(jnp.where(place < lengths[0], y, 0.0), axis=0, keepdims=True)

        @pl.when(step == 1)
        def _():
            local = lax.broadcasted_iota(jnp.int32, (SHORT, 1), 0)
            per = tile // SHORT
            for k in range(per):
                slot = i * per + k
                length = jnp.where(i == 0, lengths[1 + k], lengths[1 + per + k])
                part = jnp.where(local < length, y[k * SHORT:(k + 1) * SHORT, :], 0.0)
                pooled_ref[pl.ds(slot, 1), :] = jnp.sum(part, axis=0, keepdims=True)

        e = cot_ref[rows, :].astype(F32)
        dr = norm_back(e, normed, inverse, a2)
        low = dr.astype(BF)
        dr_ref[rows, :] = dr
        df_ref[rows, :] = low
        grad_ref[0:1, :] += jnp.sum(low.astype(F32), axis=0, keepdims=True)
        grad_ref[1:2, :] += jnp.sum(e * normed, axis=0, keepdims=True)
        grad_ref[2:3, :] += jnp.sum(e, axis=0, keepdims=True)
        return 0

    lax.fori_loop(0, rows_all // tile, tail, 0)

    @pl.when(step == 0)
    def _():
        pooled_ref[0:1, :] = pooled_ref[0:1, :] / jnp.maximum(lengths[0], 1).astype(F32)

    @pl.when(step == 1)
    def _():
        for s in range(4):
            pooled_ref[s:s + 1, :] = pooled_ref[s:s + 1, :] / jnp.maximum(lengths[1 + s], 1).astype(F32)


def forward(slots, tokens, cot, ao, ap, wo, w1, w2, b1, vectors):
    rows, d = tokens.shape[0] // 2, tokens.shape[1]
    width = w1[0].shape[1]
    blk = rows // 2

    def row(cols):
        return pl.BlockSpec((blk, cols), lambda i: (i, 0))

    def picked(cols):
        return pl.BlockSpec((blk, cols), lambda i: (2 * i + lax.axis_index("tensor"), 0))

    def whole(a):
        return pl.BlockSpec(a.shape, lambda i: (0, 0), pipeline_mode=pl.Buffered(1))

    shape = jax.ShapeDtypeStruct
    return pl.pallas_call(
        forward_kernel,
        grid=(2,),
        out_shape=(
            shape((rows, d), BF), shape((16, d), F32), shape((rows, d), F32), shape((rows, 128), F32),
            shape((rows, d), BF), shape((rows, width), BF), shape((rows, width), BF), shape((rows, width), BF),
            shape((rows, width), BF), shape((rows, d), BF), shape((rows, d), F32), shape((8, d), F32),
        ),
        in_specs=[SM, SM, SM, picked(d), picked(d), row(ao.shape[1]), row(ao.shape[1])]
        + [whole(a) for a in wo] + [ANY] * 4 + [whole(a) for a in (*b1, *vectors)],
        out_specs=(
            row(d), pl.BlockSpec((8, d), lambda i: (i, 0)), row(d), row(128), row(d), row(width), row(width),
            row(width), row(width), row(d), row(d), pl.BlockSpec((8, d), lambda i: (0, 0)),
        ),
        scratch_shapes=[
            pltpu.VMEM((d, width), BF), pltpu.VMEM((d, width), BF), pltpu.VMEM((width, d), BF),
            pltpu.VMEM((width, d), BF), pltpu.SemaphoreType.DMA((4,))],
        compiler_params=params(),
        cost_estimate=pl.CostEstimate(flops=2 * rows * d * (width * 4 + d), bytes_accessed=50 << 20, transcendentals=rows * width * 4),
        name="forward",
    )(*slots, tokens, cot, ao, ap, *wo, *w1, *w2, *b1, *vectors)


def peer(sub, bit):
    me = lax.axis_index("dp")
    group = me // sub
    value = (group // (1 << bit)) % 2
    other = me + (1 - 2 * value) * (sub << bit)
    return value, {"dp": other}


def remote(src, dst, s, r, device):
    return pltpu.make_async_remote_copy(
        src_ref=src, dst_ref=dst, send_sem=s, recv_sem=r, device_id=device, device_id_type=MESH)


class Halving:
    orders = ((0, 1, 2, 3), (1, 0, 2, 3))

    def __init__(self, sub, sums, sends, ins, first, s_sem, r_sem):
        self.links = [peer(sub, bit) for bit in range(BITS)]
        self.partner = {"tensor": 1 - lax.axis_index("tensor")}
        self.sums, self.sends, self.ins, self.first = sums, sends, ins, first
        self.s_sem, self.r_sem = s_sem, r_sem
        self.stage = {}
        self.copy = {}

    def greet(self):
        barrier = pltpu.get_barrier_semaphore()
        for device in [self.partner] + [link[1] for link in self.links]:
            pl.semaphore_signal(barrier, inc=1, device_id=device, device_id_type=MESH)

    def meet(self):
        pl.semaphore_wait(pltpu.get_barrier_semaphore(), BITS + 1)

    def region(self, u, count, bit=None):
        fixed = self.orders[u % 2][:count]
        index = [u]
        for b in reversed(range(BITS)):
            value = self.links[b][0]
            index.append(value if b in fixed else 1 - value if b == bit else slice(None))
        return tuple(index)

    def swap(self, u):
        k = u - self.first[0]
        self.stage[u] = 0
        self.copy[u] = remote(
            self.sends.at[k], self.ins[0].at[k], self.s_sem.at[u, BITS], self.r_sem.at[u, BITS], self.partner)
        self.copy[u].start()

    def resume(self, u, stage):
        self.stage[u] = stage

    def arrive(self, u):
        stage = self.stage[u]
        self.copy[u].wait()
        index = self.region(u, stage)
        brought = self.ins[stage][u - self.first[stage]].astype(F32)
        total = self.sums[index].astype(F32) + brought
        if stage == BITS:
            return total
        self.sums[index] = total.astype(BF)
        return None

    def depart(self, u):
        stage = self.stage[u]
        bit = self.orders[u % 2][stage]
        index = self.region(u, stage, bit)
        self.copy[u] = remote(
            self.sums.at[index], self.ins[stage + 1].at[u - self.first[stage + 1]],
            self.s_sem.at[u, stage], self.r_sem.at[u, stage], self.links[bit][1])
        self.copy[u].start()
        self.stage[u] = stage + 1

    def move(self, *units):
        for u in units:
            self.arrive(u)
            self.depart(u)


def halving_scratch(first, units):
    shapes = ((2, 2, 2, 2), (2, 2, 2), (2, 2), (2,), ())
    return [pltpu.VMEM((max(units - f, 1), *s, 48, UNIT), BF) for f, s in zip(first, shapes)] + [
        pltpu.SemaphoreType.DMA((units, BITS + 1)), pltpu.SemaphoreType.DMA((units, BITS + 1))]


def weight_grad(out_ref, units, left_ref, right_ref, cols):
    def part(i, _):
        value = dot_tn(left_ref[:, spans(i * UNIT, UNIT)], right_ref[:, cols]).astype(BF)
        for k, u in enumerate(units):
            out_ref[u, i] = value[:, k * UNIT:(k + 1) * UNIT].reshape(2, 2, 2, 48, UNIT)
        return 0

    lax.fori_loop(0, left_ref.shape[1] // UNIT, part, 0)


FIRST_A = (0, 0, 0, 0, 0)
STAGES_A = (3, 3, 2, 2, 1, 1, 0, 0)


def ffn_back_kernel(
    sub, df_hbm, h_hbm, dr_hbm, gp_hbm, go_hbm, dp_hbm, do_hbm, w1p_hbm, w1o_hbm, w2p_hbm, w2o_hbm,
    sums_out, dh_ref, bp_ref, bo_ref,
    df_ref, h_ref, g_ref, slope_ref, w1_ref, w2_ref, u_ref, sums_ref, send_ref,
    in0_ref, in1_ref, in2_ref, in3_ref, in4_ref, s_sem, r_sem, load_sem, out_sem,
):
    rows_all, d = df_ref.shape
    width = w1_ref.shape[2]
    chunk = 2 * UNIT
    chunks = width // chunk
    tile = 256
    red = Halving(sub, sums_ref, send_ref, (in0_ref, in1_ref, in2_ref, in3_ref, in4_ref), FIRST_A, s_sem, r_sem)
    red.greet()
    loads = {}

    def load(name, src, dst):
        loads[name] = pltpu.make_async_copy(src, dst, load_sem.at[len(loads)])
        loads[name].start()

    def need(*names):
        for name in names:
            loads.pop(name).wait()
            loads[name + "!"] = None

    load("df", df_hbm, df_ref)
    for c in range(chunks):
        cols = pl.ds(c * chunk, chunk)
        for k, hbm in enumerate((gp_hbm, go_hbm)):
            load(f"g{k}{c}", hbm.at[:, cols], g_ref.at[k, :, cols])
    load("h", h_hbm, h_ref)
    for c in range(chunks):
        cols = pl.ds(c * chunk, chunk)
        for k, (w2_hbm, d_hbm) in enumerate(((w2p_hbm, dp_hbm), (w2o_hbm, do_hbm))):
            load(f"w{k}{c}", w2_hbm.at[cols], w2_ref.at[k, cols])
            load(f"d{k}{c}", d_hbm.at[:, cols], slope_ref.at[k, :, cols])
    load("dr", dr_hbm, dh_ref)
    for k, w1_hbm in enumerate((w1p_hbm, w1o_hbm)):
        load(f"i{k}", w1_hbm, w1_ref.at[k])

    bp_ref[...] = jnp.zeros_like(bp_ref)
    bo_ref[...] = jnp.zeros_like(bo_ref)
    need("df")
    for c in range(chunks):
        cols = slice(c * chunk, (c + 1) * chunk)
        units = (2 * c, 2 * c + 1)
        for k, out_ref in enumerate((send_ref, sums_ref)):
            need(f"g{k}{c}")
            weight_grad(out_ref, units, df_ref, g_ref.at[k], cols)
            if k == 0:
                if c == 0:
                    red.meet()
                for u in units:
                    red.swap(u)
        if c == 1:
            red.move(0, 1)
    need("h")
    for c in range(chunks):
        cols = slice(c * chunk, (c + 1) * chunk)
        units = (2 * chunks + 2 * c, 2 * chunks + 2 * c + 1)
        for k, (out_ref, bias_ref) in enumerate(((send_ref, bp_ref), (sums_ref, bo_ref))):
            need(f"w{k}{c}", f"d{k}{c}")

            def part(i, _, k=k, bias_ref=bias_ref, cols=cols):
                rows = spans(i * tile, tile)
                du = (dot_nt(df_ref[rows, :], w2_ref[k, cols, :]) * slope_ref[k, rows, cols].astype(F32)).astype(BF)
                u_ref[k, rows, cols] = du
                bias_ref[0:1, cols] += jnp.sum(du.astype(F32), axis=0, keepdims=True)
                return 0

            lax.fori_loop(0, rows_all // tile, part, 0)
            weight_grad(out_ref, units, h_ref, u_ref.at[k], cols)
            if k == 0:
                for u in units:
                    red.swap(u)
            if (c, k) == (0, 0):
                red.move(2, 3)
            if (c, k) == (1, 0):
                red.move(0, 1)
    need("dr", "i0", "i1")

    def back(i, _):
        rows = spans(i * tile, tile)
        dh_ref[rows, :] += dot_nt(u_ref[0, rows, :], w1_ref[0]) + dot_nt(u_ref[1, rows, :], w1_ref[1])
        return 0

    red.move(4, 5)
    lax.fori_loop(0, rows_all // tile // 2, back, 0)
    red.move(2, 3)
    red.move(0, 1)
    lax.fori_loop(rows_all // tile // 2, rows_all // tile, back, 0)
    for u in range(4 * chunks):
        red.arrive(u)
    outs = pltpu.make_async_copy(sums_ref, sums_out, out_sem)
    outs.start()
    outs.wait()


def ffn_back(sub, df, h, dr, g, slope, w1, w2):
    rows, d = df.shape
    width = w1[0].shape[1]
    units = 2 * width // UNIT
    shape = jax.ShapeDtypeStruct
    return pl.pallas_call(
        functools.partial(ffn_back_kernel, sub),
        out_shape=(
            shape((units, 2, 2, 2, 2, 48, UNIT), BF), shape((rows, d), F32), shape((8, width), F32), shape((8, width), F32),
        ),
        in_specs=[ANY] * 11,
        out_specs=(ANY, VM, VM, VM),
        scratch_shapes=[
            pltpu.VMEM((rows, d), BF), pltpu.VMEM((rows, d), BF), pltpu.VMEM((2, rows, width), BF),
            pltpu.VMEM((2, rows, width), BF), pltpu.VMEM((2, d, width), BF), pltpu.VMEM((2, width, d), BF),
            pltpu.VMEM((2, rows, width), BF),
            pltpu.VMEM((units, 2, 2, 2, 2, 48, UNIT), BF), pltpu.VMEM((units, 2, 2, 2, 2, 48, UNIT), BF),
            *halving_scratch(FIRST_A, units), pltpu.SemaphoreType.DMA((20,)), pltpu.SemaphoreType.DMA,
        ],
        compiler_params=params(collective_id=1, has_side_effects=True),
        name="ffn_back",
    )(df, h, dr, *g, *slope, *w1, *w2)


FIRST_B = (8, 6, 4, 2, 0)


def attn_back_kernel(
    sub, long_ref, short_ref, count_ref, sums_hbm, dh_hbm, n1_hbm, r1_hbm, gain_ref, tok_hbm, qkvp_hbm, qkvo_hbm,
    ap_hbm, ao_hbm, lsep_hbm, lseo_hbm, wop_hbm, woo_hbm, wcp_hbm, wco_hbm, grad2_ref, b1p_ref, b1o_ref,
    outer_ref, inner_ref, q_ref, k_ref, v_ref, output_ref, dx_out, vec_out,
    dx_ref, n1_ref, r1_ref, x_ref, qkv_ref, a_ref, lse_ref, wo_ref, wc_ref, low_ref, da_ref, dqkv_ref,
    grad_ref, vsend_ref, vec_ref, vin_ref, sums_ref, send_ref,
    in0_ref, in1_ref, in2_ref, in3_ref, in4_ref, s_sem, r_sem, vs_sem, vr_sem, load_sem, out_sem, swap_sem,
):
    rows_all, d = dx_ref.shape
    pairs = a_ref.shape[2] // PAIR
    tile = 256
    half = halves()
    lane = lax.broadcasted_iota(jnp.int32, (1, PAIR), 1)
    lengths = my_slots(long_ref, short_ref, count_ref)
    tensor = lax.axis_index("tensor")
    red = Halving(sub, sums_ref, send_ref, (in0_ref, in1_ref, in2_ref, in3_ref, in4_ref), FIRST_B, s_sem, r_sem)
    red.greet()
    loads = []

    def load(src, dst):
        loads.append(pltpu.make_async_copy(src, dst, load_sem.at[len(loads)]))
        loads[-1].start()
        return loads[-1]

    handed = len(STAGES_A)
    pieces = []
    for u, stage in enumerate(STAGES_A):
        red.resume(u, stage)
        index = red.region(u, stage)
        pieces.append(load(sums_hbm.at[index], sums_ref.at[index]))
    norms = [load(dh_hbm, dx_ref), load(n1_hbm, n1_ref), load(r1_hbm, r1_ref)]
    heads = [load(ap_hbm, a_ref.at[0]), load(ao_hbm, a_ref.at[1]), load(wop_hbm, wo_ref.at[0]), load(woo_hbm, wo_ref.at[1])]
    heads += [load(qkvp_hbm, qkv_ref.at[0]), load(qkvo_hbm, qkv_ref.at[1]), load(lsep_hbm, lse_ref.at[0]), load(lseo_hbm, lse_ref.at[1])]
    rows_in = my_rows(tok_hbm, x_ref, load_sem.at[pl.ds(len(loads), 2)])
    for copy in rows_in:
        copy.start()
    loads += rows_in
    last = [load(wcp_hbm, wc_ref.at[0]), load(wco_hbm, wc_ref.at[1])]

    for piece in pieces:
        piece.wait()
    red.meet()
    for u in range(handed):
        red.depart(u)
    final = {}

    def finish(*units):
        for u in units:
            value = red.arrive(u)
            if u < 4:
                outer_ref[u * UNIT:(u + 1) * UNIT, :] = value.T
            elif u < 8:
                inner_ref[:, (u - 4) * UNIT:(u - 3) * UNIT] = value
            elif u == 8:
                output_ref[...] = value.T
            else:
                for i, ref in enumerate((q_ref, k_ref, v_ref)):
                    ref[:, (u - 9) * PAIR:(u - 8) * PAIR] = value[:, i * PAIR:(i + 1) * PAIR]

    for copy in norms:
        copy.wait()
    grad_ref[...] = jnp.zeros_like(grad_ref)

    def first(i, _):
        rows = spans(i * tile, tile)
        e, normed = dx_ref[rows, :], n1_ref[rows, :]
        dr = norm_back(e, normed, r1_ref[rows, 0:1], gain_ref[...])
        low = dr.astype(BF)
        dx_ref[rows, :] = dr
        low_ref[rows, :] = low
        grad_ref[0:1, :] += jnp.sum(low.astype(F32), axis=0, keepdims=True)
        grad_ref[1:2, :] += jnp.sum(e * normed, axis=0, keepdims=True)
        grad_ref[2:3, :] += jnp.sum(e, axis=0, keepdims=True)
        return 0

    lax.fori_loop(0, rows_all // tile, first, 0)
    for copy in heads + rows_in:
        copy.wait()
    weight_grad(send_ref, (0,), low_ref, a_ref.at[0], slice(0, UNIT))
    red.swap(8)
    weight_grad(sums_ref, (8,), low_ref, a_ref.at[1], slice(0, UNIT))

    def lift(i, _):
        rows = spans(i * tile, tile)
        for k in range(2):
            da_ref[k, rows, :] = dot_nt(low_ref[rows, :], wo_ref[k]).astype(BF)
        return 0

    lax.fori_loop(0, rows_all // tile, lift, 0)
    red.move(4, 5)
    red.move(2, 3)
    finish(0, 1)
    red.move(6, 7)

    def block(row0, count, length, k, p):
        rows = slice(row0, row0 + count)
        scale, bias = key_terms(length, count)
        qp = qkv_ref[k, rows, p * 384:p * 384 + 128] * scale
        kp = qkv_ref[k, rows, p * 384 + 128:p * 384 + 256]
        vp = qkv_ref[k, rows, p * 384 + 256:p * 384 + 384]
        dap = da_ref[k, rows, p * 128:p * 128 + 128]
        prod = dap.astype(F32) * a_ref[k, rows, p * 128:p * 128 + 128].astype(F32)
        ks = kp * scale
        stat = lse_ref[k, rows, :]
        dq = dk = dv = None
        for h in range(2):
            own = half == h
            zero = jnp.zeros_like(qp)
            qh, dah = jnp.where(own, qp, zero), jnp.where(own, dap, zero)
            delta = jnp.sum(jnp.where(own, prod, 0.0), axis=1, keepdims=True)
            lse = jnp.sum(jnp.where(lane == p * 2 + h, stat, 0.0), axis=1, keepdims=True)
            prob = jnp.exp(dot_nt(qh, kp) + bias - lse)
            ds = (prob * (dot_nt(dah, vp) - delta)).astype(BF)
            dvh = dot_tn(prob.astype(BF), dah)
            dkh = dot_tn(ds, qh)
            dqh = dot(ds, jnp.where(own, ks, zero))
            dq = dqh if dq is None else dq + dqh
            dk = dkh if dk is None else dk + dkh
            dv = dvh if dv is None else dv + dvh
        dqkv_ref[k, rows, p * 384:p * 384 + 128] = dq.astype(BF)
        dqkv_ref[k, rows, p * 384 + 128:p * 384 + 256] = dk.astype(BF)
        dqkv_ref[k, rows, p * 384 + 256:p * 384 + 384] = dv.astype(BF)

    after = {
        (0, 0): lambda: red.move(8, 4, 5),
        (0, 1): lambda: finish(2, 3),
        (1, 0): lambda: red.move(6, 7, 8, 9),
        (1, 1): lambda: finish(4, 5),
        (2, 0): lambda: red.move(6, 7, 8, 9, 10),
        (2, 1): lambda: None,
    }
    for p in range(pairs):
        for k, out_ref in enumerate((send_ref, sums_ref)):
            def half_pair(k, p=p):
                block(0, LONG, lengths[0], k, p)
                for s in range((rows_all - LONG) // SHORT):
                    block(LONG + SHORT * s, SHORT, lengths[1 + s], k, p)

            half_pair(k)
            cols = slice(p * 384, (p + 1) * 384)
            weight_grad(out_ref, (1 + p if k == 0 else 9 + p,), x_ref, dqkv_ref.at[k], cols)
            if k == 0:
                red.swap(9 + p)
            after[p, k]()

    bias_rows = ((b1p_ref, vsend_ref), (b1o_ref, vec_ref.at[0]))
    for k, (b1_ref, ref) in enumerate(bias_rows):
        ref[...] = jnp.zeros(ref.shape, F32)
        ref[0:3, :] = grad_ref[0:3, :]
        ref[3:6, :] = grad2_ref[0:3, :]
        ref[6:7, :] = b1_ref[0:1, 0:d]
        ref[7:8, :] = b1_ref[0:1, d:2 * d]
        sums = jnp.sum(dqkv_ref[k].astype(F32), axis=0, keepdims=True)
        ref[8:9, :] = sums[:, 0:d]
        ref[9:10, 0:sums.shape[1] - d] = sums[:, d:]
    vnow = remote(vsend_ref, vin_ref.at[BITS], vs_sem.at[BITS], vr_sem.at[BITS], red.partner)
    vnow.start()
    red.move(11)
    for copy in last:
        copy.wait()

    def back(i, _):
        rows = spans(i * tile, tile)
        dx_ref[rows, :] += dot_nt(dqkv_ref[1, rows, :], wc_ref[1]) + dot_nt(dqkv_ref[0, rows, :], wc_ref[0])
        return 0

    def vmove(step):
        vec_ref[step + 1] = vec_ref[step] + vin_ref[step]

    tiles = rows_all // tile
    outs = []
    span = rows_all // 2
    for i in range(tiles):
        lax.fori_loop(i, i + 1, back, 0)
        if i * tile % span == span - tile:
            g = i * tile // span
            here = dx_ref.at[pl.ds(g * span, span)]
            there = dx_out.at[pl.ds(pl.multiple_of((2 * g + tensor) * span, span), span)]
            outs.append(pltpu.make_async_copy(here, there, out_sem.at[g]))
            outs.append(remote(here, there, swap_sem.at[0, g], swap_sem.at[1, g], red.partner))
            outs[-1].start()
            outs[-2].start()
        if i < BITS:
            vnow.wait()
            if i == 0:
                vec_ref[0] = vec_ref[0] + vin_ref[BITS]
            else:
                vmove(i - 1)
            vnow = remote(vec_ref.at[i], vin_ref.at[i], vs_sem.at[i], vr_sem.at[i], red.links[i][1])
            vnow.start()
        if i == 0:
            red.move(10)
        if i == 1:
            red.move(8, 9, 11)
        if i == 2:
            finish(6, 7)
            red.move(10)
    red.move(11, 9)
    finish(8)
    red.move(10, 11)
    vnow.wait()
    vec_out[...] = vec_ref[BITS - 1] + vin_ref[BITS - 1]
    finish(9, 10, 11)
    for copy in outs:
        copy.wait()


def attn_back(sub, slots, sums, dh, n1, r1, gain, tokens, qkv, a, lse, wo, wc, grad2, b1):
    rows, d = dh.shape
    inner = a[0].shape[1]
    ff = b1[0].shape[1]
    units = sums.shape[0] + 1 + 3 * inner // UNIT
    shape = jax.ShapeDtypeStruct
    return pl.pallas_call(
        functools.partial(attn_back_kernel, sub),
        out_shape=(
            shape((ff, 48), F32), shape((48, ff), F32), shape((48, inner), F32), shape((48, inner), F32),
            shape((48, inner), F32), shape((inner, 48), F32), shape((2 * rows, d), F32), shape((16, d), F32),
        ),
        in_specs=[SM, SM, SM, ANY, ANY, ANY, ANY, VM] + [ANY] * 11 + [VM, VM, VM],
        out_specs=(VM, VM, VM, VM, VM, VM, ANY, VM),
        scratch_shapes=[
            pltpu.VMEM((rows, d), F32), pltpu.VMEM((rows, d), F32), pltpu.VMEM((rows, 128), F32),
            pltpu.VMEM((rows, d), BF), pltpu.VMEM((2, rows, 3 * inner), BF), pltpu.VMEM((2, rows, inner), BF),
            pltpu.VMEM((2, rows, 128), F32), pltpu.VMEM((2, inner, d), BF), pltpu.VMEM((2, d, 3 * inner), BF),
            pltpu.VMEM((rows, d), BF), pltpu.VMEM((2, rows, inner), BF), pltpu.VMEM((2, rows, 3 * inner), BF),
            pltpu.VMEM((8, d), F32), pltpu.VMEM((16, d), F32), pltpu.VMEM((BITS, 16, d), F32), pltpu.VMEM((BITS + 1, 16, d), F32),
            pltpu.VMEM((units, 2, 2, 2, 2, 48, UNIT), BF), pltpu.VMEM((4, 2, 2, 2, 2, 48, UNIT), BF),
            *halving_scratch(FIRST_B, units), pltpu.SemaphoreType.DMA((BITS + 1,)), pltpu.SemaphoreType.DMA((BITS + 1,)),
            pltpu.SemaphoreType.DMA((32,)), pltpu.SemaphoreType.DMA((2,)), pltpu.SemaphoreType.DMA((2, 2)),
        ],
        compiler_params=params(collective_id=2, has_side_effects=True),
        name="attn_back",
    )(*slots, sums, dh, n1, r1, gain, tokens, *qkv, *a, *lse, *wo, *wc, grad2, *b1)


def per_device(
    dp_size, tokens, cotangent, long_lengths, short_lengths, live_counts, query_weight, query_bias, key_weight,
    value_weight, value_bias, output_weight, output_bias, attn_gain, attn_shift, inner_weight, inner_bias,
    outer_weight, outer_bias, ffn_gain, ffn_shift,
):
    d = tokens.shape[1]
    sub = dp_size // GROUPS
    tensor = lax.axis_index("tensor")
    dp = lax.axis_index("dp")
    n_long, n_short = long_lengths.shape[0], short_lengths.shape[0]
    rows = n_long // 2 * LONG
    pairs = query_weight.shape[1] // PAIR
    slots = (long_lengths, short_lengths, live_counts)

    def both(own, other):
        return jnp.where(tensor == 0, own, other), jnp.where(tensor == 0, other, own)

    def swap(a):
        return lax.ppermute(a, "tensor", [(0, 1), (1, 0)])

    bias_own = jnp.concatenate([query_bias, value_bias, inner_bias]).reshape(1, -1)
    weights = (query_weight, key_weight, value_weight)
    weights_other = tuple(swap(w) for w in weights)
    bias_other = swap(bias_own)
    wo_other, w1_other, w2_other = swap(output_weight), swap(inner_weight), swap(outer_weight)

    qkv_own, a_own, lse_own, wc_own = attend(slots, tokens, weights, bias_own)
    qkv_other, a_other, lse_other, wc_other = attend(slots, tokens, weights_other, bias_other)
    vectors = [a.reshape(1, d) for a in (output_bias, attn_gain, attn_shift, outer_bias, ffn_gain, ffn_shift)]
    (result, pooled, n1, r1, h, g_own, g_other, slope_own, slope_other, df, dr, grad2) = forward(
        slots, tokens, cotangent, a_own, a_other, (output_weight, wo_other), (inner_weight, w1_other),
        (outer_weight, w2_other), (bias_own, bias_other), vectors)
    result_other = swap(result)
    pooled_own = jnp.concatenate([pooled[:n_long // 2], pooled[8:8 + n_short // 2]])
    pooled_other = swap(pooled_own)
    sums, dh, b1p, b1o = ffn_back(
        sub, df, h, dr, (g_other, g_own), (slope_other, slope_own), (w1_other, inner_weight), (w2_other, outer_weight))
    d_outer, d_inner, d_q, d_k, d_v, d_output, dx, total = attn_back(
        sub, slots, sums, dh, n1, r1, vectors[1], tokens, (qkv_other, qkv_own), (a_other, a_own),
        (lse_other, lse_own), (wo_other, output_weight), (wc_other, wc_own), grad2, (b1p, b1o))

    if sub > 1:
        groups = [[g * sub + i for i in range(sub)] for g in range(GROUPS)]

        def rest(a, dim):
            return lax.psum_scatter(a, "dp", scatter_dimension=dim, axis_index_groups=groups, tiled=True)

        d_outer, d_output = rest(d_outer, 1), rest(d_output, 1)
        d_inner, d_q, d_k, d_v = (rest(a, 0) for a in (d_inner, d_q, d_k, d_v))
        total = lax.psum(total, "dp", axis_index_groups=groups)
    mine_of = lax.dynamic_slice_in_dim(total, dp * (d // dp_size), d // dp_size, 1)
    d_b1 = total[6:8].reshape(-1)
    d_bc = total[8:10].reshape(-1)[:pairs * 384].reshape(pairs, 3, PAIR)

    first, second = both(result, result_other)
    result_all = jnp.concatenate([first[:rows], second[:rows], first[rows:], second[rows:]], axis=0)
    pooled_both = both(pooled_own, pooled_other)
    pooled_all = jnp.concatenate(
        [p[:n_long // 2] for p in pooled_both] + [p[n_long // 2:] for p in pooled_both])
    return (
        result_all, pooled_all, dx, d_q, d_bc[:, 0].reshape(-1), d_k, d_v, d_bc[:, 2].reshape(-1), d_output,
        mine_of[0], mine_of[1], mine_of[2], d_inner, d_b1, d_outer, mine_of[3], mine_of[4], mine_of[5],
    )


def solution(mesh):
    in_specs = (
        P("dp", None), P("dp", None), P("dp"), P("dp"), P("dp", None), P(None, "tensor"), P("tensor"),
        P(None, "tensor"), P(None, "tensor"), P("tensor"), P("tensor", None), P(), P(), P(), P(None, "tensor"),
        P("tensor"), P("tensor", None), P(), P(), P(),
    )
    out_specs = (
        P("dp", None), P("dp", None), P("dp", None), P("dp", "tensor"), P("tensor"), P("dp", "tensor"),
        P("dp", "tensor"), P("tensor"), P("tensor", "dp"), P("dp"), P("dp"), P("dp"), P("dp", "tensor"),
        P("tensor"), P("tensor", "dp"), P("dp"), P("dp"), P("dp"),
    )
    return jax.shard_map(
        functools.partial(per_device, mesh.shape["dp"]), mesh=mesh, in_specs=in_specs, out_specs=out_specs,
        check_vma=False)
```

```python
import functools

import jax
import jax.numpy as jnp
from jax import lax
from jax.experimental import pallas as pl
from jax.experimental.pallas import tpu as pltpu
from jax.sharding import PartitionSpec as P

HEAD_DIM = 64
LONG = 512
SHORT = 128
PAIR = 128
NORM_EPS = 1e-12
MASKED = -1000000000.0
SCORE_SCALE = 0.125
INV_ROOT_TAU = 0.3989422804014327
ROOT_HALF = 0.7071067811865476
BF = jnp.bfloat16
F32 = jnp.float32
MESH = pl.DeviceIdType.MESH
UNIT = 384
BITS = 4
GROUPS = 1 << BITS

VM = pl.BlockSpec(memory_space=pltpu.VMEM)
SM = pl.BlockSpec(memory_space=pltpu.SMEM)
ANY = pl.BlockSpec(memory_space=pl.ANY)


def params(**more):
    return pltpu.CompilerParams(vmem_limit_bytes=58 << 20, **more)


def dot(a, b):
    return jnp.dot(a, b, preferred_element_type=F32)


def dot_nt(a, b):
    return lax.dot_general(a, b, (((1,), (1,)), ((), ())), preferred_element_type=F32)


def dot_tn(a, b):
    return lax.dot_general(a, b, (((0,), (0,)), ((), ())), preferred_element_type=F32)


def spans(start, unit, size=None):
    return pl.ds(pl.multiple_of(start, unit), unit if size is None else size)


def my_slots(long_ref, short_ref, count_ref):
    tensor = lax.axis_index("tensor")
    n_long, n_short = long_ref.shape[0] // 2, short_ref.shape[0] // 2
    lengths = []
    for ref, n, column in ((long_ref, n_long, 0), (short_ref, n_short, 1)):
        for j in range(n):
            slot = tensor * n + j
            lengths.append(jnp.where(slot < count_ref[0, column], ref[slot], 0))
    return lengths


def my_rows(whole_ref, mine_ref, sem):
    tensor = lax.axis_index("tensor")
    half = mine_ref.shape[0] // 2
    return [
        pltpu.make_async_copy(
            whole_ref.at[pl.ds(pl.multiple_of((2 * k + tensor) * half, half), half)],
            mine_ref.at[pl.ds(k * half, half)], sem.at[k])
        for k in range(2)
    ]


def key_terms(length, count):
    keys = lax.broadcasted_iota(jnp.int32, (1, count), 1)
    scale = jnp.where(length > 0, SCORE_SCALE, 0.0).astype(BF)
    bias = jnp.where((keys < length) | (length <= 0), 0.0, MASKED)
    return scale, bias


def halves():
    return lax.broadcasted_iota(jnp.int32, (1, PAIR), 1) // HEAD_DIM


class Loads:
    def __init__(self, sem):
        self.sem, self.count, self.open = sem, 0, {}

    def __call__(self, name, src, dst):
        copy = pltpu.make_async_copy(src, dst, self.sem.at[self.count])
        self.count += 1
        self.open.setdefault(name, []).append(copy)
        copy.start()

    def need(self, *names):
        for name in names:
            for copy in self.open.pop(name):
                copy.wait()

    def drain(self):
        self.need(*list(self.open))


def load_rows(loads, name, whole_ref, mine_ref):
    tensor = lax.axis_index("tensor")
    half = mine_ref.shape[0] // 2
    for k in range(2):
        loads(name, whole_ref.at[pl.ds(pl.multiple_of((2 * k + tensor) * half, half), half)],
              mine_ref.at[pl.ds(k * half, half)])


def slot_parts(kind, lengths):
    if kind == 0:
        return [(slice(0, LONG), *key_terms(lengths[0], LONG))]
    return [
        (slice(LONG + SHORT * s, LONG + SHORT * (s + 1)), *key_terms(length, SHORT))
        for s, length in enumerate(lengths[1:])]


def stack(values):
    return values[0] if len(values) == 1 else jnp.concatenate(values, axis=0)


def keep(own, value, other=None):
    return jnp.where(own, value, jnp.zeros_like(value) if other is None else other)


def attend_kernel(
    long_ref, short_ref, count_ref, tok_hbm, wq_hbm, wk_hbm, wv_hbm, wo_hbm, w1_hbm, w2_hbm, bq_ref, bv_ref, b1_ref,
    qkv_out, a_out, lse_out, wc_out, wo_other, w1_other, w2_other, b1_other,
    qkv_ref, a_ref, lse_ref, wc_ref, x_ref, bq_other, bv_other, sem, s_sem, r_sem,
):
    width = qkv_ref.shape[2]
    pairs = width // (3 * PAIR)
    partner = {"tensor": 1 - lax.axis_index("tensor")}
    barrier = pltpu.get_barrier_semaphore()
    pl.semaphore_signal(barrier, inc=1, device_id=partner, device_id_type=MESH)
    loads = Loads(sem)
    load_rows(loads, "x", tok_hbm, x_ref)
    blocks = []
    for p in range(pairs):
        for j, w_hbm in enumerate((wq_hbm, wk_hbm, wv_hbm)):
            at = (3 * p + j) * PAIR
            blocks.append((w_hbm.at[:, p * PAIR:(p + 1) * PAIR], slice(at, at + PAIR)))
    for src, cols in blocks:
        loads("x", src, wc_ref.at[1, :, cols])
    lengths = my_slots(long_ref, short_ref, count_ref)
    half = halves()
    slots = [slot_parts(kind, lengths) for kind in range(2)]

    def project(k, bq, bv):
        parts = []
        for p in range(pairs):
            cols = slice(p * PAIR, (p + 1) * PAIR)
            parts += [bq[:, cols], jnp.zeros((1, PAIR), F32), bv[:, cols]]
        qkv_ref[k] = (dot(x_ref[...], wc_ref[k]) + jnp.concatenate(parts, axis=1)).astype(BF)
        loads("out", qkv_ref.at[k], qkv_out.at[k])
        loads("out", wc_ref.at[k], wc_out.at[k])

    def attention(k):
        def scores(kind, p, h):
            out = []
            for rows, scale, key_bias in slots[kind]:
                q = qkv_ref[k, rows, p * 384:p * 384 + 128] * scale
                out.append(dot_nt(keep(half == h, q), qkv_ref[k, rows, p * 384 + 128:p * 384 + 256]) + key_bias)
            return stack(out)

        def mix(kind, p, h, e):
            out = []
            for i, (rows, _, _) in enumerate(slots[kind]):
                v = qkv_ref[k, rows, p * 384 + 256:p * 384 + 384]
                count = rows.stop - rows.start
                out.append(dot(e[i * count:(i + 1) * count], keep(half == h, v, jnp.ones_like(v))))
            return stack(out)

        tasks = [(kind, p, h) for p in range(pairs) for kind in range(2) for h in range(2)]
        ahead = scores(*tasks[0])
        held = None
        for i, (kind, p, h) in enumerate(tasks):
            s = ahead
            if i + 1 < len(tasks):
                ahead = scores(*tasks[i + 1])
            high = jnp.max(s, axis=1, keepdims=True)
            mixed = mix(kind, p, h, jnp.exp(s - high).astype(BF))
            if h == 0:
                held = high, mixed
                continue
            rows = slice(slots[kind][0][0].start, slots[kind][-1][0].stop)
            cols = slice(p * PAIR, (p + 1) * PAIR)
            total = pltpu.roll(jnp.where(half == 0, mixed, held[1]), HEAD_DIM, 1)
            a_ref[k, rows, cols] = (jnp.where(half == 0, held[1], mixed) / total).astype(BF)
            lse_ref[k, rows, cols] = jnp.where(half == 0, held[0], high) + jnp.log(total)
        loads("out", a_ref.at[k], a_out.at[k])
        loads("out", lse_ref.at[k], lse_out.at[k])

    loads.need("x")
    project(1, bq_ref[...].reshape(1, -1), bv_ref[...].reshape(1, -1))
    pl.semaphore_wait(barrier, 1)
    swaps = []
    for src, dst in [(src, wc_ref.at[0, :, cols]) for src, cols in blocks] + [
            (bq_ref, bq_other), (bv_ref, bv_other), (b1_ref, b1_other), (wo_hbm, wo_other), (w1_hbm, w1_other),
            (w2_hbm, w2_other)]:
        n = len(swaps)
        swaps.append(remote(src, dst, s_sem.at[n], r_sem.at[n], partner))
        swaps[-1].start()
    first = len(blocks) + 2
    attention(1)
    for copy in swaps[:first]:
        copy.wait()
    project(0, bq_other[...].reshape(1, -1), bv_other[...].reshape(1, -1))
    attention(0)
    for copy in swaps[first:]:
        copy.wait()
    loads.drain()


def attend(slots, tokens, weights, biases):
    rows, d = tokens.shape[0] // 2, tokens.shape[1]
    inner = weights[0].shape[1]
    shape, vmem, dma = jax.ShapeDtypeStruct, pltpu.VMEM, pltpu.SemaphoreType.DMA
    outs = ((rows, 3 * inner), BF), ((rows, inner), BF), ((rows, inner), F32), ((d, 3 * inner), BF)
    like = [shape(a.shape, a.dtype) for a in (*weights[3:], biases[2])]
    return pl.pallas_call(
        attend_kernel,
        out_shape=(*(shape((2, *s), t) for s, t in outs), *like),
        in_specs=[SM, SM, SM] + [ANY] * 7 + [VM] * 3,
        out_specs=(ANY,) * 7 + (VM,),
        scratch_shapes=[
            *(vmem((2, *s), t) for s, t in outs), vmem((rows, d), BF), vmem((inner,), F32), vmem((inner,), F32),
            dma((24,)), dma((16,)), dma((16,))],
        compiler_params=params(collective_id=3, has_side_effects=True),
        name="attend",
    )(*slots, tokens, *weights, *biases)


def norm(v, gain, shift):
    centre = v - jnp.mean(v, axis=-1, keepdims=True)
    inverse = lax.rsqrt(jnp.mean(centre * centre, axis=-1, keepdims=True) + NORM_EPS)
    normed = centre * inverse
    return normed * gain + shift, normed, inverse


def norm_back(e, normed, inverse, gain):
    scaled = e * gain
    plain = jnp.mean(scaled, axis=-1, keepdims=True)
    cross = jnp.mean(scaled * normed, axis=-1, keepdims=True)
    return inverse * (scaled - plain - normed * cross)


def gelu_terms(u):
    cdf = 0.5 + 0.5 * lax.erf(u * ROOT_HALF)
    return u * cdf, cdf + u * jnp.exp(-0.5 * u * u) * INV_ROOT_TAU


def column_sum(value):
    return jnp.sum(value, axis=0, keepdims=True)


def forward_kernel(
    long_ref, short_ref, count_ref, tok_hbm, cot_hbm, a_hbm, woo_hbm, wop_hbm, w1o_hbm, w1p_hbm, w2o_hbm,
    w2p_hbm, bo_ref, bp_ref, attn_bias_ref, a1_ref, s1_ref, ffn_bias_ref, a2_ref, s2_ref,
    result_out, pooled_ref, n1_out, r1_out, h_out, g_out, slope_out, df_out, dr_out, grad_ref,
    x_ref, cot_ref, a_ref, wo_ref, w1_ref, w2_ref, result_ref, n1_ref, r1_ref, h_ref, g_ref, slope_ref, df_ref, dr_ref,
    sem,
):
    loads = Loads(sem)
    stores = Loads(sem.at[pl.ds(16, 32)])
    inner = a_hbm.shape[2]
    load_rows(loads, "x", tok_hbm, x_ref)
    for k, wo_hbm in enumerate((wop_hbm, woo_hbm)):
        loads("x", a_hbm.at[k], a_ref.at[:, k * inner:(k + 1) * inner])
        loads("x", wo_hbm, wo_ref.at[k * inner:(k + 1) * inner])
    loads("w11", w1o_hbm, w1_ref.at[1])
    loads("w10", w1p_hbm, w1_ref.at[0])
    load_rows(loads, "tail", cot_hbm, cot_ref)
    loads("tail", w2o_hbm, w2_ref.at[1])
    loads("tail", w2p_hbm, w2_ref.at[0])
    lengths = my_slots(long_ref, short_ref, count_ref)
    rows_all = x_ref.shape[0]
    width = w1_ref.shape[2]
    attn_bias, a1, s1, ffn_bias, a2, s2 = (
        ref[...].reshape(1, -1) for ref in (attn_bias_ref, a1_ref, s1_ref, ffn_bias_ref, a2_ref, s2_ref))
    loads.need("x")
    tile = 256
    for i in range(rows_all // tile):
        rows = slice(i * tile, (i + 1) * tile)
        attn = dot(a_ref[rows, :], wo_ref[...]) + attn_bias
        h1, normed, inverse = norm(x_ref[rows, :].astype(F32) + attn, a1, s1)
        n1_ref[rows, :] = normed
        r1_ref[rows, :] = jnp.broadcast_to(inverse, (tile, 128))
        h_ref[rows, :] = h1.astype(BF)
    for ref, out in ((n1_ref, n1_out), (r1_ref, r1_out), (h_ref, h_out)):
        stores("out", ref, out)

    tile, chunk = 128, 512
    for k, b_ref in ((1, bo_ref), (0, bp_ref)):
        loads.need(f"w1{k}")
        b1 = b_ref[...].reshape(1, -1)
        for c in range(width // chunk):
            cols = slice(c * chunk, (c + 1) * chunk)
            for i in range(rows_all // tile):
                rows = slice(i * tile, (i + 1) * tile)
                g, slope = gelu_terms(dot(h_ref[rows, :], w1_ref[k, :, cols]) + b1[:, cols])
                g_ref[k, rows, cols] = g.astype(BF)
                slope_ref[k, rows, cols] = slope.astype(BF)
        stores("out", g_ref.at[k], g_out.at[k])
        stores("out", slope_ref.at[k], slope_out.at[k])

    loads.need("tail")
    tile = 256
    grad_ref[...] = jnp.zeros_like(grad_ref)
    pooled_ref[...] = jnp.zeros_like(pooled_ref)
    for i in range(rows_all // tile):
        rows = slice(i * tile, (i + 1) * tile)
        ffn = dot(g_ref[0, rows, :], w2_ref[0]) + dot(g_ref[1, rows, :], w2_ref[1]) + ffn_bias
        y, normed, inverse = norm(n1_ref[rows, :] * a1 + s1 + ffn, a2, s2)
        result_ref[rows, :] = y.astype(BF)
        step = LONG if i * tile < LONG else SHORT
        for k in range(max(tile // step, 1)):
            start = i * tile + k * step
            slot = 0 if start < LONG else 1 + (start - LONG) // SHORT
            count = min(step, tile)
            place = (start if slot == 0 else 0) + lax.broadcasted_iota(jnp.int32, (count, 1), 0)
            part = y[k * count:(k + 1) * count, :]
            pooled_ref[slot:slot + 1, :] += column_sum(jnp.where(place < lengths[slot], part, 0.0))
        e = cot_ref[rows, :].astype(F32)
        dr = norm_back(e, normed, inverse, a2)
        low = dr.astype(BF)
        dr_ref[rows, :] = dr
        df_ref[rows, :] = low
        grad_ref[0:1, :] += column_sum(low.astype(F32))
        grad_ref[1:2, :] += column_sum(e * normed)
        grad_ref[2:3, :] += column_sum(e)
        for ref, out in ((result_ref, result_out), (df_ref, df_out), (dr_ref, dr_out)):
            stores("out", ref.at[rows], out.at[rows])
    for slot, length in enumerate(lengths):
        pooled_ref[slot:slot + 1, :] = pooled_ref[slot:slot + 1, :] / jnp.maximum(length, 1).astype(F32)
    stores.drain()


def forward(slots, tokens, cot, a, wo, w1, w2, b1, vectors):
    rows, d = tokens.shape[0] // 2, tokens.shape[1]
    width = w1[0].shape[1]
    inner = a.shape[2]
    shape, vmem = jax.ShapeDtypeStruct, pltpu.VMEM
    return pl.pallas_call(
        forward_kernel,
        out_shape=(
            shape((rows, d), BF), shape((8, d), F32), shape((rows, d), F32), shape((rows, 128), F32),
            shape((rows, d), BF), shape((2, rows, width), BF), shape((2, rows, width), BF), shape((rows, d), BF),
            shape((rows, d), F32), shape((8, d), F32),
        ),
        in_specs=[SM, SM, SM] + [ANY] * 9 + [VM] * 8,
        out_specs=(ANY, VM) + (ANY,) * 7 + (VM,),
        scratch_shapes=[
            vmem((rows, d), BF), vmem((rows, d), BF), vmem((rows, 2 * inner), BF), vmem((2 * inner, d), BF),
            vmem((2, d, width), BF), vmem((2, width, d), BF), vmem((rows, d), BF), vmem((rows, d), F32),
            vmem((rows, 128), F32), vmem((rows, d), BF), vmem((2, rows, width), BF), vmem((2, rows, width), BF),
            vmem((rows, d), BF), vmem((rows, d), F32), pltpu.SemaphoreType.DMA((48,))],
        compiler_params=params(),
        cost_estimate=pl.CostEstimate(
            flops=2 * rows * d * (width * 4 + d), bytes_accessed=50 << 20, transcendentals=rows * width * 4),
        name="forward",
    )(*slots, tokens, cot, a, *wo, *w1, *w2, *b1, *vectors)


def peer(sub, bit):
    me = lax.axis_index("dp")
    group = me // sub
    value = (group // (1 << bit)) % 2
    other = me + (1 - 2 * value) * (sub << bit)
    return value, {"dp": other}


def remote(src, dst, s, r, device):
    return pltpu.make_async_remote_copy(
        src_ref=src, dst_ref=dst, send_sem=s, recv_sem=r, device_id=device, device_id_type=MESH)


class Halving:
    orders = ((0, 1, 2, 3), (1, 0, 2, 3))

    def __init__(self, sub, sums, sends, ins, first, s_sem, r_sem):
        self.links = [peer(sub, bit) for bit in range(BITS)]
        self.partner = {"tensor": 1 - lax.axis_index("tensor")}
        self.sums, self.sends, self.ins, self.first = sums, sends, ins, first
        self.s_sem, self.r_sem = s_sem, r_sem
        self.stage = {}
        self.copy = {}

    def greet(self):
        barrier = pltpu.get_barrier_semaphore()
        for device in [self.partner] + [link[1] for link in self.links]:
            pl.semaphore_signal(barrier, inc=1, device_id=device, device_id_type=MESH)

    def meet(self):
        pl.semaphore_wait(pltpu.get_barrier_semaphore(), BITS + 1)

    def region(self, u, count, bit=None):
        fixed = self.orders[u % 2][:count]
        index = [u]
        for b in reversed(range(BITS)):
            value = self.links[b][0]
            index.append(value if b in fixed else 1 - value if b == bit else slice(None))
        return tuple(index)

    def swap(self, u):
        k = u - self.first[0]
        self.stage[u] = 0
        self.copy[u] = remote(
            self.sends.at[k], self.ins[0].at[k], self.s_sem.at[u, BITS], self.r_sem.at[u, BITS], self.partner)
        self.copy[u].start()

    def resume(self, u, stage):
        self.stage[u] = stage

    def arrive(self, u):
        stage = self.stage[u]
        self.copy[u].wait()
        index = self.region(u, stage)
        brought = self.ins[stage][u - self.first[stage]].astype(F32)
        total = self.sums[index].astype(F32) + brought
        if stage == BITS:
            return total
        self.sums[index] = total.astype(BF)
        return None

    def depart(self, u):
        stage = self.stage[u]
        bit = self.orders[u % 2][stage]
        index = self.region(u, stage, bit)
        self.copy[u] = remote(
            self.sums.at[index], self.ins[stage + 1].at[u - self.first[stage + 1]],
            self.s_sem.at[u, stage], self.r_sem.at[u, stage], self.links[bit][1])
        self.copy[u].start()
        self.stage[u] = stage + 1

    def move(self, *units):
        for u in units:
            self.arrive(u)
            self.depart(u)


def halving_scratch(first, units):
    shapes = ((2, 2, 2, 2), (2, 2, 2), (2, 2), (2,), ())
    return [pltpu.VMEM((max(units - f, 1), *s, 48, UNIT), BF) for f, s in zip(first, shapes)] + [
        pltpu.SemaphoreType.DMA((units, BITS + 1)), pltpu.SemaphoreType.DMA((units, BITS + 1))]


def weight_grad(send, own, left, right, width):
    value = dot_tn(left, right).astype(BF)
    for k, place in enumerate(send + own):
        ref, u = place
        ref[u] = value[:, k * width:(k + 1) * width].reshape(2, 2, 2, 2, 48, width)


FIRST_A = (0, 0, 0, 0, 8)
STAGES_A = (3, 3, 2, 2, 1, 1, 0, 0)


def ffn_back_kernel(
    sub, df_hbm, h_hbm, dr_hbm, g_hbm, d_hbm, w1p_hbm, w1o_hbm, w2p_hbm, w2o_hbm,
    sums_out, dh_out, bp_ref, bo_ref,
    df_ref, h_ref, g_ref, slope_ref, w1_ref, w2_ref, dh_ref, sums_ref, send_ref,
    in0_ref, in1_ref, in2_ref, in3_ref, in4_ref, s_sem, r_sem, load_sem, out_sem,
):
    rows_all, d = df_ref.shape
    width = w1_ref.shape[2]
    chunk = 2 * UNIT
    chunks = width // chunk
    red = Halving(sub, sums_ref, send_ref, (in0_ref, in1_ref, in2_ref, in3_ref, in4_ref), FIRST_A, s_sem, r_sem)
    red.greet()
    loads = Loads(load_sem)
    loads("df", df_hbm, df_ref)
    for c in range(chunks):
        cols = pl.ds(c * chunk, chunk)
        for k in range(2):
            loads(f"g{k}{c}", g_hbm.at[k, :, cols], g_ref.at[k, :, cols])
    loads("h", h_hbm, h_ref)
    for c in range(chunks):
        cols = pl.ds(c * chunk, chunk)
        for k, w2_hbm in enumerate((w2p_hbm, w2o_hbm)):
            loads(f"w{k}{c}", w2_hbm.at[cols], w2_ref.at[k, cols])
            loads(f"w{k}{c}", d_hbm.at[k, :, cols], slope_ref.at[k, :, cols])
    loads("dr", dr_hbm, dh_ref)
    for k, w1_hbm in enumerate((w1p_hbm, w1o_hbm)):
        loads("dr", w1_hbm, w1_ref.at[k])

    bp_ref[...] = jnp.zeros_like(bp_ref)
    bo_ref[...] = jnp.zeros_like(bo_ref)
    loads.need("df")
    for c in range(chunks):
        cols = slice(c * chunk, (c + 1) * chunk)
        units = (2 * c, 2 * c + 1)
        for k, out_ref in enumerate((send_ref, sums_ref)):
            loads.need(f"g{k}{c}")
            weight_grad([(out_ref, u) for u in units], [], df_ref[...], g_ref[k, :, cols], UNIT)
            if k == 0:
                if c == 0:
                    red.meet()
                for u in units:
                    red.swap(u)
        if c == 1:
            red.move(0, 1)
    loads.need("h")
    for c in range(chunks):
        cols = slice(c * chunk, (c + 1) * chunk)
        units = (2 * chunks + 2 * c, 2 * chunks + 2 * c + 1)
        for k, (out_ref, bias_ref) in enumerate(((send_ref, bp_ref), (sums_ref, bo_ref))):
            loads.need(f"w{k}{c}")
            for n in range(c * chunk, (c + 1) * chunk, 256):
                part = slice(n, n + 256)
                slope = slope_ref[k, :, part].astype(F32)
                du = (dot_nt(df_ref[...], w2_ref[k, part, :]) * slope).astype(BF)
                slope_ref[k, :, part] = du
                bias_ref[0:1, part] = column_sum(du.astype(F32))
            weight_grad([(out_ref, u) for u in units], [], h_ref[...], slope_ref[k, :, cols], UNIT)
            if k == 0:
                for u in units:
                    red.swap(u)
            if (c, k) == (0, 0):
                red.move(2, 3)
            if (c, k) == (1, 0):
                red.move(0, 1)
    loads.need("dr")
    red.move(4, 5)
    for i in range(2):
        rows = slice(i * rows_all // 2, (i + 1) * rows_all // 2)
        dh_ref[rows, :] += dot_nt(slope_ref[0, rows, :], w1_ref[0]) + dot_nt(slope_ref[1, rows, :], w1_ref[1])
        loads("out", dh_ref.at[rows], dh_out.at[rows])
        if i == 0:
            red.move(2, 3, 0, 1)
    for u in range(4 * chunks):
        red.arrive(u)
    outs = pltpu.make_async_copy(sums_ref, sums_out, out_sem)
    outs.start()
    loads.drain()
    outs.wait()


def ffn_back(sub, df, h, dr, g, slope, w1, w2):
    rows, d = df.shape
    width = w1[0].shape[1]
    units = 2 * width // UNIT
    shape, vmem = jax.ShapeDtypeStruct, pltpu.VMEM
    return pl.pallas_call(
        functools.partial(ffn_back_kernel, sub),
        out_shape=(
            shape((units, 2, 2, 2, 2, 48, UNIT), BF), shape((rows, d), F32), shape((8, width), F32), shape((8, width), F32),
        ),
        in_specs=[ANY] * 9,
        out_specs=(ANY, ANY, VM, VM),
        scratch_shapes=[
            vmem((rows, d), BF), vmem((rows, d), BF), vmem((2, rows, width), BF), vmem((2, rows, width), BF),
            vmem((2, d, width), BF), vmem((2, width, d), BF), vmem((rows, d), F32),
            vmem((units, 2, 2, 2, 2, 48, UNIT), BF), vmem((units, 2, 2, 2, 2, 48, UNIT), BF),
            *halving_scratch(FIRST_A, units), pltpu.SemaphoreType.DMA((24,)), pltpu.SemaphoreType.DMA,
        ],
        compiler_params=params(collective_id=1, has_side_effects=True),
        name="ffn_back",
    )(df, h, dr, g, slope, *w1, *w2)


FIRST_B = (8, 6, 4, 2, 0)


def attn_back_kernel(
    sub, long_ref, short_ref, count_ref, sums_hbm, dh_hbm, n1_hbm, r1_hbm, gain_ref, tok_hbm, qkv_hbm,
    a_hbm, lse_hbm, wop_hbm, woo_hbm, wc_hbm, grad2_ref, b1p_ref, b1o_ref,
    outer_ref, inner_ref, q_ref, k_ref, v_ref, output_ref, dx_out, vec_out,
    dx_ref, n1_ref, r1_ref, x_ref, qkv_ref, a_ref, lse_ref, wo_ref, wc_ref, low_ref, da_ref, dqkv_ref,
    grad_ref, vsend_ref, vec_ref, vin_ref, sums_ref, send_ref,
    in0_ref, in1_ref, in2_ref, in3_ref, in4_ref, s_sem, r_sem, vs_sem, vr_sem, load_sem, swap_sem,
):
    rows_all, d = dx_ref.shape
    inner = a_ref.shape[1] // 2
    pairs = inner // PAIR
    half = halves()
    lengths = my_slots(long_ref, short_ref, count_ref)
    tensor = lax.axis_index("tensor")
    red = Halving(sub, sums_ref, send_ref, (in0_ref, in1_ref, in2_ref, in3_ref, in4_ref), FIRST_B, s_sem, r_sem)
    red.greet()
    loads = Loads(load_sem)
    handed = len(STAGES_A)
    for u, stage in enumerate(STAGES_A):
        red.resume(u, stage)
        index = red.region(u, stage)
        loads("sums", sums_hbm.at[index], sums_ref.at[index])
    for src, dst in ((dh_hbm, dx_ref), (n1_hbm, n1_ref), (r1_hbm, r1_ref)):
        loads("norm", src, dst)
    for k, wo_hbm in enumerate((wop_hbm, woo_hbm)):
        cols = slice(k * inner, (k + 1) * inner)
        loads("heads", a_hbm.at[k], a_ref.at[:, cols])
        loads("heads", wo_hbm, wo_ref.at[cols])
        loads("heads", lse_hbm.at[k], lse_ref.at[k])
        loads("heads", qkv_hbm.at[k], qkv_ref.at[k])
        for p in range(pairs):
            loads("last", wc_hbm.at[k, :, p * 384:(p + 1) * 384], wc_ref.at[p, :, k * 384:(k + 1) * 384])
    load_rows(loads, "heads", tok_hbm, x_ref)

    loads.need("sums")
    red.meet()
    for u in range(handed):
        red.depart(u)

    def finish(*units):
        for u in units:
            value = red.arrive(u)
            if u < 4:
                outer_ref[:, u * UNIT:(u + 1) * UNIT] = value
            elif u < 8:
                inner_ref[:, (u - 4) * UNIT:(u - 3) * UNIT] = value
            elif u == 8:
                output_ref[...] = value
            else:
                for i, ref in enumerate((q_ref, k_ref, v_ref)):
                    ref[:, (u - 9) * PAIR:(u - 8) * PAIR] = value[:, i * PAIR:(i + 1) * PAIR]

    loads.need("norm")
    grad_ref[...] = jnp.zeros_like(grad_ref)
    tile = 256
    gain = gain_ref[...].reshape(1, -1)
    for i in range(rows_all // tile):
        rows = slice(i * tile, (i + 1) * tile)
        e, normed = dx_ref[rows, :], n1_ref[rows, :]
        dr = norm_back(e, normed, r1_ref[rows, 0:1], gain)
        low = dr.astype(BF)
        dx_ref[rows, :] = dr
        low_ref[rows, :] = low
        grad_ref[0:1, :] += column_sum(low.astype(F32))
        grad_ref[1:2, :] += column_sum(e * normed)
        grad_ref[2:3, :] += column_sum(e)
    loads.need("heads")
    weight_grad([(send_ref, 0)], [(sums_ref, 8)], low_ref[...], a_ref[...], UNIT)
    red.swap(8)
    da_ref[...] = dot_nt(low_ref[...], wo_ref[...]).astype(BF)
    red.move(4, 5, 2, 3)
    finish(0, 1)
    red.move(6, 7)

    slots = [slot_parts(kind, lengths) for kind in range(2)]

    def attention(p, k):
        at = k * inner + p * PAIR
        q_cols, k_cols, v_cols = (slice(p * 384 + j * 128, p * 384 + (j + 1) * 128) for j in range(3))

        def scores(kind, h):
            s, dp = [], []
            for rows, scale, key_bias in slots[kind]:
                q = qkv_ref[k, rows, q_cols] * scale
                s.append(dot_nt(keep(half == h, q), qkv_ref[k, rows, k_cols]) + key_bias)
                dp.append(dot_nt(keep(half == h, da_ref[rows, at:at + PAIR]), qkv_ref[k, rows, v_cols]))
            return stack(s), stack(dp)

        def grads(kind, h, prob, ds):
            dq, dk, dv = [], [], []
            for i, (rows, scale, _) in enumerate(slots[kind]):
                count = rows.stop - rows.start
                part = slice(i * count, (i + 1) * count)
                dv.append(dot_tn(prob[part], keep(half == h, da_ref[rows, at:at + PAIR])))
                dk.append(dot_tn(ds[part], keep(half == h, qkv_ref[k, rows, q_cols] * scale)))
                dq.append(dot(ds[part], keep(half == h, qkv_ref[k, rows, k_cols] * scale)))
            return stack(dq), stack(dk), stack(dv)

        tasks = [(kind, h) for kind in range(2) for h in range(2)]
        ahead = scores(*tasks[0])
        held = None
        for i, (kind, h) in enumerate(tasks):
            s, dp = ahead
            if i + 1 < len(tasks):
                ahead = scores(*tasks[i + 1])
            rows = slice(slots[kind][0][0].start, slots[kind][-1][0].stop)
            product = da_ref[rows, at:at + PAIR].astype(F32) * a_ref[rows, at:at + PAIR].astype(F32)
            delta = jnp.sum(keep(half == h, product), axis=1, keepdims=True)
            lane = p * PAIR + h * HEAD_DIM
            prob = jnp.exp(s - lse_ref[k, rows, lane:lane + 1])
            value = grads(kind, h, prob.astype(BF), (prob * (dp - delta)).astype(BF))
            if h == 0:
                held = value
                continue
            for j in range(3):
                cols = slice(k * 384 + j * 128, k * 384 + (j + 1) * 128)
                dqkv_ref[p, rows, cols] = (held[j] + value[j]).astype(BF)

    after = {
        (0, 0): lambda: red.move(8, 4, 5),
        (0, 1): lambda: finish(2, 3),
        (1, 0): lambda: red.move(6, 7, 8),
        (1, 1): lambda: (finish(4, 5), red.move(9)),
        (2, 0): lambda: red.move(6, 7, 8, 9),
        (2, 1): lambda: red.move(10),
    }
    for p in range(pairs):
        for k in range(2):
            attention(p, k)
            if k == 1:
                weight_grad([(send_ref, 1 + p)], [(sums_ref, 9 + p)], x_ref[...], dqkv_ref[p], UNIT)
                red.swap(9 + p)
            after[p, k]()

    for k, (b1_ref, ref) in enumerate(((b1p_ref, vsend_ref), (b1o_ref, vec_ref.at[0]))):
        ref[...] = jnp.zeros(ref.shape, F32)
        ref[0:3, :] = grad_ref[0:3, :]
        ref[3:6, :] = grad2_ref[0:3, :]
        ref[6:7, :] = b1_ref[0:1, 0:d]
        ref[7:8, :] = b1_ref[0:1, d:2 * d]
        for p in range(pairs):
            sums = column_sum(dqkv_ref[p, :, k * 384:(k + 1) * 384].astype(F32))
            ref[8:9, p * PAIR:(p + 1) * PAIR] = sums[:, 0:128]
            ref[8:9, inner + p * PAIR:inner + (p + 1) * PAIR] = sums[:, 256:384]
    vnow = remote(vsend_ref, vin_ref.at[BITS], vs_sem.at[BITS], vr_sem.at[BITS], red.partner)
    vnow.start()
    red.move(11)
    loads.need("last")
    tile = 256
    span = rows_all // 2
    outs = []
    for i in range(rows_all // tile):
        rows = slice(i * tile, (i + 1) * tile)
        dx_ref[rows, :] += sum(dot_nt(dqkv_ref[p, rows, :], wc_ref[p]) for p in range(pairs))
        if i * tile % span == span - tile:
            g = i * tile // span
            here = dx_ref.at[pl.ds(g * span, span)]
            there = dx_out.at[pl.ds(pl.multiple_of((2 * g + tensor) * span, span), span)]
            loads("dx", here, there)
            outs.append(remote(here, there, swap_sem.at[0, g], swap_sem.at[1, g], red.partner))
            outs[-1].start()
        if i < BITS:
            vnow.wait()
            if i == 0:
                vec_ref[0] = vec_ref[0] + vin_ref[BITS]
            else:
                vec_ref[i] = vec_ref[i - 1] + vin_ref[i - 1]
            vnow = remote(vec_ref.at[i], vin_ref.at[i], vs_sem.at[i], vr_sem.at[i], red.links[i][1])
            vnow.start()
        if i == 0:
            red.move(10)
        if i == 1:
            red.move(8, 9, 11)
        if i == 2:
            finish(6, 7)
            red.move(10)
    red.move(11, 9)
    finish(8)
    red.move(10, 11)
    vnow.wait()
    vec_out[...] = vec_ref[BITS - 1] + vin_ref[BITS - 1]
    finish(9, 10, 11)
    for copy in outs:
        copy.wait()
    loads.drain()


def attn_back(sub, slots, sums, dh, n1, r1, gain, tokens, qkv, a, lse, wo, wc, grad2, b1):
    rows, d = dh.shape
    inner = a.shape[2]
    pairs = inner // PAIR
    ff = b1[0].shape[1]
    units = sums.shape[0] + 1 + 3 * inner // UNIT
    shape, vmem, dma = jax.ShapeDtypeStruct, pltpu.VMEM, pltpu.SemaphoreType.DMA
    return pl.pallas_call(
        functools.partial(attn_back_kernel, sub),
        out_shape=(
            shape((48, ff), F32), shape((48, ff), F32), shape((48, inner), F32), shape((48, inner), F32),
            shape((48, inner), F32), shape((48, inner), F32), shape((2 * rows, d), F32), shape((16, d), F32),
        ),
        in_specs=[SM, SM, SM, ANY, ANY, ANY, ANY, VM] + [ANY] * 7 + [VM, VM, VM],
        out_specs=(VM, VM, VM, VM, VM, VM, ANY, VM),
        scratch_shapes=[
            vmem((rows, d), F32), vmem((rows, d), F32), vmem((rows, 128), F32), vmem((rows, d), BF),
            vmem((2, rows, 3 * inner), BF), vmem((rows, 2 * inner), BF), vmem((2, rows, inner), F32),
            vmem((2 * inner, d), BF), vmem((pairs, d, 768), BF), vmem((rows, d), BF), vmem((rows, 2 * inner), BF),
            vmem((pairs, rows, 768), BF), vmem((8, d), F32), vmem((16, d), F32), vmem((BITS, 16, d), F32),
            vmem((BITS + 1, 16, d), F32),
            vmem((units, 2, 2, 2, 2, 48, UNIT), BF), vmem((4, 2, 2, 2, 2, 48, UNIT), BF),
            *halving_scratch(FIRST_B, units), dma((BITS + 1,)), dma((BITS + 1,)), dma((36,)), dma((2, 2)),
        ],
        compiler_params=params(collective_id=2, has_side_effects=True),
        name="attn_back",
    )(*slots, sums, dh, n1, r1, gain, tokens, qkv, a, lse, *wo, wc, grad2, *b1)


def deliver_kernel(
    short_half, own_hbm, other_hbm, pool_own_ref, pool_other_ref, dx_hbm, total_ref, *refs,
):
    grads = refs[:6]
    result_out, pooled_out, dx_out = refs[6:9]
    grad_outs = refs[9:15]
    shard_outs = refs[15:21]
    bq_out, bv_out, b1_out, dx_ref, result_ref, sem = refs[21:]
    tensor = lax.axis_index("tensor")
    loads = Loads(sem)
    half = own_hbm.shape[0] // 2
    parts = 4 * half // 256
    moves = []
    for n in range(parts):
        rows = pl.ds(n * 256, 256)
        moves.append((dx_hbm.at[rows], dx_ref.at[rows], dx_out.at[rows]))
    for n, (hbm, place) in enumerate(((own_hbm, tensor), (other_hbm, 1 - tensor))):
        for k in range(2):
            here = pl.ds((2 * n + k) * half, half)
            moves.append((hbm.at[pl.ds(k * half, half)], result_ref.at[here],
                          result_out.at[pl.ds(pl.multiple_of((2 * k + place) * half, half), half)]))
    for n, (src, here, _) in enumerate(moves):
        loads(n, src, here)
    for src, dst in zip(grads, grad_outs):
        dst[...] = src[...]
    first = jnp.where(tensor == 0, pool_own_ref[...], pool_other_ref[...])
    second = jnp.where(tensor == 0, pool_other_ref[...], pool_own_ref[...])
    pooled_out[0:1, :] = first[0:1]
    pooled_out[1:2, :] = second[0:1]
    pooled_out[2:2 + short_half, :] = first[1:1 + short_half]
    pooled_out[2 + short_half:2 + 2 * short_half, :] = second[1:1 + short_half]
    total = total_ref[...]
    d = total.shape[1]
    share = shard_outs[0].shape[0]
    start = lax.axis_index("dp") * share
    moved = pltpu.roll(total[0:8, :], (d - start) % d, 1)
    for k, out in enumerate(shard_outs):
        out[...] = moved[k, 0:share]
    inner = bq_out.shape[0]
    bq_out[...] = total[8, 0:inner]
    bv_out[...] = total[8, inner:2 * inner]
    b1_out[0:d] = total[6]
    b1_out[d:2 * d] = total[7]
    for n, (_, here, dst) in enumerate(moves):
        loads.need(n)
        loads("out", here, dst)
    loads.drain()


def deliver(own, other, pool_own, pool_other, dx, total, grads, share, inner, short_half):
    rows, d = own.shape
    shape = jax.ShapeDtypeStruct
    return pl.pallas_call(
        functools.partial(deliver_kernel, short_half),
        out_shape=(
            shape((2 * rows, d), BF), shape((2 + 2 * short_half, d), F32), shape((2 * rows, d), F32),
            *(shape(g.shape, F32) for g in grads), *(shape((share,), F32) for _ in range(6)),
            shape((inner,), F32), shape((inner,), F32), shape((2 * d,), F32),
        ),
        in_specs=[ANY, ANY, VM, VM, ANY, VM] + [VM] * 6,
        out_specs=(ANY, VM, ANY) + (VM,) * 15,
        scratch_shapes=[pltpu.VMEM(dx.shape, F32), pltpu.VMEM((2 * rows, d), BF), pltpu.SemaphoreType.DMA((32,))],
        compiler_params=params(),
        name="deliver",
    )(own, other, pool_own, pool_other, dx, total, *grads)


def per_device(
    dp_size, tokens, cotangent, long_lengths, short_lengths, live_counts, query_weight, query_bias, key_weight,
    value_weight, value_bias, output_weight, output_bias, attn_gain, attn_shift, inner_weight, inner_bias,
    outer_weight, outer_bias, ffn_gain, ffn_shift,
):
    d = tokens.shape[1]
    sub = dp_size // GROUPS
    slots = (long_lengths, short_lengths, live_counts)

    def swap(a):
        return lax.ppermute(a, "tensor", [(0, 1), (1, 0)])

    qkv, a, lse, wc, wo_other, w1_other, w2_other, b1_other = attend(
        slots, tokens, (query_weight, key_weight, value_weight, output_weight, inner_weight, outer_weight),
        (query_bias, value_bias, inner_bias))
    wo, w1, w2 = (wo_other, output_weight), (w1_other, inner_weight), (w2_other, outer_weight)
    result, pooled, n1, r1, h, g, slope, df, dr, grad2 = forward(
        slots, tokens, cotangent, a, wo[::-1], w1[::-1], w2[::-1], (inner_bias, b1_other),
        (output_bias, attn_gain, attn_shift, outer_bias, ffn_gain, ffn_shift))
    result_other, pooled_other = swap(result), swap(pooled)
    sums, dh, b1p, b1o = ffn_back(sub, df, h, dr, g, slope, w1, w2)
    *grads, dx, total = attn_back(
        sub, slots, sums, dh, n1, r1, attn_gain, tokens, qkv, a, lse, wo, wc, grad2, (b1p, b1o))
    if sub > 1:
        groups = [[g * sub + i for i in range(sub)] for g in range(GROUPS)]
        grads = [lax.psum_scatter(g, "dp", scatter_dimension=0, axis_index_groups=groups, tiled=True) for g in grads]
        total = lax.psum(total, "dp", axis_index_groups=groups)
    (result_all, pooled_all, dx_all, d_outer, d_inner, d_q, d_k, d_v, d_output, *shards, d_bq, d_bv, d_b1) = deliver(
        result, result_other, pooled, pooled_other, dx, total, grads, d // dp_size, query_weight.shape[1],
        short_lengths.shape[0] // 2)
    return (
        result_all, pooled_all, dx_all, d_q, d_bq, d_k, d_v, d_bv, d_output.T, *shards[:3], d_inner, d_b1, d_outer.T,
        *shards[3:],
    )


def solution(mesh):
    in_specs = (
        P("dp", None), P("dp", None), P("dp"), P("dp"), P("dp", None), P(None, "tensor"), P("tensor"),
        P(None, "tensor"), P(None, "tensor"), P("tensor"), P("tensor", None), P(), P(), P(), P(None, "tensor"),
        P("tensor"), P("tensor", None), P(), P(), P(),
    )
    out_specs = (
        P("dp", None), P("dp", None), P("dp", None), P("dp", "tensor"), P("tensor"), P("dp", "tensor"),
        P("dp", "tensor"), P("tensor"), P("tensor", "dp"), P("dp"), P("dp"), P("dp"), P("dp", "tensor"),
        P("tensor"), P("tensor", "dp"), P("dp"), P("dp"), P("dp"),
    )
    return jax.shard_map(
        functools.partial(per_device, mesh.shape["dp"]), mesh=mesh, in_specs=in_specs, out_specs=out_specs,
        check_vma=False)
```

```python
import functools

import jax
import jax.numpy as jnp
from jax import lax
from jax.experimental import pallas as pl
from jax.experimental.pallas import tpu as pltpu
from jax.sharding import PartitionSpec as P

HEAD_DIM = 64
LONG = 512
SHORT = 128
PAIR = 128
NORM_EPS = 1e-12
MASKED = -1000000000.0
SCORE_SCALE = 0.125
INV_ROOT_TAU = 0.3989422804014327
ROOT_HALF = 0.7071067811865476
BF = jnp.bfloat16
F32 = jnp.float32
MESH = pl.DeviceIdType.MESH
UNIT = 384
BITS = 4
GROUPS = 1 << BITS

VM = pl.BlockSpec(memory_space=pltpu.VMEM)
SM = pl.BlockSpec(memory_space=pltpu.SMEM)
ANY = pl.BlockSpec(memory_space=pl.ANY)


def params(**more):
    return pltpu.CompilerParams(vmem_limit_bytes=62 << 20, **more)


def dot(a, b):
    return jnp.dot(a, b, preferred_element_type=F32)


def dot_nt(a, b):
    return lax.dot_general(a, b, (((1,), (1,)), ((), ())), preferred_element_type=F32)


def dot_tn(a, b):
    return lax.dot_general(a, b, (((0,), (0,)), ((), ())), preferred_element_type=F32)


def spans(start, unit, size=None):
    return pl.ds(pl.multiple_of(start, unit), unit if size is None else size)


def my_slots(long_ref, short_ref, count_ref):
    tensor = lax.axis_index("tensor")
    n_long, n_short = long_ref.shape[0] // 2, short_ref.shape[0] // 2
    lengths = []
    for ref, n, column in ((long_ref, n_long, 0), (short_ref, n_short, 1)):
        for j in range(n):
            slot = tensor * n + j
            lengths.append(jnp.where(slot < count_ref[0, column], ref[slot], 0))
    return lengths


def my_rows(whole_ref, mine_ref, sem):
    tensor = lax.axis_index("tensor")
    half = mine_ref.shape[0] // 2
    return [
        pltpu.make_async_copy(
            whole_ref.at[pl.ds(pl.multiple_of((2 * k + tensor) * half, half), half)],
            mine_ref.at[pl.ds(k * half, half)], sem.at[k])
        for k in range(2)
    ]


def key_terms(length, count):
    keys = lax.broadcasted_iota(jnp.int32, (1, count), 1)
    scale = jnp.where(length > 0, SCORE_SCALE, 0.0).astype(BF)
    bias = jnp.where((keys < length) | (length <= 0), 0.0, MASKED)
    return scale, bias


def halves():
    return lax.broadcasted_iota(jnp.int32, (1, PAIR), 1) // HEAD_DIM


class Loads:
    def __init__(self, sem):
        self.sem, self.count, self.open = sem, 0, {}

    def __call__(self, name, src, dst):
        copy = pltpu.make_async_copy(src, dst, self.sem.at[self.count])
        self.count += 1
        self.open.setdefault(name, []).append(copy)
        copy.start()

    def need(self, *names):
        for name in names:
            for copy in self.open.pop(name):
                copy.wait()

    def drain(self):
        self.need(*list(self.open))


def load_rows(loads, name, whole_ref, mine_ref):
    tensor = lax.axis_index("tensor")
    half = mine_ref.shape[0] // 2
    for k in range(2):
        loads(name, whole_ref.at[pl.ds(pl.multiple_of((2 * k + tensor) * half, half), half)],
              mine_ref.at[pl.ds(k * half, half)])


def slot_parts(kind, lengths):
    if kind == 0:
        return [(slice(0, LONG), *key_terms(lengths[0], LONG))]
    return [
        (slice(LONG + SHORT * s, LONG + SHORT * (s + 1)), *key_terms(length, SHORT))
        for s, length in enumerate(lengths[1:])]


def stack(values):
    return values[0] if len(values) == 1 else jnp.concatenate(values, axis=0)


def keep(own, value, other=None):
    return jnp.where(own, value, jnp.zeros_like(value) if other is None else other)


def attend_kernel(
    long_ref, short_ref, count_ref, tok_hbm, wq_hbm, wk_hbm, wv_hbm, wo_hbm, w1_hbm, w2_hbm, bq_ref, bv_ref, b1_ref,
    qkv_out, a_out, lse_out, wc_out, wo_other, w1_other, w2_other, b1_other,
    qkv_ref, a_ref, lse_ref, wc_ref, x_ref, bq_other, bv_other, sem, s_sem, r_sem,
):
    width = qkv_ref.shape[2]
    pairs = width // (3 * PAIR)
    partner = {"tensor": 1 - lax.axis_index("tensor")}
    barrier = pltpu.get_barrier_semaphore()
    pl.semaphore_signal(barrier, inc=1, device_id=partner, device_id_type=MESH)
    loads = Loads(sem)
    load_rows(loads, "x", tok_hbm, x_ref)
    blocks = []
    for p in range(pairs):
        for j, w_hbm in enumerate((wq_hbm, wk_hbm, wv_hbm)):
            at = (3 * p + j) * PAIR
            blocks.append((w_hbm.at[:, p * PAIR:(p + 1) * PAIR], slice(at, at + PAIR)))
    for src, cols in blocks:
        loads("x", src, wc_ref.at[1, :, cols])
    lengths = my_slots(long_ref, short_ref, count_ref)
    half = halves()
    lane = lax.broadcasted_iota(jnp.int32, (1, PAIR), 1) % HEAD_DIM
    slots = [slot_parts(kind, lengths) for kind in range(2)]

    def project(k, bq, bv):
        parts = []
        for p in range(pairs):
            cols = slice(p * PAIR, (p + 1) * PAIR)
            parts += [bq[:, cols], jnp.zeros((1, PAIR), F32), bv[:, cols]]
        qkv_ref[k] = (dot(x_ref[...], wc_ref[k]) + jnp.concatenate(parts, axis=1)).astype(BF)
        loads("out", qkv_ref.at[k], qkv_out.at[k])
        loads("out", wc_ref.at[k], wc_out.at[k])

    def attention(k):
        def scores(kind, p, h):
            out = []
            for rows, scale, key_bias in slots[kind]:
                q = qkv_ref[k, rows, p * 384:p * 384 + 128] * scale
                out.append(dot_nt(keep(half == h, q), qkv_ref[k, rows, p * 384 + 128:p * 384 + 256]) + key_bias)
            return stack(out)

        def mix(kind, p, h, e):
            out = []
            for i, (rows, _, _) in enumerate(slots[kind]):
                v = qkv_ref[k, rows, p * 384 + 256:p * 384 + 384]
                count = rows.stop - rows.start
                out.append(dot(e[i * count:(i + 1) * count], keep(half == h, v, jnp.ones_like(v))))
            return stack(out)

        tasks = [(kind, p, h) for p in range(pairs) for kind in range(2) for h in range(2)]
        ahead = scores(*tasks[0])
        held = None
        for i, (kind, p, h) in enumerate(tasks):
            s = ahead
            if i + 1 < len(tasks):
                ahead = scores(*tasks[i + 1])
            high = jnp.max(s, axis=1, keepdims=True)
            mixed = mix(kind, p, h, jnp.exp(s - high).astype(BF))
            if h == 0:
                held = high, mixed
                continue
            rows = slice(slots[kind][0][0].start, slots[kind][-1][0].stop)
            cols = slice(p * PAIR, (p + 1) * PAIR)
            total = pltpu.roll(jnp.where(half == 0, mixed, held[1]), HEAD_DIM, 1)
            a_ref[k, rows, cols] = (jnp.where(half == 0, held[1], mixed) / total).astype(BF)
            lse = jnp.where(half == 0, held[0], high) + jnp.log(total)
            lse_ref[k, rows, :] = lse if p == 0 else jnp.where(lane == p, lse, lse_ref[k, rows, :])
        loads("out", a_ref.at[k], a_out.at[k])
        loads("out", lse_ref.at[k], lse_out.at[k])

    loads.need("x")
    project(1, bq_ref[...].reshape(1, -1), bv_ref[...].reshape(1, -1))
    pl.semaphore_wait(barrier, 1)
    swaps = []
    for src, dst in [(src, wc_ref.at[0, :, cols]) for src, cols in blocks] + [
            (bq_ref, bq_other), (bv_ref, bv_other), (b1_ref, b1_other), (wo_hbm, wo_other), (w1_hbm, w1_other),
            (w2_hbm, w2_other)]:
        n = len(swaps)
        swaps.append(remote(src, dst, s_sem.at[n], r_sem.at[n], partner))
        swaps[-1].start()
    first = len(blocks) + 2
    attention(1)
    for copy in swaps[:first]:
        copy.wait()
    project(0, bq_other[...].reshape(1, -1), bv_other[...].reshape(1, -1))
    attention(0)
    for copy in swaps[first:]:
        copy.wait()
    loads.drain()


def attend(slots, tokens, weights, biases):
    rows, d = tokens.shape[0] // 2, tokens.shape[1]
    inner = weights[0].shape[1]
    shape, vmem, dma = jax.ShapeDtypeStruct, pltpu.VMEM, pltpu.SemaphoreType.DMA
    outs = ((rows, 3 * inner), BF), ((rows, inner), BF), ((rows, PAIR), F32), ((d, 3 * inner), BF)
    like = [shape(a.shape, a.dtype) for a in (*weights[3:], biases[2])]
    return pl.pallas_call(
        attend_kernel,
        out_shape=(*(shape((2, *s), t) for s, t in outs), *like),
        in_specs=[SM, SM, SM] + [ANY] * 7 + [VM] * 3,
        out_specs=(ANY,) * 7 + (VM,),
        scratch_shapes=[
            *(vmem((2, *s), t) for s, t in outs), vmem((rows, d), BF), vmem((inner,), F32), vmem((inner,), F32),
            dma((24,)), dma((16,)), dma((16,))],
        compiler_params=params(collective_id=3, has_side_effects=True),
        name="attend",
    )(*slots, tokens, *weights, *biases)


def norm(v, gain, shift):
    centre = v - jnp.mean(v, axis=-1, keepdims=True)
    inverse = lax.rsqrt(jnp.mean(centre * centre, axis=-1, keepdims=True) + NORM_EPS)
    normed = centre * inverse
    return normed * gain + shift, normed, inverse


def norm_back(e, normed, inverse, gain):
    scaled = e * gain
    plain = jnp.mean(scaled, axis=-1, keepdims=True)
    cross = jnp.mean(scaled * normed, axis=-1, keepdims=True)
    return inverse * (scaled - plain - normed * cross)


def gelu_terms(u):
    cdf = 0.5 + 0.5 * lax.erf(u * ROOT_HALF)
    return u * cdf, cdf + u * jnp.exp(-0.5 * u * u) * INV_ROOT_TAU


def column_sum(value):
    return jnp.sum(value, axis=0, keepdims=True)


def forward_kernel(
    long_ref, short_ref, count_ref, tok_hbm, cot_hbm, a_hbm, woo_hbm, wop_hbm, w1o_hbm, w1p_hbm, w2o_hbm,
    w2p_hbm, bo_ref, bp_ref, attn_bias_ref, a1_ref, s1_ref, ffn_bias_ref, a2_ref, s2_ref,
    result_out, pooled_ref, n1_out, r1_out, h_out, g_out, slope_out, df_out, dr_out, grad_ref,
    x_ref, cot_ref, a_ref, wo_ref, w1_ref, w2_ref, result_ref, n1_ref, r1_ref, h_ref, g_ref, slope_ref, df_ref, dr_ref,
    sem,
):
    loads = Loads(sem)
    stores = Loads(sem.at[pl.ds(16, 32)])
    inner = a_hbm.shape[2]
    load_rows(loads, "x", tok_hbm, x_ref)
    for k, wo_hbm in enumerate((wop_hbm, woo_hbm)):
        loads("x", a_hbm.at[k], a_ref.at[:, k * inner:(k + 1) * inner])
        loads("x", wo_hbm, wo_ref.at[k * inner:(k + 1) * inner])
    loads("w11", w1o_hbm, w1_ref.at[1])
    loads("w10", w1p_hbm, w1_ref.at[0])
    load_rows(loads, "tail", cot_hbm, cot_ref)
    loads("tail", w2o_hbm, w2_ref.at[1])
    loads("tail", w2p_hbm, w2_ref.at[0])
    lengths = my_slots(long_ref, short_ref, count_ref)
    rows_all = x_ref.shape[0]
    width = w1_ref.shape[2]
    attn_bias, a1, s1, ffn_bias, a2, s2 = (
        ref[...].reshape(1, -1) for ref in (attn_bias_ref, a1_ref, s1_ref, ffn_bias_ref, a2_ref, s2_ref))
    loads.need("x")
    tile = 256
    for i in range(rows_all // tile):
        rows = slice(i * tile, (i + 1) * tile)
        attn = dot(a_ref[rows, :], wo_ref[...]) + attn_bias
        h1, normed, inverse = norm(x_ref[rows, :].astype(F32) + attn, a1, s1)
        n1_ref[rows, :] = normed
        r1_ref[rows, :] = jnp.broadcast_to(inverse, (tile, 128))
        h_ref[rows, :] = h1.astype(BF)
    for ref, out in ((n1_ref, n1_out), (r1_ref, r1_out), (h_ref, h_out)):
        stores("out", ref, out)

    tile, chunk = 128, 512
    for k, b_ref in ((1, bo_ref), (0, bp_ref)):
        loads.need(f"w1{k}")
        b1 = b_ref[...].reshape(1, -1)
        for c in range(width // chunk):
            cols = slice(c * chunk, (c + 1) * chunk)
            for i in range(rows_all // tile):
                rows = slice(i * tile, (i + 1) * tile)
                g, slope = gelu_terms(dot(h_ref[rows, :], w1_ref[k, :, cols]) + b1[:, cols])
                g_ref[k, rows, cols] = g.astype(BF)
                slope_ref[k, rows, cols] = slope.astype(BF)
        stores("out", g_ref.at[k], g_out.at[k])
        stores("out", slope_ref.at[k], slope_out.at[k])

    loads.need("tail")
    tile = 256
    grad_ref[...] = jnp.zeros_like(grad_ref)
    pooled_ref[...] = jnp.zeros_like(pooled_ref)
    for i in range(rows_all // tile):
        rows = slice(i * tile, (i + 1) * tile)
        ffn = dot(g_ref[0, rows, :], w2_ref[0]) + dot(g_ref[1, rows, :], w2_ref[1]) + ffn_bias
        y, normed, inverse = norm(n1_ref[rows, :] * a1 + s1 + ffn, a2, s2)
        result_ref[rows, :] = y.astype(BF)
        step = LONG if i * tile < LONG else SHORT
        for k in range(max(tile // step, 1)):
            start = i * tile + k * step
            slot = 0 if start < LONG else 1 + (start - LONG) // SHORT
            count = min(step, tile)
            place = (start if slot == 0 else 0) + lax.broadcasted_iota(jnp.int32, (count, 1), 0)
            part = y[k * count:(k + 1) * count, :]
            pooled_ref[slot:slot + 1, :] += column_sum(jnp.where(place < lengths[slot], part, 0.0))
        e = cot_ref[rows, :].astype(F32)
        dr = norm_back(e, normed, inverse, a2)
        low = dr.astype(BF)
        dr_ref[rows, :] = dr
        df_ref[rows, :] = low
        grad_ref[0:1, :] += column_sum(low.astype(F32))
        grad_ref[1:2, :] += column_sum(e * normed)
        grad_ref[2:3, :] += column_sum(e)
        for ref, out in ((result_ref, result_out), (df_ref, df_out), (dr_ref, dr_out)):
            stores("out", ref.at[rows], out.at[rows])
    for slot, length in enumerate(lengths):
        pooled_ref[slot:slot + 1, :] = pooled_ref[slot:slot + 1, :] / jnp.maximum(length, 1).astype(F32)
    stores.drain()


def forward(slots, tokens, cot, a, wo, w1, w2, b1, vectors):
    rows, d = tokens.shape[0] // 2, tokens.shape[1]
    width = w1[0].shape[1]
    inner = a.shape[2]
    shape, vmem = jax.ShapeDtypeStruct, pltpu.VMEM
    return pl.pallas_call(
        forward_kernel,
        out_shape=(
            shape((rows, d), BF), shape((8, d), F32), shape((rows, d), F32), shape((rows, 128), F32),
            shape((rows, d), BF), shape((2, rows, width), BF), shape((2, rows, width), BF), shape((rows, d), BF),
            shape((rows, d), F32), shape((8, d), F32),
        ),
        in_specs=[SM, SM, SM] + [ANY] * 9 + [VM] * 8,
        out_specs=(ANY, VM) + (ANY,) * 7 + (VM,),
        scratch_shapes=[
            vmem((rows, d), BF), vmem((rows, d), BF), vmem((rows, 2 * inner), BF), vmem((2 * inner, d), BF),
            vmem((2, d, width), BF), vmem((2, width, d), BF), vmem((rows, d), BF), vmem((rows, d), F32),
            vmem((rows, 128), F32), vmem((rows, d), BF), vmem((2, rows, width), BF), vmem((2, rows, width), BF),
            vmem((rows, d), BF), vmem((rows, d), F32), pltpu.SemaphoreType.DMA((48,))],
        compiler_params=params(),
        cost_estimate=pl.CostEstimate(
            flops=2 * rows * d * (width * 4 + d), bytes_accessed=50 << 20, transcendentals=rows * width * 4),
        name="forward",
    )(*slots, tokens, cot, a, *wo, *w1, *w2, *b1, *vectors)


def peer(sub, bit):
    me = lax.axis_index("dp")
    group = me // sub
    value = (group // (1 << bit)) % 2
    other = me + (1 - 2 * value) * (sub << bit)
    return value, {"dp": other}


def remote(src, dst, s, r, device):
    return pltpu.make_async_remote_copy(
        src_ref=src, dst_ref=dst, send_sem=s, recv_sem=r, device_id=device, device_id_type=MESH)


SENDS = 4
ORDERS = ((0, 2, 1, 3), (1, 2, 0, 3), (2, 0, 1, 3))


class Halving:
    def __init__(self, sub, pieces, sums, sends, ins, s_sem, r_sem):
        self.links = [peer(sub, bit) for bit in range(BITS)]
        self.partner = {"tensor": 1 - lax.axis_index("tensor")}
        self.pieces, self.sums, self.sends, self.ins = pieces, sums, sends, ins
        self.s_sem, self.r_sem = s_sem, r_sem
        self.stage = {}
        self.copy = {}

    def greet(self):
        barrier = pltpu.get_barrier_semaphore()
        for device in [self.partner] + [link[1] for link in self.links]:
            pl.semaphore_signal(barrier, inc=1, device_id=device, device_id_type=MESH)

    def meet(self):
        pl.semaphore_wait(pltpu.get_barrier_semaphore(), BITS + 1)

    def region(self, n, count, bit=None):
        unit, cols, order = self.pieces[n]
        fixed = order[:count]
        index = [unit]
        for b in reversed(range(BITS)):
            value = self.links[b][0]
            index.append(value if b in fixed else 1 - value if b == bit else slice(None))
        return (*index, slice(None), cols)

    def brought(self, n, stage):
        unit, cols, _ = self.pieces[n]
        return (unit, *([slice(None)] * (BITS - stage)), slice(None), cols)

    def send(self, n, src, dst, stage, device):
        self.copy[n] = remote(src, dst, self.s_sem.at[n, stage], self.r_sem.at[n, stage], device)
        self.copy[n].start()
        self.stage[n] = stage

    def swap(self, slot, *ns):
        for n in ns:
            unit, cols, _ = self.pieces[n]
            every = [slice(None)] * (BITS + 1)
            self.send(n, self.sends.at[(slot + unit - self.pieces[ns[0]][0], *every, cols)],
                      self.ins[0].at[self.brought(n, 0)], 0, self.partner)

    def arrive(self, n):
        stage = self.stage[n]
        self.copy[n].wait()
        index = self.region(n, stage)
        brought = self.ins[stage][self.brought(n, stage)]
        if stage == BITS:
            return self.sums[index].astype(F32) + brought.astype(F32)
        self.sums[index] = self.sums[index] + brought
        return None

    def depart(self, n):
        stage = self.stage[n] + 1
        bit = self.pieces[n][2][stage - 1]
        self.send(n, self.sums.at[self.region(n, stage - 1, bit)], self.ins[stage].at[self.brought(n, stage)], stage,
                  self.links[bit][1])

    def move(self, *ns):
        for n in ns:
            self.arrive(n)
            self.depart(n)


def halving_scratch(units, pieces):
    shapes = ((2, 2, 2, 2), (2, 2, 2), (2, 2), (2,), ())
    return [pltpu.VMEM((units, *s, 48, UNIT), BF) for s in shapes] + [
        pltpu.SemaphoreType.DMA((pieces, BITS + 1)), pltpu.SemaphoreType.DMA((pieces, BITS + 1))]


def weight_grad(places, left, right):
    value = dot_tn(left, right).astype(BF)
    for k, (ref, u) in enumerate(places):
        ref[u] = value[:, k * UNIT:(k + 1) * UNIT].reshape(2, 2, 2, 2, 48, UNIT)


def backward_kernel(
    sub, pieces, long_ref, short_ref, count_ref, tok_hbm, df_hbm, h_hbm, dr_hbm, g_hbm, d_hbm, n1_hbm, r1_hbm, qkv_hbm,
    a_hbm, lse_hbm, wc_hbm, w1p_hbm, w1o_hbm, w2p_hbm, w2o_hbm, wop_hbm, woo_hbm, gain_ref, grad2_ref,
    outer_ref, inner_ref, q_ref, k_ref, v_ref, output_ref, dx_out, vec_out,
    df_ref, h_ref, g_ref, slope_ref, w1_ref, w2_ref, dx_ref, n1_ref, r1_ref, x_ref, lse_ref, low_ref,
    grad_ref, vsend_ref, vec_ref, vin_ref, sums_ref, send_ref,
    in0_ref, in1_ref, in2_ref, in3_ref, in4_ref, s_sem, r_sem, vs_sem, vr_sem, load_sem, swap_sem,
):
    rows_all, d = dx_ref.shape
    width = w1_ref.shape[2]
    inner = a_hbm.shape[2]
    pairs = inner // PAIR
    chunk = 2 * UNIT
    chunks = width // chunk
    half = halves()
    lengths = my_slots(long_ref, short_ref, count_ref)
    tensor = lax.axis_index("tensor")
    red = Halving(sub, pieces, sums_ref, send_ref, (in0_ref, in1_ref, in2_ref, in3_ref, in4_ref), s_sem, r_sem)
    red.greet()
    loads = Loads(load_sem)
    loads("df", df_hbm, df_ref)
    for c in range(chunks):
        cols = pl.ds(c * chunk, chunk)
        for k in range(2):
            loads(f"g{k}{c}", g_hbm.at[k, :, cols], g_ref.at[k, :, cols])
    loads("h", h_hbm, h_ref)
    for c in range(chunks):
        cols = pl.ds(c * chunk, chunk)
        for k, w2_hbm in enumerate((w2p_hbm, w2o_hbm)):
            loads(f"w{k}{c}", w2_hbm.at[cols], w2_ref.at[k, cols])
            loads(f"w{k}{c}", d_hbm.at[k, :, cols], slope_ref.at[k, :, cols])
    for k, w1_hbm in enumerate((w1p_hbm, w1o_hbm)):
        loads("dr", w1_hbm, w1_ref.at[k])
    loads("dr", dr_hbm, dx_ref)
    loads("norm", n1_hbm, n1_ref)
    loads("norm", r1_hbm, r1_ref)
    load_rows(loads, "x", tok_hbm, x_ref)
    for k in range(2):
        loads("heads", lse_hbm.at[k], lse_ref.at[k])

    def finish(*ns):
        for n in ns:
            unit, cols, _ = pieces[n]
            value = red.arrive(n)
            if unit < 4:
                outer_ref[:, unit * UNIT:(unit + 1) * UNIT] = value
            elif unit < 8:
                inner_ref[:, (unit - 4) * UNIT:(unit - 3) * UNIT] = value
            elif unit == 8:
                output_ref[...] = value
            else:
                for i in range(cols.start // PAIR, cols.stop // PAIR):
                    at = i * PAIR - cols.start
                    (q_ref, k_ref, v_ref)[i][:, (unit - 9) * PAIR:(unit - 8) * PAIR] = value[:, at:at + PAIR]

    loads.need("df")
    for c in range(chunks):
        cols = slice(c * chunk, (c + 1) * chunk)
        units = (2 * c, 2 * c + 1)
        loads.need(f"g0{c}")
        weight_grad([(send_ref, u % SENDS) for u in units], df_ref[...], g_ref[0, :, cols])
        if c == 0:
            red.meet()
        red.swap(units[0] % SENDS, *units)
        if c == 1:
            red.move(0, 1)
        loads.need(f"g1{c}")
        weight_grad([(sums_ref, u) for u in units], df_ref[...], g_ref[1, :, cols])

    bias_sums = [[], []]
    loads.need("h")
    for c in range(chunks):
        cols = slice(c * chunk, (c + 1) * chunk)
        units = (4 + 2 * c, 5 + 2 * c)
        for k, out_ref in enumerate((send_ref, sums_ref)):
            loads.need(f"w{k}{c}")
            for n in range(c * chunk, (c + 1) * chunk, 256):
                part = slice(n, n + 256)
                slope = slope_ref[k, :, part].astype(F32)
                du = (dot_nt(df_ref[...], w2_ref[k, part, :]) * slope).astype(BF)
                slope_ref[k, :, part] = du
                bias_sums[k].append(column_sum(du.astype(F32)))
            if k == 0:
                places = [(send_ref, u % SENDS) for u in units]
            else:
                places = [(sums_ref, u) for u in units]
            weight_grad(places, h_ref[...], slope_ref[k, :, cols])
            if k == 0:
                red.swap(units[0] % SENDS, *units)
            if (c, k) == (0, 0):
                red.move(2, 3)
            if (c, k) == (1, 0):
                red.move(0, 1)
            if (c, k) == (1, 1):
                red.move(4, 5)
    a_ref, da_ref = h_ref, df_ref
    for k in range(2):
        loads("heads", a_hbm.at[k], a_ref.at[:, k * inner:(k + 1) * inner])
        for p in range(pairs):
            loads("last", wc_hbm.at[k, :, p * 384:(p + 1) * 384],
                  w2_ref.at[p // 2, p % 2 * 768:(p % 2 + 1) * 768, k * 384:(k + 1) * 384])

    def wc(p):
        return w2_ref[p // 2, p % 2 * 768:(p % 2 + 1) * 768, :]

    def dqkv(p):
        return p // 2, slice(p % 2 * 768, (p % 2 + 1) * 768)

    loads.need("dr", "norm")
    grad_ref[...] = jnp.zeros_like(grad_ref)
    gain = gain_ref[...].reshape(1, -1)

    def first_norm(rows):
        e, normed = dx_ref[rows, :], n1_ref[rows, :]
        dr = norm_back(e, normed, r1_ref[rows, 0:1], gain)
        low = dr.astype(BF)
        dx_ref[rows, :] = dr
        low_ref[rows, :] = low
        grad_ref[0:1, :] += column_sum(low.astype(F32))
        grad_ref[1:2, :] += column_sum(e * normed)
        grad_ref[2:3, :] += column_sum(e)

    parts = [slice(i * rows_all // 2, (i + 1) * rows_all // 2) for i in range(2)]
    for i, rows in enumerate(parts):
        dx_ref[rows, :] += dot_nt(slope_ref[0, rows, :], w1_ref[0]) + dot_nt(slope_ref[1, rows, :], w1_ref[1])
        if i == 0:
            red.move(2, 3)
        first_norm(rows)
    for k, wo_hbm in enumerate((wop_hbm, woo_hbm)):
        loads("wo", wo_hbm, w1_ref.at[0, k * inner:(k + 1) * inner, 0:d])
        loads("qkv", qkv_hbm.at[k], slope_ref.at[k, :, 0:3 * inner])
    red.move(0, 1)
    red.move(6, 7)
    loads.need("heads")
    weight_grad([(send_ref, 0), (sums_ref, 8)], low_ref[...], a_ref[...])
    red.swap(0, 8)
    loads.need("wo")
    da_ref[...] = dot_nt(low_ref[...], w1_ref[0, :, 0:d]).astype(BF)
    red.move(4, 5, 2, 3, 0, 1, 8)
    loads.need("qkv", "x")

    slots = [slot_parts(kind, lengths) for kind in range(2)]

    def attention(p, k):
        at = k * inner + p * PAIR
        q_cols, k_cols, v_cols = (slice(p * 384 + j * 128, p * 384 + (j + 1) * 128) for j in range(3))

        def scores(kind, h):
            s, dp = [], []
            for rows, scale, key_bias in slots[kind]:
                q = slope_ref[k, rows, q_cols] * scale
                s.append(dot_nt(keep(half == h, q), slope_ref[k, rows, k_cols]) + key_bias)
                dp.append(dot_nt(keep(half == h, da_ref[rows, at:at + PAIR]), slope_ref[k, rows, v_cols]))
            return stack(s), stack(dp)

        def grads(kind, h, prob, ds):
            dq, dk, dv = [], [], []
            for i, (rows, scale, _) in enumerate(slots[kind]):
                count = rows.stop - rows.start
                part = slice(i * count, (i + 1) * count)
                dv.append(dot_tn(prob[part], keep(half == h, da_ref[rows, at:at + PAIR])))
                dk.append(dot_tn(ds[part], keep(half == h, slope_ref[k, rows, q_cols] * scale)))
                dq.append(dot(ds[part], keep(half == h, slope_ref[k, rows, k_cols] * scale)))
            return stack(dq), stack(dk), stack(dv)

        tasks = [(kind, h) for kind in range(2) for h in range(2)]
        ahead = scores(*tasks[0])
        held = None
        for i, (kind, h) in enumerate(tasks):
            s, dp = ahead
            if i + 1 < len(tasks):
                ahead = scores(*tasks[i + 1])
            rows = slice(slots[kind][0][0].start, slots[kind][-1][0].stop)
            product = da_ref[rows, at:at + PAIR].astype(F32) * a_ref[rows, at:at + PAIR].astype(F32)
            delta = jnp.sum(keep(half == h, product), axis=1, keepdims=True)
            lane = h * HEAD_DIM + p
            prob = jnp.exp(s - lse_ref[k, rows, lane:lane + 1])
            value = grads(kind, h, prob.astype(BF), (prob * (dp - delta)).astype(BF))
            if h == 0:
                held = value
                continue
            slot, cols = dqkv(p)
            for j in range(3):
                at_col = cols.start + k * 384 + j * 128
                g_ref[slot, rows, at_col:at_col + 128] = (held[j] + value[j]).astype(BF)

    last = tuple(n for n, piece in enumerate(pieces) if piece[0] == 11)
    after = {
        (0, 0): lambda: None,
        (0, 1): lambda: finish(0, 1),
        (1, 0): lambda: red.move(6, 7, 4, 5, 2, 3, 9),
        (1, 1): lambda: (finish(2, 3), red.move(8)),
        (2, 0): lambda: red.move(10, 4, 5, 6, 7),
        (2, 1): lambda: (finish(4, 5), red.move(8, 9)),
    }
    for p in range(pairs):
        for k in range(2):
            attention(p, k)
            if k == 1:
                slot, cols = dqkv(p)
                weight_grad([(send_ref, 1 + p), (sums_ref, 9 + p)], x_ref[...], g_ref[slot, :, cols])
                red.swap(1 + p, *((9 + p,) if p < 2 else last))
            after[p, k]()

    for k, ref in enumerate((vsend_ref, vec_ref.at[0])):
        ref[...] = jnp.zeros(ref.shape, F32)
        ref[0:3, :] = grad_ref[0:3, :]
        ref[3:6, :] = grad2_ref[0:3, :]
        for n, sums in enumerate(bias_sums[k]):
            ref[6 + n // 3:7 + n // 3, n % 3 * 256:(n % 3 + 1) * 256] = sums
        for p in range(pairs):
            slot, cols = dqkv(p)
            sums = column_sum(g_ref[slot, :, cols.start + k * 384:cols.start + (k + 1) * 384].astype(F32))
            ref[8:9, p * PAIR:(p + 1) * PAIR] = sums[:, 0:128]
            ref[8:9, inner + p * PAIR:inner + (p + 1) * PAIR] = sums[:, 256:384]
    vnow = remote(vsend_ref, vin_ref.at[BITS], vs_sem.at[BITS], vr_sem.at[BITS], red.partner)
    vnow.start()
    loads.need("last")
    red.move(*last)
    tile = 256
    span = rows_all // 2
    outs = []
    for i in range(rows_all // tile):
        rows = slice(i * tile, (i + 1) * tile)
        dx_ref[rows, :] += sum(dot_nt(g_ref[dqkv(p)[0], rows, dqkv(p)[1]], wc(p)) for p in range(pairs))
        if i * tile % span == span - tile:
            g = i * tile // span
            here = dx_ref.at[pl.ds(g * span, span)]
            there = dx_out.at[pl.ds(pl.multiple_of((2 * g + tensor) * span, span), span)]
            loads("dx", here, there)
            outs.append(remote(here, there, swap_sem.at[0, g], swap_sem.at[1, g], red.partner))
            outs[-1].start()
        if i < BITS:
            vnow.wait()
            if i == 0:
                vec_ref[0] = vec_ref[0] + vin_ref[BITS]
            else:
                vec_ref[i] = vec_ref[i - 1] + vin_ref[i - 1]
            vnow = remote(vec_ref.at[i], vin_ref.at[i], vs_sem.at[i], vr_sem.at[i], red.links[i][1])
            vnow.start()
        if i == 1:
            red.move(6, 7, 8, 9)
        if i == 2:
            red.move(10)
        if i == 3:
            red.move(*last)
            finish(6, 7, 8)
    red.move(9, 10, *last)
    finish(9)
    red.move(10, *last)
    vnow.wait()
    vec_out[...] = vec_ref[BITS - 1] + vin_ref[BITS - 1]
    finish(10, *last)
    for copy in outs:
        copy.wait()
    loads.drain()


def backward(sub, slots, tokens, df, h, dr, g, slope, n1, r1, qkv, a, lse, wc, w1, w2, wo, gain, grad2):
    rows, d = df.shape
    inner = a.shape[2]
    ff = w1[0].shape[1]
    units = 2 * ff // UNIT + 1 + 3 * inner // UNIT
    whole = slice(0, UNIT)
    pieces = [(u, whole, ORDERS[u % 2]) for u in range(units - 1)]
    pieces += [(units - 1, slice(j * PAIR, (j + 1) * PAIR), ORDERS[j]) for j in range(3)]
    shape, vmem, dma = jax.ShapeDtypeStruct, pltpu.VMEM, pltpu.SemaphoreType.DMA
    return pl.pallas_call(
        functools.partial(backward_kernel, sub, pieces),
        out_shape=(
            shape((48, ff), F32), shape((48, ff), F32), shape((48, inner), F32), shape((48, inner), F32),
            shape((48, inner), F32), shape((48, inner), F32), shape((2 * rows, d), F32), shape((16, d), F32),
        ),
        in_specs=[SM, SM, SM] + [ANY] * 18 + [VM] * 2,
        out_specs=(VM, VM, VM, VM, VM, VM, ANY, VM),
        scratch_shapes=[
            vmem((rows, d), BF), vmem((rows, d), BF), vmem((2, rows, ff), BF), vmem((2, rows, ff), BF),
            vmem((2, d, ff), BF), vmem((2, ff, d), BF), vmem((rows, d), F32), vmem((rows, d), F32),
            vmem((rows, 128), F32), vmem((rows, d), BF), vmem((2, rows, PAIR), F32), vmem((rows, d), BF),
            vmem((8, d), F32), vmem((16, d), F32), vmem((BITS, 16, d), F32), vmem((BITS + 1, 16, d), F32),
            vmem((units, 2, 2, 2, 2, 48, UNIT), BF), vmem((SENDS, 2, 2, 2, 2, 48, UNIT), BF),
            *halving_scratch(units, len(pieces)), dma((BITS + 1,)), dma((BITS + 1,)), dma((48,)), dma((2, 2)),
        ],
        compiler_params=params(collective_id=1, has_side_effects=True),
        name="backward",
    )(*slots, tokens, df, h, dr, g, slope, n1, r1, qkv, a, lse, wc, *w1, *w2, *wo, gain, grad2)


def deliver_kernel(
    short_half, own_hbm, other_hbm, pool_own_ref, pool_other_ref, dx_hbm, total_ref, *refs,
):
    grads = refs[:6]
    result_out, pooled_out, dx_out = refs[6:9]
    grad_outs = refs[9:15]
    shard_outs = refs[15:21]
    bq_out, bv_out, b1_out, dx_ref, result_ref, sem = refs[21:]
    tensor = lax.axis_index("tensor")
    loads = Loads(sem)
    half = own_hbm.shape[0] // 2
    parts = 4 * half // 256
    moves = []
    for n in range(parts):
        rows = pl.ds(n * 256, 256)
        moves.append((dx_hbm.at[rows], dx_ref.at[rows], dx_out.at[rows]))
    for n, (hbm, place) in enumerate(((own_hbm, tensor), (other_hbm, 1 - tensor))):
        for k in range(2):
            here = pl.ds((2 * n + k) * half, half)
            moves.append((hbm.at[pl.ds(k * half, half)], result_ref.at[here],
                          result_out.at[pl.ds(pl.multiple_of((2 * k + place) * half, half), half)]))
    for n, (src, here, _) in enumerate(moves):
        loads(n, src, here)
    for src, dst in zip(grads, grad_outs):
        dst[...] = src[...]
    first = jnp.where(tensor == 0, pool_own_ref[...], pool_other_ref[...])
    second = jnp.where(tensor == 0, pool_other_ref[...], pool_own_ref[...])
    pooled_out[0:1, :] = first[0:1]
    pooled_out[1:2, :] = second[0:1]
    pooled_out[2:2 + short_half, :] = first[1:1 + short_half]
    pooled_out[2 + short_half:2 + 2 * short_half, :] = second[1:1 + short_half]
    total = total_ref[...]
    d = total.shape[1]
    share = shard_outs[0].shape[0]
    start = lax.axis_index("dp") * share
    moved = pltpu.roll(total[0:8, :], (d - start) % d, 1)
    for k, out in enumerate(shard_outs):
        out[...] = moved[k, 0:share]
    inner = bq_out.shape[0]
    bq_out[...] = total[8, 0:inner]
    bv_out[...] = total[8, inner:2 * inner]
    b1_out[0:d] = total[6]
    b1_out[d:2 * d] = total[7]
    for n, (_, here, dst) in enumerate(moves):
        loads.need(n)
        loads("out", here, dst)
    loads.drain()


def deliver(own, other, pool_own, pool_other, dx, total, grads, share, inner, short_half):
    rows, d = own.shape
    shape = jax.ShapeDtypeStruct
    return pl.pallas_call(
        functools.partial(deliver_kernel, short_half),
        out_shape=(
            shape((2 * rows, d), BF), shape((2 + 2 * short_half, d), F32), shape((2 * rows, d), F32),
            *(shape(g.shape, F32) for g in grads), *(shape((share,), F32) for _ in range(6)),
            shape((inner,), F32), shape((inner,), F32), shape((2 * d,), F32),
        ),
        in_specs=[ANY, ANY, VM, VM, ANY, VM] + [VM] * 6,
        out_specs=(ANY, VM, ANY) + (VM,) * 15,
        scratch_shapes=[pltpu.VMEM(dx.shape, F32), pltpu.VMEM((2 * rows, d), BF), pltpu.SemaphoreType.DMA((32,))],
        compiler_params=params(),
        name="deliver",
    )(own, other, pool_own, pool_other, dx, total, *grads)


def per_device(
    dp_size, tokens, cotangent, long_lengths, short_lengths, live_counts, query_weight, query_bias, key_weight,
    value_weight, value_bias, output_weight, output_bias, attn_gain, attn_shift, inner_weight, inner_bias,
    outer_weight, outer_bias, ffn_gain, ffn_shift,
):
    d = tokens.shape[1]
    sub = dp_size // GROUPS
    slots = (long_lengths, short_lengths, live_counts)

    def swap(a):
        return lax.ppermute(a, "tensor", [(0, 1), (1, 0)])

    qkv, a, lse, wc, wo_other, w1_other, w2_other, b1_other = attend(
        slots, tokens, (query_weight, key_weight, value_weight, output_weight, inner_weight, outer_weight),
        (query_bias, value_bias, inner_bias))
    wo, w1, w2 = (wo_other, output_weight), (w1_other, inner_weight), (w2_other, outer_weight)
    result, pooled, n1, r1, h, g, slope, df, dr, grad2 = forward(
        slots, tokens, cotangent, a, wo[::-1], w1[::-1], w2[::-1], (inner_bias, b1_other),
        (output_bias, attn_gain, attn_shift, outer_bias, ffn_gain, ffn_shift))
    result_other, pooled_other = swap(result), swap(pooled)
    *grads, dx, total = backward(
        sub, slots, tokens, df, h, dr, g, slope, n1, r1, qkv, a, lse, wc, w1, w2, wo, attn_gain, grad2)
    if sub > 1:
        groups = [[g * sub + i for i in range(sub)] for g in range(GROUPS)]
        grads = [lax.psum_scatter(g, "dp", scatter_dimension=0, axis_index_groups=groups, tiled=True) for g in grads]
        total = lax.psum(total, "dp", axis_index_groups=groups)
    (result_all, pooled_all, dx_all, d_outer, d_inner, d_q, d_k, d_v, d_output, *shards, d_bq, d_bv, d_b1) = deliver(
        result, result_other, pooled, pooled_other, dx, total, grads, d // dp_size, query_weight.shape[1],
        short_lengths.shape[0] // 2)
    return (
        result_all, pooled_all, dx_all, d_q, d_bq, d_k, d_v, d_bv, d_output.T, *shards[:3], d_inner, d_b1, d_outer.T,
        *shards[3:],
    )


def solution(mesh):
    in_specs = (
        P("dp", None), P("dp", None), P("dp"), P("dp"), P("dp", None), P(None, "tensor"), P("tensor"),
        P(None, "tensor"), P(None, "tensor"), P("tensor"), P("tensor", None), P(), P(), P(), P(None, "tensor"),
        P("tensor"), P("tensor", None), P(), P(), P(),
    )
    out_specs = (
        P("dp", None), P("dp", None), P("dp", None), P("dp", "tensor"), P("tensor"), P("dp", "tensor"),
        P("dp", "tensor"), P("tensor"), P("tensor", "dp"), P("dp"), P("dp"), P("dp"), P("dp", "tensor"),
        P("tensor"), P("tensor", "dp"), P("dp"), P("dp"), P("dp"),
    )
    return jax.shard_map(
        functools.partial(per_device, mesh.shape["dp"]), mesh=mesh, in_specs=in_specs, out_specs=out_specs,
        check_vma=False)
```

```python
import functools

import jax
import jax.numpy as jnp
from jax import lax
from jax.experimental import pallas as pl
from jax.experimental.pallas import tpu as pltpu
from jax.sharding import PartitionSpec as P

HEAD_DIM = 64
LONG = 512
SHORT = 128
PAIR = 128
NORM_EPS = 1e-12
MASKED = -1000000000.0
SCORE_SCALE = 0.125
INV_ROOT_TAU = 0.3989422804014327
ROOT_HALF = 0.7071067811865476
BF = jnp.bfloat16
F32 = jnp.float32
MESH = pl.DeviceIdType.MESH
UNIT = 384
BITS = 4
GROUPS = 1 << BITS

VM = pl.BlockSpec(memory_space=pltpu.VMEM)
SM = pl.BlockSpec(memory_space=pltpu.SMEM)
ANY = pl.BlockSpec(memory_space=pl.ANY)


def params(**more):
    return pltpu.CompilerParams(vmem_limit_bytes=62 << 20, **more)


def dot(a, b):
    return jnp.dot(a, b, preferred_element_type=F32)


def dot_nt(a, b):
    return lax.dot_general(a, b, (((1,), (1,)), ((), ())), preferred_element_type=F32)


def dot_tn(a, b):
    return lax.dot_general(a, b, (((0,), (0,)), ((), ())), preferred_element_type=F32)


def spans(start, unit, size=None):
    return pl.ds(pl.multiple_of(start, unit), unit if size is None else size)


def my_slots(long_ref, short_ref, count_ref):
    tensor = lax.axis_index("tensor")
    n_long, n_short = long_ref.shape[0] // 2, short_ref.shape[0] // 2
    lengths = []
    for ref, n, column in ((long_ref, n_long, 0), (short_ref, n_short, 1)):
        for j in range(n):
            slot = tensor * n + j
            lengths.append(jnp.where(slot < count_ref[0, column], ref[slot], 0))
    return lengths


def my_rows(whole_ref, mine_ref, sem):
    tensor = lax.axis_index("tensor")
    half = mine_ref.shape[0] // 2
    return [
        pltpu.make_async_copy(
            whole_ref.at[pl.ds(pl.multiple_of((2 * k + tensor) * half, half), half)],
            mine_ref.at[pl.ds(k * half, half)], sem.at[k])
        for k in range(2)
    ]


def key_terms(length, count):
    keys = lax.broadcasted_iota(jnp.int32, (1, count), 1)
    scale = jnp.where(length > 0, SCORE_SCALE, 0.0).astype(BF)
    bias = jnp.where((keys < length) | (length <= 0), 0.0, MASKED)
    return scale, bias


def halves():
    return lax.broadcasted_iota(jnp.int32, (1, PAIR), 1) // HEAD_DIM


class Loads:
    def __init__(self, sem):
        self.sem, self.count, self.open = sem, 0, {}

    def __call__(self, name, src, dst):
        copy = pltpu.make_async_copy(src, dst, self.sem.at[self.count])
        self.count += 1
        self.open.setdefault(name, []).append(copy)
        copy.start()

    def need(self, *names):
        for name in names:
            for copy in self.open.pop(name):
                copy.wait()

    def drain(self):
        self.need(*list(self.open))


def load_rows(loads, name, whole_ref, mine_ref):
    tensor = lax.axis_index("tensor")
    half = mine_ref.shape[0] // 2
    for k in range(2):
        loads(name, whole_ref.at[pl.ds(pl.multiple_of((2 * k + tensor) * half, half), half)],
              mine_ref.at[pl.ds(k * half, half)])


def slot_parts(kind, lengths):
    if kind == 0:
        return [(slice(0, LONG), *key_terms(lengths[0], LONG))]
    return [
        (slice(LONG + SHORT * s, LONG + SHORT * (s + 1)), *key_terms(length, SHORT))
        for s, length in enumerate(lengths[1:])]


def stack(values):
    return values[0] if len(values) == 1 else jnp.concatenate(values, axis=0)


def keep(own, value, other=None):
    return jnp.where(own, value, jnp.zeros_like(value) if other is None else other)


def norm(v, gain, shift):
    centre = v - jnp.mean(v, axis=-1, keepdims=True)
    inverse = lax.rsqrt(jnp.mean(centre * centre, axis=-1, keepdims=True) + NORM_EPS)
    normed = centre * inverse
    return normed * gain + shift, normed, inverse


def norm_back(e, normed, inverse, gain):
    scaled = e * gain
    plain = jnp.mean(scaled, axis=-1, keepdims=True)
    cross = jnp.mean(scaled * normed, axis=-1, keepdims=True)
    return inverse * (scaled - plain - normed * cross)


def gelu_terms(u):
    cdf = 0.5 + 0.5 * lax.erf(u * ROOT_HALF)
    return u * cdf, cdf + u * jnp.exp(-0.5 * u * u) * INV_ROOT_TAU


def column_sum(value):
    return jnp.sum(value, axis=0, keepdims=True)


def forward_kernel(
    long_ref, short_ref, count_ref, tok_hbm, cot_hbm, wq_hbm, wk_hbm, wv_hbm, wo_hbm, w1_hbm, w2_hbm,
    bq_ref, bv_ref, b1_ref, attn_bias_ref, a1_ref, s1_ref, ffn_bias_ref, a2_ref, s2_ref,
    qkv_out, a_out, lse_out, wc_out, wo_out, w1_out, w2_out, result_out, n1_out, r1_out, h_out, g_out, slope_out,
    df_out, dr_out, pooled_ref, grad_ref,
    x_ref, cot_ref, qkv_ref, a_ref, lse_ref, wc_ref, wo_ref, w1_ref, w2_ref, result_ref, n1_ref, r1_ref, h_ref, g_ref,
    slope_ref, df_ref, dr_ref, bq_other, bv_other, b1_other, load_sem, store_sem, s_sem, r_sem,
):
    rows_all, width = x_ref.shape[0], w1_ref.shape[2]
    pairs = qkv_ref.shape[2] // (3 * PAIR)
    inner = pairs * PAIR
    partner = {"tensor": 1 - lax.axis_index("tensor")}
    barrier = pltpu.get_barrier_semaphore()
    pl.semaphore_signal(barrier, inc=1, device_id=partner, device_id_type=MESH)
    loads, stores = Loads(load_sem), Loads(store_sem)
    load_rows(loads, "x", tok_hbm, x_ref)
    blocks = []
    for p in range(pairs):
        for j, w_hbm in enumerate((wq_hbm, wk_hbm, wv_hbm)):
            at = (3 * p + j) * PAIR
            blocks.append((w_hbm.at[:, p * PAIR:(p + 1) * PAIR], slice(at, at + PAIR)))
    for src, cols in blocks:
        loads("x", src, wc_ref.at[1, :, cols])
    lengths = my_slots(long_ref, short_ref, count_ref)
    half = halves()
    lane = lax.broadcasted_iota(jnp.int32, (1, PAIR), 1) % HEAD_DIM
    slots = [slot_parts(kind, lengths) for kind in range(2)]

    def project(k, bq, bv):
        parts = []
        for p in range(pairs):
            cols = slice(p * PAIR, (p + 1) * PAIR)
            parts += [bq[:, cols], jnp.zeros((1, PAIR), F32), bv[:, cols]]
        qkv_ref[k] = (dot(x_ref[...], wc_ref[k]) + jnp.concatenate(parts, axis=1)).astype(BF)
        stores("out", qkv_ref.at[k], qkv_out.at[k])
        stores("out", wc_ref.at[k], wc_out.at[k])

    def attention(k):
        def scores(kind, p, h):
            out = []
            for rows, scale, key_bias in slots[kind]:
                q = qkv_ref[k, rows, p * 384:p * 384 + 128] * scale
                out.append(dot_nt(keep(half == h, q), qkv_ref[k, rows, p * 384 + 128:p * 384 + 256]) + key_bias)
            return stack(out)

        def mix(kind, p, h, e):
            out = []
            for i, (rows, _, _) in enumerate(slots[kind]):
                v = qkv_ref[k, rows, p * 384 + 256:p * 384 + 384]
                count = rows.stop - rows.start
                out.append(dot(e[i * count:(i + 1) * count], keep(half == h, v, jnp.ones_like(v))))
            return stack(out)

        tasks = [(kind, p, h) for p in range(pairs) for kind in range(2) for h in range(2)]
        ahead = scores(*tasks[0])
        held = None
        for i, (kind, p, h) in enumerate(tasks):
            s = ahead
            if i + 1 < len(tasks):
                ahead = scores(*tasks[i + 1])
            high = jnp.max(s, axis=1, keepdims=True)
            mixed = mix(kind, p, h, jnp.exp(s - high).astype(BF))
            if h == 0:
                held = high, mixed
                continue
            rows = slice(slots[kind][0][0].start, slots[kind][-1][0].stop)
            total = pltpu.roll(jnp.where(half == 0, mixed, held[1]), HEAD_DIM, 1)
            at = k * inner + p * PAIR
            a_ref[rows, at:at + PAIR] = (jnp.where(half == 0, held[1], mixed) / total).astype(BF)
            lse = jnp.where(half == 0, held[0], high) + jnp.log(total)
            lse_ref[k, rows, :] = lse if p == 0 else jnp.where(lane == p, lse, lse_ref[k, rows, :])
        stores("out", lse_ref.at[k], lse_out.at[k])

    loads.need("x")
    project(1, bq_ref[...].reshape(1, -1), bv_ref[...].reshape(1, -1))
    pl.semaphore_wait(barrier, 1)
    swaps = []
    for src, dst in [(src, wc_ref.at[0, :, cols]) for src, cols in blocks] + [
            (bq_ref, bq_other), (bv_ref, bv_other), (b1_ref, b1_other), (wo_hbm, wo_ref.at[0:inner]),
            (w1_hbm, w1_ref.at[0]), (w2_hbm, w2_ref.at[0])]:
        n = len(swaps)
        swaps.append(remote(src, dst, s_sem.at[n], r_sem.at[n], partner))
        swaps[-1].start()
    loads("wo", wo_hbm, wo_ref.at[inner:2 * inner])
    loads("w1", w1_hbm, w1_ref.at[1])
    load_rows(loads, "tail", cot_hbm, cot_ref)
    loads("tail", w2_hbm, w2_ref.at[1])
    attention(1)
    for copy in swaps[:-4]:
        copy.wait()
    project(0, bq_other[...].reshape(1, -1), bv_other[...].reshape(1, -1))
    attention(0)
    for copy in swaps[-4:-2]:
        copy.wait()
    loads.need("wo", "w1")
    stores("out", a_ref, a_out)
    stores("out", wo_ref.at[0:inner], wo_out)

    attn_bias, a1, s1, ffn_bias, a2, s2 = (
        ref[...].reshape(1, -1) for ref in (attn_bias_ref, a1_ref, s1_ref, ffn_bias_ref, a2_ref, s2_ref))
    tile = 256
    for i in range(rows_all // tile):
        rows = slice(i * tile, (i + 1) * tile)
        attn = dot(a_ref[rows, :], wo_ref[...]) + attn_bias
        h1, normed, inverse = norm(x_ref[rows, :].astype(F32) + attn, a1, s1)
        n1_ref[rows, :] = normed
        r1_ref[rows, :] = jnp.broadcast_to(inverse, (tile, 128))
        h_ref[rows, :] = h1.astype(BF)
    for ref, out in ((n1_ref, n1_out), (r1_ref, r1_out), (h_ref, h_out)):
        stores("out", ref, out)

    tile, chunk = 128, 512
    for k, b_ref in ((1, b1_ref), (0, b1_other)):
        if k == 0:
            swaps[-2].wait()
            stores("out", w1_ref.at[0], w1_out)
        b1 = b_ref[...].reshape(1, -1)
        for c in range(width // chunk):
            cols = slice(c * chunk, (c + 1) * chunk)
            for i in range(rows_all // tile):
                rows = slice(i * tile, (i + 1) * tile)
                g, slope = gelu_terms(dot(h_ref[rows, :], w1_ref[k, :, cols]) + b1[:, cols])
                g_ref[k, rows, cols] = g.astype(BF)
                slope_ref[k, rows, cols] = slope.astype(BF)
        stores("out", g_ref.at[k], g_out.at[k])
        stores("out", slope_ref.at[k], slope_out.at[k])

    swaps[-1].wait()
    stores("out", w2_ref.at[0], w2_out)
    loads.need("tail")
    tile = 256
    grad_ref[...] = jnp.zeros_like(grad_ref)
    pooled_ref[...] = jnp.zeros_like(pooled_ref)
    for i in range(rows_all // tile):
        rows = slice(i * tile, (i + 1) * tile)
        ffn = dot(g_ref[0, rows, :], w2_ref[0]) + dot(g_ref[1, rows, :], w2_ref[1]) + ffn_bias
        y, normed, inverse = norm(n1_ref[rows, :] * a1 + s1 + ffn, a2, s2)
        result_ref[rows, :] = y.astype(BF)
        step = LONG if i * tile < LONG else SHORT
        for k in range(max(tile // step, 1)):
            start = i * tile + k * step
            slot = 0 if start < LONG else 1 + (start - LONG) // SHORT
            count = min(step, tile)
            place = (start if slot == 0 else 0) + lax.broadcasted_iota(jnp.int32, (count, 1), 0)
            part = y[k * count:(k + 1) * count, :]
            pooled_ref[slot:slot + 1, :] += column_sum(jnp.where(place < lengths[slot], part, 0.0))
        e = cot_ref[rows, :].astype(F32)
        dr = norm_back(e, normed, inverse, a2)
        low = dr.astype(BF)
        dr_ref[rows, :] = dr
        df_ref[rows, :] = low
        grad_ref[0:1, :] += column_sum(low.astype(F32))
        grad_ref[1:2, :] += column_sum(e * normed)
        grad_ref[2:3, :] += column_sum(e)
        for ref, out in ((result_ref, result_out), (df_ref, df_out), (dr_ref, dr_out)):
            stores("out", ref.at[rows], out.at[rows])
    for slot, length in enumerate(lengths):
        pooled_ref[slot:slot + 1, :] = pooled_ref[slot:slot + 1, :] / jnp.maximum(length, 1).astype(F32)
    stores.drain()


def forward(slots, tokens, cot, weights, biases, vectors):
    rows, d = tokens.shape[0] // 2, tokens.shape[1]
    inner, width = weights[0].shape[1], weights[4].shape[1]
    shape, vmem, dma = jax.ShapeDtypeStruct, pltpu.VMEM, pltpu.SemaphoreType.DMA
    row, row_f32 = ((rows, d), BF), ((rows, d), F32)
    qkv, a, lse, wc = ((2, rows, 3 * inner), BF), ((rows, 2 * inner), BF), ((2, rows, PAIR), F32), ((2, d, 3 * inner), BF)
    hidden, r1 = ((2, rows, width), BF), ((rows, 128), F32)
    outs = [qkv, a, lse, wc, *((w.shape, BF) for w in weights[3:]), row, row_f32, r1, row, hidden, hidden, row, row_f32,
            ((8, d), F32), ((8, d), F32)]
    scratch = [row, row, qkv, a, lse, wc, ((2 * inner, d), BF), ((2, d, width), BF), ((2, width, d), BF), row, row_f32, r1,
               row, hidden, hidden, row, row_f32, *((b.shape, F32) for b in biases)]
    return pl.pallas_call(
        forward_kernel,
        out_shape=[shape(*o) for o in outs],
        in_specs=[SM, SM, SM] + [ANY] * 8 + [VM] * 9,
        out_specs=[ANY] * 15 + [VM] * 2,
        scratch_shapes=[*(vmem(*s) for s in scratch), dma((20,)), dma((40,)), dma((16,)), dma((16,))],
        compiler_params=params(collective_id=3, has_side_effects=True),
        name="forward",
    )(*slots, tokens, cot, *weights, *biases, *vectors)


def peer(sub, bit):
    me = lax.axis_index("dp")
    group = me // sub
    value = (group // (1 << bit)) % 2
    other = me + (1 - 2 * value) * (sub << bit)
    return value, {"dp": other}


def remote(src, dst, s, r, device):
    return pltpu.make_async_remote_copy(
        src_ref=src, dst_ref=dst, send_sem=s, recv_sem=r, device_id=device, device_id_type=MESH)


SENDS = 4
PIECES = (
    (0, 2, 0, 384, (1, 0, 3, 2)),
    (2, 2, 0, 384, (0, 2, 1, 3)),
    (4, 2, 0, 384, (2, 1, 0, 3)),
    (6, 2, 0, 384, (1, 2, 0, 3)),
    (8, 1, 0, 384, (0, 1, 3, 2)),
    (9, 1, 0, 384, (0, 2, 1, 3)),
    (10, 1, 0, 384, (1, 0, 2, 3)),
    (11, 1, 0, 128, (2, 1, 0, 3)),
    (11, 1, 128, 256, (1, 0, 2, 3)),
    (11, 1, 256, 384, (1, 0, 3, 2)),
)
PLAN = {
    "A11": (0,),
    "B00w": (1,),
    "B10u": (2,),
    "C0": (0, 3,),
    "C1": (1,),
    "F00": (0, 2, 4,),
    "F0w": (1,),
    "F10": (3, 5,),
    "F11": (0, 4, 2,),
    "F20": (1, 6,),
    "F21": (0, 3, 4, 5,),
    "F2w": (2,),
    "vec": (1, 7, 8,),
    "G0": (9, 6, 3,),
    "G1": (4, 5,),
    "G2": (8,),
    "end": (9, 7, 2, 6, 5, 8, 4, 9, 7, 3, 6, 8, 7, 5, 9, 6, 8, 7, 9,),
}


class Halving:
    def __init__(self, sub, pieces, sums, sends, ins, s_sem, r_sem):
        self.links = [peer(sub, bit) for bit in range(BITS)]
        self.partner = {"tensor": 1 - lax.axis_index("tensor")}
        self.pieces, self.sums, self.sends, self.ins = pieces, sums, sends, ins
        self.s_sem, self.r_sem = s_sem, r_sem
        self.stage = {}
        self.copy = {}

    def greet(self):
        barrier = pltpu.get_barrier_semaphore()
        for device in [self.partner] + [link[1] for link in self.links]:
            pl.semaphore_signal(barrier, inc=1, device_id=device, device_id_type=MESH)

    def meet(self):
        pl.semaphore_wait(pltpu.get_barrier_semaphore(), BITS + 1)

    def region(self, n, count, bit=None):
        units, cols, order = self.pieces[n]
        fixed = order[:count]
        index = [units]
        for b in reversed(range(BITS)):
            value = self.links[b][0]
            index.append(value if b in fixed else 1 - value if b == bit else slice(None))
        return (*index, slice(None), cols)

    def brought(self, n, stage):
        units, cols, _ = self.pieces[n]
        return (units, *([slice(None)] * (BITS - stage)), slice(None), cols)

    def send(self, n, src, dst, stage, device):
        self.copy[n] = remote(src, dst, self.s_sem.at[n, stage], self.r_sem.at[n, stage], device)
        self.copy[n].start()
        self.stage[n] = stage

    def swap(self, slot, unit):
        for n, (units, cols, _) in enumerate(self.pieces):
            if units.start == unit:
                out = slice(slot, slot + units.stop - units.start)
                self.send(n, self.sends.at[(out, *([slice(None)] * (BITS + 1)), cols)],
                          self.ins[0].at[self.brought(n, 0)], 0, self.partner)

    def arrive(self, n):
        stage = self.stage[n]
        self.copy[n].wait()
        index = self.region(n, stage)
        brought = self.ins[stage][self.brought(n, stage)]
        if stage == BITS:
            return self.sums[index].astype(F32) + brought.astype(F32)
        self.sums[index] = self.sums[index] + brought
        return None

    def depart(self, n):
        stage = self.stage[n] + 1
        bit = self.pieces[n][2][stage - 1]
        self.send(n, self.sums.at[self.region(n, stage - 1, bit)], self.ins[stage].at[self.brought(n, stage)], stage,
                  self.links[bit][1])

    def move(self, *ns):
        for n in ns:
            self.arrive(n)
            self.depart(n)


def halving_scratch(units, pieces):
    shapes = ((2, 2, 2, 2), (2, 2, 2), (2, 2), (2,), ())
    return [pltpu.VMEM((units, *s, 48, UNIT), BF) for s in shapes] + [
        pltpu.SemaphoreType.DMA((pieces, BITS + 1)), pltpu.SemaphoreType.DMA((pieces, BITS + 1))]


def weight_grad(places, left, right):
    value = dot_tn(left, right).astype(BF)
    for k, (ref, u) in enumerate(places):
        ref[u] = value[:, k * UNIT:(k + 1) * UNIT].reshape(2, 2, 2, 2, 48, UNIT)


def backward_kernel(
    sub, pieces, long_ref, short_ref, count_ref, tok_hbm, df_hbm, h_hbm, dr_hbm, g_hbm, d_hbm, n1_hbm, r1_hbm, qkv_hbm,
    a_hbm, lse_hbm, wc_hbm, w1p_hbm, w1o_hbm, w2p_hbm, w2o_hbm, wop_hbm, woo_hbm, gain_ref, grad2_ref,
    outer_ref, inner_ref, q_ref, k_ref, v_ref, output_ref, dx_out, vec_out,
    df_ref, h_ref, g_ref, slope_ref, w1_ref, w2_ref, dx_ref, n1_ref, r1_ref, x_ref, lse_ref, low_ref,
    grad_ref, vsend_ref, vec_ref, vin_ref, sums_ref, send_ref,
    in0_ref, in1_ref, in2_ref, in3_ref, in4_ref, s_sem, r_sem, vs_sem, vr_sem, load_sem, swap_sem,
):
    rows_all, d = dx_ref.shape
    width = w1_ref.shape[2]
    inner = a_hbm.shape[1] // 2
    pairs = inner // PAIR
    chunk = 2 * UNIT
    chunks = width // chunk
    half = halves()
    lengths = my_slots(long_ref, short_ref, count_ref)
    tensor = lax.axis_index("tensor")
    red = Halving(sub, pieces, sums_ref, send_ref, (in0_ref, in1_ref, in2_ref, in3_ref, in4_ref), s_sem, r_sem)
    red.greet()
    loads = Loads(load_sem)

    def fetch(*names):
        for name in names:
            kind, place = name[0], name[1:]
            if kind in "gw":
                k, c = int(place[0]), int(place[1])
                cols = pl.ds(c * chunk, chunk)
                if kind == "g":
                    loads(name, g_hbm.at[k, :, cols], g_ref.at[k, :, cols])
                else:
                    loads(name, (w2p_hbm, w2o_hbm)[k].at[cols], w2_ref.at[k, cols])
                    loads(name, d_hbm.at[k, :, cols], slope_ref.at[k, :, cols])
            elif kind == "i":
                loads("dr", (w1p_hbm, w1o_hbm)[int(place)], w1_ref.at[int(place)])
            elif name == "x":
                load_rows(loads, "x", tok_hbm, x_ref)
            else:
                src, dst = {
                    "df": (df_hbm, df_ref), "h": (h_hbm, h_ref), "dr": (dr_hbm, dx_ref), "norm": (n1_hbm, n1_ref),
                    "r": (r1_hbm, r1_ref), "lse": (lse_hbm, lse_ref)}[name]
                loads({"r": "norm", "lse": "heads"}.get(name, name), src, dst)

    fetch("df", "g00", "g10")

    def finish(*ns):
        for n in ns:
            units, cols, _ = pieces[n]
            values = red.arrive(n)
            for unit in range(units.start, units.stop):
                value = values[unit - units.start]
                if unit < 4:
                    outer_ref[:, unit * UNIT:(unit + 1) * UNIT] = value
                elif unit < 8:
                    inner_ref[:, (unit - 4) * UNIT:(unit - 3) * UNIT] = value
                elif unit == 8:
                    output_ref[...] = value
                else:
                    for i in range(cols.start // PAIR, cols.stop // PAIR):
                        at = i * PAIR - cols.start
                        (q_ref, k_ref, v_ref)[i][:, (unit - 9) * PAIR:(unit - 8) * PAIR] = value[:, at:at + PAIR]

    def tick(name):
        for n in PLAN.get(name, ()):
            if red.stage[n] == BITS:
                finish(n)
            else:
                red.move(n)

    loads.need("df")
    for c in range(chunks):
        cols = slice(c * chunk, (c + 1) * chunk)
        units = (2 * c, 2 * c + 1)
        loads.need(f"g0{c}")
        weight_grad([(send_ref, u % SENDS) for u in units], df_ref[...], g_ref[0, :, cols])
        if c == 0:
            red.meet()
        red.swap(units[0] % SENDS, units[0])
        fetch(*(("g01", "g11"), ("w10",))[c])
        tick(f"A{c}0")
        loads.need(f"g1{c}")
        fetch(*(("h", "w00"), ("w01",))[c])
        weight_grad([(sums_ref, u) for u in units], df_ref[...], g_ref[1, :, cols])
        tick(f"A{c}1")

    bias_sums = [[], []]
    loads.need("h")
    for c in range(chunks):
        cols = slice(c * chunk, (c + 1) * chunk)
        units = (4 + 2 * c, 5 + 2 * c)
        for k, out_ref in enumerate((send_ref, sums_ref)):
            loads.need(f"w{k}{c}")
            fetch(*{(0, 0): ("w11",), (0, 1): ("i0", "r"), (1, 0): ("i1", "dr"), (1, 1): ("norm", "lse")}[c, k])
            for n in range(c * chunk, (c + 1) * chunk, 256):
                part = slice(n, n + 256)
                slope = slope_ref[k, :, part].astype(F32)
                du = (dot_nt(df_ref[...], w2_ref[k, part, :]) * slope).astype(BF)
                slope_ref[k, :, part] = du
                bias_sums[k].append(column_sum(du.astype(F32)))
            tick(f"B{c}{k}u")
            places = [(out_ref, u if k else u % SENDS) for u in units]
            weight_grad(places, h_ref[...], slope_ref[k, :, cols])
            if k == 0:
                red.swap(units[0] % SENDS, units[0])
            tick(f"B{c}{k}w")
    a_ref, da_ref = h_ref, df_ref
    loads("heads", a_hbm, a_ref)
    for k in range(2):
        for p in range(pairs):
            loads("last", wc_hbm.at[k, :, p * 384:(p + 1) * 384],
                  w2_ref.at[p // 2, p % 2 * 768:(p % 2 + 1) * 768, k * 384:(k + 1) * 384])

    def wc(p):
        return w2_ref[p // 2, p % 2 * 768:(p % 2 + 1) * 768, :]

    def dqkv(p):
        return p // 2, slice(p % 2 * 768, (p % 2 + 1) * 768)

    loads.need("dr", "norm")
    grad_ref[...] = jnp.zeros_like(grad_ref)
    gain = gain_ref[...].reshape(1, -1)

    def first_norm(rows):
        e, normed = dx_ref[rows, :], n1_ref[rows, :]
        dr = norm_back(e, normed, r1_ref[rows, 0:1], gain)
        low = dr.astype(BF)
        dx_ref[rows, :] = dr
        low_ref[rows, :] = low
        grad_ref[0:1, :] += column_sum(low.astype(F32))
        grad_ref[1:2, :] += column_sum(e * normed)
        grad_ref[2:3, :] += column_sum(e)

    parts = [slice(i * rows_all // 2, (i + 1) * rows_all // 2) for i in range(2)]
    for i, rows in enumerate(parts):
        dx_ref[rows, :] += dot_nt(slope_ref[0, rows, :], w1_ref[0]) + dot_nt(slope_ref[1, rows, :], w1_ref[1])
        first_norm(rows)
        tick(f"C{i}")
    fetch("x")
    for k, wo_hbm in enumerate((wop_hbm, woo_hbm)):
        loads("wo", wo_hbm, w1_ref.at[0, k * inner:(k + 1) * inner, 0:d])
        loads("qkv", qkv_hbm.at[k], slope_ref.at[k, :, 0:3 * inner])
    loads.need("heads")
    weight_grad([(send_ref, 0), (sums_ref, 8)], low_ref[...], a_ref[...])
    red.swap(0, 8)
    tick("E")
    loads.need("wo")
    da_ref[...] = dot_nt(low_ref[...], w1_ref[0, :, 0:d]).astype(BF)
    tick("E2")
    loads.need("qkv", "x")

    slots = [slot_parts(kind, lengths) for kind in range(2)]

    def attention(p, k):
        at = k * inner + p * PAIR
        q_cols, k_cols, v_cols = (slice(p * 384 + j * 128, p * 384 + (j + 1) * 128) for j in range(3))

        def scores(kind, h):
            s, dp = [], []
            for rows, scale, key_bias in slots[kind]:
                q = slope_ref[k, rows, q_cols] * scale
                s.append(dot_nt(keep(half == h, q), slope_ref[k, rows, k_cols]) + key_bias)
                dp.append(dot_nt(keep(half == h, da_ref[rows, at:at + PAIR]), slope_ref[k, rows, v_cols]))
            return stack(s), stack(dp)

        def grads(kind, h, prob, ds):
            dq, dk, dv = [], [], []
            for i, (rows, scale, _) in enumerate(slots[kind]):
                count = rows.stop - rows.start
                part = slice(i * count, (i + 1) * count)
                dv.append(dot_tn(prob[part], keep(half == h, da_ref[rows, at:at + PAIR])))
                dk.append(dot_tn(ds[part], keep(half == h, slope_ref[k, rows, q_cols] * scale)))
                dq.append(dot(ds[part], keep(half == h, slope_ref[k, rows, k_cols] * scale)))
            return stack(dq), stack(dk), stack(dv)

        tasks = [(kind, h) for kind in range(2) for h in range(2)]
        ahead = scores(*tasks[0])
        held = None
        for i, (kind, h) in enumerate(tasks):
            s, dp = ahead
            if i + 1 < len(tasks):
                ahead = scores(*tasks[i + 1])
            rows = slice(slots[kind][0][0].start, slots[kind][-1][0].stop)
            product = da_ref[rows, at:at + PAIR].astype(F32) * a_ref[rows, at:at + PAIR].astype(F32)
            delta = jnp.sum(keep(half == h, product), axis=1, keepdims=True)
            lane = h * HEAD_DIM + p
            prob = jnp.exp(s - lse_ref[k, rows, lane:lane + 1])
            value = grads(kind, h, prob.astype(BF), (prob * (dp - delta)).astype(BF))
            if h == 0:
                held = value
                continue
            slot, cols = dqkv(p)
            for j in range(3):
                at_col = cols.start + k * 384 + j * 128
                g_ref[slot, rows, at_col:at_col + 128] = (held[j] + value[j]).astype(BF)

    for p in range(pairs):
        for k in range(2):
            attention(p, k)
            tick(f"F{p}{k}")
        slot, cols = dqkv(p)
        weight_grad([(send_ref, 1 + p), (sums_ref, 9 + p)], x_ref[...], g_ref[slot, :, cols])
        red.swap(1 + p, 9 + p)
        tick(f"F{p}w")

    for k, ref in enumerate((vsend_ref, vec_ref.at[0])):
        ref[...] = jnp.zeros(ref.shape, F32)
        ref[0:3, :] = grad_ref[0:3, :]
        ref[3:6, :] = grad2_ref[0:3, :]
        for n, sums in enumerate(bias_sums[k]):
            ref[6 + n // 3:7 + n // 3, n % 3 * 256:(n % 3 + 1) * 256] = sums
        for p in range(pairs):
            slot, cols = dqkv(p)
            sums = column_sum(g_ref[slot, :, cols.start + k * 384:cols.start + (k + 1) * 384].astype(F32))
            ref[8:9, p * PAIR:(p + 1) * PAIR] = sums[:, 0:128]
            ref[8:9, inner + p * PAIR:inner + (p + 1) * PAIR] = sums[:, 256:384]
    vnow = remote(vsend_ref, vin_ref.at[BITS], vs_sem.at[BITS], vr_sem.at[BITS], red.partner)
    vnow.start()
    loads.need("last")
    tick("vec")
    tile = 256
    span = rows_all // 2
    outs = []
    for i in range(rows_all // tile):
        rows = slice(i * tile, (i + 1) * tile)
        dx_ref[rows, :] += sum(dot_nt(g_ref[dqkv(p)[0], rows, dqkv(p)[1]], wc(p)) for p in range(pairs))
        if i * tile % span == span - tile:
            g = i * tile // span
            here = dx_ref.at[pl.ds(g * span, span)]
            there = dx_out.at[pl.ds(pl.multiple_of((2 * g + tensor) * span, span), span)]
            loads("dx", here, there)
            outs.append(remote(here, there, swap_sem.at[0, g], swap_sem.at[1, g], red.partner))
            outs[-1].start()
        if i < BITS:
            vnow.wait()
            if i == 0:
                vec_ref[0] = vec_ref[0] + vin_ref[BITS]
            else:
                vec_ref[i] = vec_ref[i - 1] + vin_ref[i - 1]
            vnow = remote(vec_ref.at[i], vin_ref.at[i], vs_sem.at[i], vr_sem.at[i], red.links[i][1])
            vnow.start()
        tick(f"G{i}")
    vnow.wait()
    vec_out[...] = vec_ref[BITS - 1] + vin_ref[BITS - 1]
    tick("end")
    for copy in outs:
        copy.wait()
    loads.drain()


def backward(sub, slots, tokens, df, h, dr, g, slope, n1, r1, qkv, a, lse, wc, w1, w2, wo, gain, grad2):
    rows, d = df.shape
    inner = a.shape[1] // 2
    ff = w1[0].shape[1]
    units = 2 * ff // UNIT + 1 + 3 * inner // UNIT
    pieces = [(slice(unit, unit + n), slice(first, last), order) for unit, n, first, last, order in PIECES]
    shape, vmem, dma = jax.ShapeDtypeStruct, pltpu.VMEM, pltpu.SemaphoreType.DMA
    return pl.pallas_call(
        functools.partial(backward_kernel, sub, pieces),
        out_shape=(
            shape((48, ff), F32), shape((48, ff), F32), shape((48, inner), F32), shape((48, inner), F32),
            shape((48, inner), F32), shape((48, inner), F32), shape((2 * rows, d), F32), shape((16, d), F32),
        ),
        in_specs=[SM, SM, SM] + [ANY] * 18 + [VM] * 2,
        out_specs=(VM, VM, VM, VM, VM, VM, ANY, VM),
        scratch_shapes=[
            vmem((rows, d), BF), vmem((rows, d), BF), vmem((2, rows, ff), BF), vmem((2, rows, ff), BF),
            vmem((2, d, ff), BF), vmem((2, ff, d), BF), vmem((rows, d), F32), vmem((rows, d), F32),
            vmem((rows, 128), F32), vmem((rows, d), BF), vmem((2, rows, PAIR), F32), vmem((rows, d), BF),
            vmem((8, d), F32), vmem((16, d), F32), vmem((BITS, 16, d), F32), vmem((BITS + 1, 16, d), F32),
            vmem((units, 2, 2, 2, 2, 48, UNIT), BF), vmem((SENDS, 2, 2, 2, 2, 48, UNIT), BF),
            *halving_scratch(units, len(pieces)), dma((BITS + 1,)), dma((BITS + 1,)), dma((48,)), dma((2, 2)),
        ],
        compiler_params=params(collective_id=1, has_side_effects=True),
        name="backward",
    )(*slots, tokens, df, h, dr, g, slope, n1, r1, qkv, a, lse, wc, *w1, *w2, *wo, gain, grad2)


def deliver_kernel(
    share, short_half, own_hbm, other_hbm, pool_own_ref, pool_other_ref, dx_hbm, total_ref, *refs,
):
    grads = refs[:6]
    result_out, pooled_out, dx_out = refs[6:9]
    grad_outs = refs[9:15]
    moved_out, bq_out, bv_out, b1_out, dx_ref, result_ref, sem = refs[15:]
    tensor = lax.axis_index("tensor")
    loads = Loads(sem)
    half = own_hbm.shape[0] // 2
    parts = 4 * half // 256
    moves = []
    for n in range(parts):
        rows = pl.ds(n * 256, 256)
        moves.append((dx_hbm.at[rows], dx_ref.at[rows], dx_out.at[rows]))
    for n, (hbm, place) in enumerate(((own_hbm, tensor), (other_hbm, 1 - tensor))):
        for k in range(2):
            here = pl.ds((2 * n + k) * half, half)
            moves.append((hbm.at[pl.ds(k * half, half)], result_ref.at[here],
                          result_out.at[pl.ds(pl.multiple_of((2 * k + place) * half, half), half)]))
    for n, (src, here, _) in enumerate(moves):
        loads(n, src, here)
    for src, dst in zip(grads, grad_outs):
        dst[...] = src[...]
    first = jnp.where(tensor == 0, pool_own_ref[...], pool_other_ref[...])
    second = jnp.where(tensor == 0, pool_other_ref[...], pool_own_ref[...])
    pooled_out[0:1, :] = first[0:1]
    pooled_out[1:2, :] = second[0:1]
    pooled_out[2:2 + short_half, :] = first[1:1 + short_half]
    pooled_out[2 + short_half:2 + 2 * short_half, :] = second[1:1 + short_half]
    total = total_ref[...]
    d = total.shape[1]
    start = lax.axis_index("dp") * share
    moved_out[...] = pltpu.roll(total[0:8, :], (d - start) % d, 1)
    inner = bq_out.shape[0]
    bq_out[...] = total[8, 0:inner]
    bv_out[...] = total[8, inner:2 * inner]
    b1_out[0:d] = total[6]
    b1_out[d:2 * d] = total[7]
    for n, (_, here, dst) in enumerate(moves):
        loads.need(n)
        loads("out", here, dst)
    loads.drain()


def deliver(own, other, pool_own, pool_other, dx, total, grads, share, inner, short_half):
    rows, d = own.shape
    shape = jax.ShapeDtypeStruct
    return pl.pallas_call(
        functools.partial(deliver_kernel, share, short_half),
        out_shape=(
            shape((2 * rows, d), BF), shape((2 + 2 * short_half, d), F32), shape((2 * rows, d), F32),
            *(shape(g.shape, F32) for g in grads), shape((8, d), F32),
            shape((inner,), F32), shape((inner,), F32), shape((2 * d,), F32),
        ),
        in_specs=[ANY, ANY, VM, VM, ANY, VM] + [VM] * 6,
        out_specs=(ANY, VM, ANY) + (VM,) * 10,
        scratch_shapes=[pltpu.VMEM(dx.shape, F32), pltpu.VMEM((2 * rows, d), BF), pltpu.SemaphoreType.DMA((32,))],
        compiler_params=params(),
        name="deliver",
    )(own, other, pool_own, pool_other, dx, total, *grads)


def per_device(
    dp_size, tokens, cotangent, long_lengths, short_lengths, live_counts, query_weight, query_bias, key_weight,
    value_weight, value_bias, output_weight, output_bias, attn_gain, attn_shift, inner_weight, inner_bias,
    outer_weight, outer_bias, ffn_gain, ffn_shift,
):
    d = tokens.shape[1]
    sub = dp_size // GROUPS
    slots = (long_lengths, short_lengths, live_counts)

    def swap(a):
        return lax.ppermute(a, "tensor", [(0, 1), (1, 0)])

    (qkv, a, lse, wc, wo_other, w1_other, w2_other, result, n1, r1, h, g, slope, df, dr, pooled, grad2) = forward(
        slots, tokens, cotangent,
        (query_weight, key_weight, value_weight, output_weight, inner_weight, outer_weight),
        (query_bias, value_bias, inner_bias),
        (output_bias, attn_gain, attn_shift, outer_bias, ffn_gain, ffn_shift))
    wo, w1, w2 = (wo_other, output_weight), (w1_other, inner_weight), (w2_other, outer_weight)
    result_other, pooled_other = swap(result), swap(pooled)
    *grads, dx, total = backward(
        sub, slots, tokens, df, h, dr, g, slope, n1, r1, qkv, a, lse, wc, w1, w2, wo, attn_gain, grad2)
    if sub > 1:
        groups = [[g * sub + i for i in range(sub)] for g in range(GROUPS)]
        grads = [lax.psum_scatter(g, "dp", scatter_dimension=0, axis_index_groups=groups, tiled=True) for g in grads]
        total = lax.psum(total, "dp", axis_index_groups=groups)
    (result_all, pooled_all, dx_all, d_outer, d_inner, d_q, d_k, d_v, d_output, moved, d_bq, d_bv, d_b1) = deliver(
        result, result_other, pooled, pooled_other, dx, total, grads, d // dp_size, query_weight.shape[1],
        short_lengths.shape[0] // 2)
    shards = [moved[k, :d // dp_size] for k in range(6)]
    return (
        result_all, pooled_all, dx_all, d_q, d_bq, d_k, d_v, d_bv, d_output.T, *shards[:3], d_inner, d_b1, d_outer.T,
        *shards[3:],
    )


def solution(mesh):
    in_specs = (
        P("dp", None), P("dp", None), P("dp"), P("dp"), P("dp", None), P(None, "tensor"), P("tensor"),
        P(None, "tensor"), P(None, "tensor"), P("tensor"), P("tensor", None), P(), P(), P(), P(None, "tensor"),
        P("tensor"), P("tensor", None), P(), P(), P(),
    )
    out_specs = (
        P("dp", None), P("dp", None), P("dp", None), P("dp", "tensor"), P("tensor"), P("dp", "tensor"),
        P("dp", "tensor"), P("tensor"), P("tensor", "dp"), P("dp"), P("dp"), P("dp"), P("dp", "tensor"),
        P("tensor"), P("tensor", "dp"), P("dp"), P("dp"), P("dp"),
    )
    return jax.shard_map(
        functools.partial(per_device, mesh.shape["dp"]), mesh=mesh, in_specs=in_specs, out_specs=out_specs,
        check_vma=False)
```

```python
import functools

import jax
import jax.numpy as jnp
from jax import lax
from jax.experimental import pallas as pl
from jax.experimental.pallas import tpu as pltpu
from jax.sharding import PartitionSpec as P

HEAD_DIM = 64
LONG = 512
SHORT = 128
PAIR = 128
NORM_EPS = 1e-12
MASKED = -1000000000.0
SCORE_SCALE = 0.125
INV_ROOT_TAU = 0.3989422804014327
ROOT_HALF = 0.7071067811865476
BF = jnp.bfloat16
F32 = jnp.float32
MESH = pl.DeviceIdType.MESH
UNIT = 384
BITS = 4
GROUPS = 1 << BITS

VM = pl.BlockSpec(memory_space=pltpu.VMEM)
SM = pl.BlockSpec(memory_space=pltpu.SMEM)
ANY = pl.BlockSpec(memory_space=pl.ANY)


def params(**more):
    return pltpu.CompilerParams(vmem_limit_bytes=62 << 20, **more)


def dot(a, b):
    return jnp.dot(a, b, preferred_element_type=F32)


def dot_nt(a, b):
    return lax.dot_general(a, b, (((1,), (1,)), ((), ())), preferred_element_type=F32)


def dot_tn(a, b):
    return lax.dot_general(a, b, (((0,), (0,)), ((), ())), preferred_element_type=F32)


def spans(start, unit, size=None):
    return pl.ds(pl.multiple_of(start, unit), unit if size is None else size)


def my_slots(long_ref, short_ref, count_ref):
    tensor = lax.axis_index("tensor")
    n_long, n_short = long_ref.shape[0] // 2, short_ref.shape[0] // 2
    lengths = []
    for ref, n, column in ((long_ref, n_long, 0), (short_ref, n_short, 1)):
        for j in range(n):
            slot = tensor * n + j
            lengths.append(jnp.where(slot < count_ref[0, column], ref[slot], 0))
    return lengths


def my_rows(whole_ref, mine_ref, sem):
    tensor = lax.axis_index("tensor")
    half = mine_ref.shape[0] // 2
    return [
        pltpu.make_async_copy(
            whole_ref.at[pl.ds(pl.multiple_of((2 * k + tensor) * half, half), half)],
            mine_ref.at[pl.ds(k * half, half)], sem.at[k])
        for k in range(2)
    ]


def key_terms(length, count):
    keys = lax.broadcasted_iota(jnp.int32, (1, count), 1)
    scale = jnp.where(length > 0, SCORE_SCALE, 0.0).astype(BF)
    bias = jnp.where((keys < length) | (length <= 0), 0.0, MASKED)
    return scale, bias


def halves():
    return lax.broadcasted_iota(jnp.int32, (1, PAIR), 1) // HEAD_DIM


class Loads:
    def __init__(self, sem):
        self.sem, self.count, self.open = sem, 0, {}

    def __call__(self, name, src, dst):
        copy = pltpu.make_async_copy(src, dst, self.sem.at[self.count])
        self.count += 1
        self.open.setdefault(name, []).append(copy)
        copy.start()

    def need(self, *names):
        for name in names:
            for copy in self.open.pop(name):
                copy.wait()

    def drain(self):
        self.need(*list(self.open))


def load_rows(loads, name, whole_ref, mine_ref):
    tensor = lax.axis_index("tensor")
    half = mine_ref.shape[0] // 2
    for k in range(2):
        loads(name, whole_ref.at[pl.ds(pl.multiple_of((2 * k + tensor) * half, half), half)],
              mine_ref.at[pl.ds(k * half, half)])


def slot_parts(kind, lengths):
    if kind == 0:
        return [(slice(0, LONG), *key_terms(lengths[0], LONG))]
    return [
        (slice(LONG + SHORT * s, LONG + SHORT * (s + 1)), *key_terms(length, SHORT))
        for s, length in enumerate(lengths[1:])]


def stack(values):
    return values[0] if len(values) == 1 else jnp.concatenate(values, axis=0)


def keep(own, value, other=None):
    return jnp.where(own, value, jnp.zeros_like(value) if other is None else other)


def norm(v, gain, shift):
    centre = v - jnp.mean(v, axis=-1, keepdims=True)
    inverse = lax.rsqrt(jnp.mean(centre * centre, axis=-1, keepdims=True) + NORM_EPS)
    normed = centre * inverse
    return normed * gain + shift, normed, inverse


def norm_back(e, normed, inverse, gain):
    scaled = e * gain
    plain = jnp.mean(scaled, axis=-1, keepdims=True)
    cross = jnp.mean(scaled * normed, axis=-1, keepdims=True)
    return inverse * (scaled - plain - normed * cross)


def gelu_terms(u):
    cdf = 0.5 + 0.5 * lax.erf(u * ROOT_HALF)
    return u * cdf, cdf + u * jnp.exp(-0.5 * u * u) * INV_ROOT_TAU


def column_sum(value):
    return jnp.sum(value, axis=0, keepdims=True)


def forward_kernel(
    long_ref, short_ref, count_ref, tok_hbm, cot_hbm, wq_hbm, wk_hbm, wv_hbm, wo_hbm, w1_hbm, w2_hbm,
    bq_ref, bv_ref, b1_ref, attn_bias_ref, a1_ref, s1_ref, ffn_bias_ref, a2_ref, s2_ref,
    qkv_out, a_out, lse_out, wc_out, wo_out, w1_out, w2_out, result_out, n1_out, r1_out, h_out, g_out, slope_out,
    df_out, dr_out, pooled_ref, grad_ref,
    x_ref, cot_ref, qkv_ref, a_ref, lse_ref, wc_ref, wo_ref, w1_ref, w2_ref, result_ref, n1_ref, r1_ref, h_ref, g_ref,
    slope_ref, df_ref, dr_ref, bq_other, bv_other, b1_other, load_sem, store_sem, s_sem, r_sem,
):
    rows_all, width = x_ref.shape[0], w1_ref.shape[2]
    pairs = qkv_ref.shape[2] // (3 * PAIR)
    inner = pairs * PAIR
    partner = {"tensor": 1 - lax.axis_index("tensor")}
    barrier = pltpu.get_barrier_semaphore()
    pl.semaphore_signal(barrier, inc=1, device_id=partner, device_id_type=MESH)
    loads, stores = Loads(load_sem), Loads(store_sem)
    load_rows(loads, "x", tok_hbm, x_ref)
    blocks = []
    for p in range(pairs):
        for j, w_hbm in enumerate((wq_hbm, wk_hbm, wv_hbm)):
            at = (3 * p + j) * PAIR
            blocks.append((w_hbm.at[:, p * PAIR:(p + 1) * PAIR], slice(at, at + PAIR)))
    for src, cols in blocks:
        loads("x", src, wc_ref.at[1, :, cols])
    lengths = my_slots(long_ref, short_ref, count_ref)
    half = halves()
    lane = lax.broadcasted_iota(jnp.int32, (1, PAIR), 1) % HEAD_DIM
    slots = [slot_parts(kind, lengths) for kind in range(2)]

    def project(k, bq, bv):
        parts = []
        for p in range(pairs):
            cols = slice(p * PAIR, (p + 1) * PAIR)
            parts += [bq[:, cols], jnp.zeros((1, PAIR), F32), bv[:, cols]]
        qkv_ref[k] = (dot(x_ref[...], wc_ref[k]) + jnp.concatenate(parts, axis=1)).astype(BF)
        stores("out", qkv_ref.at[k], qkv_out.at[k])
        stores("out", wc_ref.at[k], wc_out.at[k])

    def attention(k):
        def scores(kind, p, h):
            out = []
            for rows, scale, key_bias in slots[kind]:
                q = qkv_ref[k, rows, p * 384:p * 384 + 128] * scale
                out.append(dot_nt(keep(half == h, q), qkv_ref[k, rows, p * 384 + 128:p * 384 + 256]) + key_bias)
            return stack(out)

        def mix(kind, p, h, e):
            out = []
            for i, (rows, _, _) in enumerate(slots[kind]):
                v = qkv_ref[k, rows, p * 384 + 256:p * 384 + 384]
                count = rows.stop - rows.start
                out.append(dot(e[i * count:(i + 1) * count], keep(half == h, v, jnp.ones_like(v))))
            return stack(out)

        tasks = [(kind, p, h) for p in range(pairs) for kind in range(2) for h in range(2)]
        ahead = scores(*tasks[0])
        held = None
        for i, (kind, p, h) in enumerate(tasks):
            s = ahead
            if i + 1 < len(tasks):
                ahead = scores(*tasks[i + 1])
            high = jnp.max(s, axis=1, keepdims=True)
            mixed = mix(kind, p, h, jnp.exp(s - high).astype(BF))
            if h == 0:
                held = high, mixed
                continue
            rows = slice(slots[kind][0][0].start, slots[kind][-1][0].stop)
            total = pltpu.roll(jnp.where(half == 0, mixed, held[1]), HEAD_DIM, 1)
            at = k * inner + p * PAIR
            a_ref[rows, at:at + PAIR] = (jnp.where(half == 0, held[1], mixed) / total).astype(BF)
            lse = jnp.where(half == 0, held[0], high) + jnp.log(total)
            lse_ref[k, rows, :] = lse if p == 0 else jnp.where(lane == p, lse, lse_ref[k, rows, :])
        stores("out", lse_ref.at[k], lse_out.at[k])

    loads.need("x")
    project(1, bq_ref[...].reshape(1, -1), bv_ref[...].reshape(1, -1))
    pl.semaphore_wait(barrier, 1)
    swaps = []
    for src, dst in [(src, wc_ref.at[0, :, cols]) for src, cols in blocks] + [
            (bq_ref, bq_other), (bv_ref, bv_other), (b1_ref, b1_other), (wo_hbm, wo_ref.at[0:inner]),
            (w1_hbm, w1_ref.at[0]), (w2_hbm, w2_ref.at[0])]:
        n = len(swaps)
        swaps.append(remote(src, dst, s_sem.at[n], r_sem.at[n], partner))
        swaps[-1].start()
    loads("wo", wo_hbm, wo_ref.at[inner:2 * inner])
    loads("w1", w1_hbm, w1_ref.at[1])
    load_rows(loads, "tail", cot_hbm, cot_ref)
    loads("tail", w2_hbm, w2_ref.at[1])
    attention(1)
    for copy in swaps[:-4]:
        copy.wait()
    project(0, bq_other[...].reshape(1, -1), bv_other[...].reshape(1, -1))
    attention(0)
    for copy in swaps[-4:-2]:
        copy.wait()
    loads.need("wo", "w1")
    stores("out", a_ref, a_out)
    stores("out", wo_ref.at[0:inner], wo_out)

    attn_bias, a1, s1, ffn_bias, a2, s2 = (
        ref[...].reshape(1, -1) for ref in (attn_bias_ref, a1_ref, s1_ref, ffn_bias_ref, a2_ref, s2_ref))
    tile = 256
    for i in range(rows_all // tile):
        rows = slice(i * tile, (i + 1) * tile)
        attn = dot(a_ref[rows, :], wo_ref[...]) + attn_bias
        h1, normed, inverse = norm(x_ref[rows, :].astype(F32) + attn, a1, s1)
        n1_ref[rows, :] = normed
        r1_ref[rows, :] = jnp.broadcast_to(inverse, (tile, 128))
        h_ref[rows, :] = h1.astype(BF)
    for ref, out in ((n1_ref, n1_out), (r1_ref, r1_out), (h_ref, h_out)):
        stores("out", ref, out)

    tile, chunk = 128, 512
    for k, b_ref in ((1, b1_ref), (0, b1_other)):
        if k == 0:
            swaps[-2].wait()
            stores("out", w1_ref.at[0], w1_out)
        b1 = b_ref[...].reshape(1, -1)
        for c in range(width // chunk):
            cols = slice(c * chunk, (c + 1) * chunk)
            for i in range(rows_all // tile):
                rows = slice(i * tile, (i + 1) * tile)
                g, slope = gelu_terms(dot(h_ref[rows, :], w1_ref[k, :, cols]) + b1[:, cols])
                g_ref[k, rows, cols] = g.astype(BF)
                slope_ref[k, rows, cols] = slope.astype(BF)
        stores("out", g_ref.at[k], g_out.at[k])
        stores("out", slope_ref.at[k], slope_out.at[k])

    swaps[-1].wait()
    stores("out", w2_ref.at[0], w2_out)
    loads.need("tail")
    tile = 256
    grad_ref[...] = jnp.zeros_like(grad_ref)
    pooled_ref[...] = jnp.zeros_like(pooled_ref)
    for i in range(rows_all // tile):
        rows = slice(i * tile, (i + 1) * tile)
        ffn = dot(g_ref[0, rows, :], w2_ref[0]) + dot(g_ref[1, rows, :], w2_ref[1]) + ffn_bias
        y, normed, inverse = norm(n1_ref[rows, :] * a1 + s1 + ffn, a2, s2)
        result_ref[rows, :] = y.astype(BF)
        step = LONG if i * tile < LONG else SHORT
        for k in range(max(tile // step, 1)):
            start = i * tile + k * step
            slot = 0 if start < LONG else 1 + (start - LONG) // SHORT
            count = min(step, tile)
            place = (start if slot == 0 else 0) + lax.broadcasted_iota(jnp.int32, (count, 1), 0)
            part = y[k * count:(k + 1) * count, :]
            pooled_ref[slot:slot + 1, :] += column_sum(jnp.where(place < lengths[slot], part, 0.0))
        e = cot_ref[rows, :].astype(F32)
        dr = norm_back(e, normed, inverse, a2)
        low = dr.astype(BF)
        dr_ref[rows, :] = dr
        df_ref[rows, :] = low
        grad_ref[0:1, :] += column_sum(low.astype(F32))
        grad_ref[1:2, :] += column_sum(e * normed)
        grad_ref[2:3, :] += column_sum(e)
        for ref, out in ((result_ref, result_out), (df_ref, df_out), (dr_ref, dr_out)):
            stores("out", ref.at[rows], out.at[rows])
    for slot, length in enumerate(lengths):
        pooled_ref[slot:slot + 1, :] = pooled_ref[slot:slot + 1, :] / jnp.maximum(length, 1).astype(F32)
    stores.drain()


def forward(slots, tokens, cot, weights, biases, vectors):
    rows, d = tokens.shape[0] // 2, tokens.shape[1]
    inner, width = weights[0].shape[1], weights[4].shape[1]
    shape, vmem, dma = jax.ShapeDtypeStruct, pltpu.VMEM, pltpu.SemaphoreType.DMA
    row, row_f32 = ((rows, d), BF), ((rows, d), F32)
    qkv, a, lse, wc = ((2, rows, 3 * inner), BF), ((rows, 2 * inner), BF), ((2, rows, PAIR), F32), ((2, d, 3 * inner), BF)
    hidden, r1 = ((2, rows, width), BF), ((rows, 128), F32)
    outs = [qkv, a, lse, wc, *((w.shape, BF) for w in weights[3:]), row, row_f32, r1, row, hidden, hidden, row, row_f32,
            ((8, d), F32), ((8, d), F32)]
    scratch = [row, row, qkv, a, lse, wc, ((2 * inner, d), BF), ((2, d, width), BF), ((2, width, d), BF), row, row_f32, r1,
               row, hidden, hidden, row, row_f32, *((b.shape, F32) for b in biases)]
    return pl.pallas_call(
        forward_kernel,
        out_shape=[shape(*o) for o in outs],
        in_specs=[SM, SM, SM] + [ANY] * 8 + [VM] * 9,
        out_specs=[ANY] * 15 + [VM] * 2,
        scratch_shapes=[*(vmem(*s) for s in scratch), dma((20,)), dma((40,)), dma((16,)), dma((16,))],
        compiler_params=params(collective_id=3, has_side_effects=True),
        name="forward",
    )(*slots, tokens, cot, *weights, *biases, *vectors)


def peer(sub, bit):
    me = lax.axis_index("dp")
    group = me // sub
    value = (group // (1 << bit)) % 2
    other = me + (1 - 2 * value) * (sub << bit)
    return value, {"dp": other}


def remote(src, dst, s, r, device):
    return pltpu.make_async_remote_copy(
        src_ref=src, dst_ref=dst, send_sem=s, recv_sem=r, device_id=device, device_id_type=MESH)


SENDS = 4
PIECES = (
    (0, 2, 0, 384, (1, 0, 3, 2)),
    (2, 2, 0, 384, (0, 2, 1, 3)),
    (4, 2, 0, 384, (2, 1, 0, 3)),
    (6, 2, 0, 384, (1, 2, 0, 3)),
    (8, 1, 0, 384, (0, 1, 3, 2)),
    (9, 1, 0, 384, (0, 2, 1, 3)),
    (10, 1, 0, 384, (1, 0, 2, 3)),
    (11, 1, 0, 128, (2, 1, 0, 3)),
    (11, 1, 128, 256, (1, 0, 2, 3)),
    (11, 1, 256, 384, (1, 0, 3, 2)),
)
VECTORS = -1
PLAN = {
    "A11": (0,),
    "B00w": (1,),
    "B10u": (2,),
    "C0": (0, 3,),
    "C1": (1,),
    "F00": (0, 2, 4,),
    "F0w": (1,),
    "F10": (3, 5,),
    "F11": (0, 4, 2,),
    "F20": (1, 6,),
    "F21": (0, 3, 4, 5,),
    "F2w": (2,),
    "vec": (1, 7, 8,),
    "G0": (9, 6, 3,),
    "G1": (4, 5, -1,),
    "G2": (8,),
    "end": (9, -1, 7, 2, 6, 5, 8, -1, 4, 9, 7, 3, 6, -1, 8, 7, 5, 9, 6, 8, -1, 7, 9,),
}


class Halving:
    def __init__(self, sub, pieces, sums, sends, ins, s_sem, r_sem):
        self.links = [peer(sub, bit) for bit in range(BITS)]
        self.partner = {"tensor": 1 - lax.axis_index("tensor")}
        self.pieces, self.sums, self.sends, self.ins = pieces, sums, sends, ins
        self.s_sem, self.r_sem = s_sem, r_sem
        self.stage = {}
        self.copy = {}

    def greet(self):
        barrier = pltpu.get_barrier_semaphore()
        for device in [self.partner] + [link[1] for link in self.links]:
            pl.semaphore_signal(barrier, inc=1, device_id=device, device_id_type=MESH)

    def meet(self):
        pl.semaphore_wait(pltpu.get_barrier_semaphore(), BITS + 1)

    def region(self, n, count, bit=None):
        units, cols, order = self.pieces[n]
        fixed = order[:count]
        index = [units]
        for b in reversed(range(BITS)):
            value = self.links[b][0]
            index.append(value if b in fixed else 1 - value if b == bit else slice(None))
        return (*index, slice(None), cols)

    def brought(self, n, stage):
        units, cols, _ = self.pieces[n]
        return (units, *([slice(None)] * (BITS - stage)), slice(None), cols)

    def send(self, n, src, dst, stage, device):
        self.copy[n] = remote(src, dst, self.s_sem.at[n, stage], self.r_sem.at[n, stage], device)
        self.copy[n].start()
        self.stage[n] = stage

    def swap(self, slot, unit):
        for n, (units, cols, _) in enumerate(self.pieces):
            if units.start == unit:
                out = slice(slot, slot + units.stop - units.start)
                self.send(n, self.sends.at[(out, *([slice(None)] * (BITS + 1)), cols)],
                          self.ins[0].at[self.brought(n, 0)], 0, self.partner)

    def arrive(self, n):
        stage = self.stage[n]
        self.copy[n].wait()
        index = self.region(n, stage)
        brought = self.ins[stage][self.brought(n, stage)]
        if stage == BITS:
            return self.sums[index].astype(F32) + brought.astype(F32)
        self.sums[index] = self.sums[index] + brought
        return None

    def depart(self, n):
        stage = self.stage[n] + 1
        bit = self.pieces[n][2][stage - 1]
        self.send(n, self.sums.at[self.region(n, stage - 1, bit)], self.ins[stage].at[self.brought(n, stage)], stage,
                  self.links[bit][1])

    def move(self, *ns):
        for n in ns:
            self.arrive(n)
            self.depart(n)


def halving_scratch(units, pieces):
    shapes = ((2, 2, 2, 2), (2, 2, 2), (2, 2), (2,), ())
    return [pltpu.VMEM((units, *s, 48, UNIT), BF) for s in shapes] + [
        pltpu.SemaphoreType.DMA((pieces, BITS + 1)), pltpu.SemaphoreType.DMA((pieces, BITS + 1))]


def weight_grad(places, left, right):
    value = dot_tn(left, right).astype(BF)
    for k, (ref, u) in enumerate(places):
        ref[u] = value[:, k * UNIT:(k + 1) * UNIT].reshape(2, 2, 2, 2, 48, UNIT)


def backward_kernel(
    sub, pieces, long_ref, short_ref, count_ref, tok_hbm, df_hbm, h_hbm, dr_hbm, g_hbm, d_hbm, n1_hbm, r1_hbm, qkv_hbm,
    a_hbm, lse_hbm, wc_hbm, w1p_hbm, w1o_hbm, w2p_hbm, w2o_hbm, wop_hbm, woo_hbm, gain_ref, grad2_ref,
    outer_ref, inner_ref, q_ref, k_ref, v_ref, output_ref, dx_out, vec_out,
    df_ref, h_ref, g_ref, slope_ref, w1_ref, w2_ref, dx_ref, n1_ref, r1_ref, x_ref, lse_ref, low_ref,
    grad_ref, vsend_ref, vec_ref, vin_ref, sums_ref, send_ref,
    in0_ref, in1_ref, in2_ref, in3_ref, in4_ref, s_sem, r_sem, vs_sem, vr_sem, load_sem, swap_sem,
):
    rows_all, d = dx_ref.shape
    width = w1_ref.shape[2]
    inner = a_hbm.shape[1] // 2
    pairs = inner // PAIR
    chunk = 2 * UNIT
    chunks = width // chunk
    half = halves()
    lengths = my_slots(long_ref, short_ref, count_ref)
    tensor = lax.axis_index("tensor")
    red = Halving(sub, pieces, sums_ref, send_ref, (in0_ref, in1_ref, in2_ref, in3_ref, in4_ref), s_sem, r_sem)
    red.greet()
    loads = Loads(load_sem)

    def fetch(*names):
        for name in names:
            kind, place = name[0], name[1:]
            if kind in "gw":
                k, c = int(place[0]), int(place[1])
                cols = pl.ds(c * chunk, chunk)
                if kind == "g":
                    loads(name, g_hbm.at[k, :, cols], g_ref.at[k, :, cols])
                else:
                    loads(name, (w2p_hbm, w2o_hbm)[k].at[cols], w2_ref.at[k, cols])
                    loads(name, d_hbm.at[k, :, cols], slope_ref.at[k, :, cols])
            elif kind == "i":
                loads("dr", (w1p_hbm, w1o_hbm)[int(place)], w1_ref.at[int(place)])
            elif name == "x":
                load_rows(loads, "x", tok_hbm, x_ref)
            else:
                src, dst = {
                    "df": (df_hbm, df_ref), "h": (h_hbm, h_ref), "dr": (dr_hbm, dx_ref), "norm": (n1_hbm, n1_ref),
                    "r": (r1_hbm, r1_ref), "lse": (lse_hbm, lse_ref)}[name]
                loads({"r": "norm", "lse": "heads"}.get(name, name), src, dst)

    fetch("df", "g00", "g10")

    def finish(*ns):
        for n in ns:
            units, cols, _ = pieces[n]
            values = red.arrive(n)
            for unit in range(units.start, units.stop):
                value = values[unit - units.start]
                if unit < 4:
                    outer_ref[:, unit * UNIT:(unit + 1) * UNIT] = value
                elif unit < 8:
                    inner_ref[:, (unit - 4) * UNIT:(unit - 3) * UNIT] = value
                elif unit == 8:
                    output_ref[...] = value
                else:
                    for i in range(cols.start // PAIR, cols.stop // PAIR):
                        at = i * PAIR - cols.start
                        (q_ref, k_ref, v_ref)[i][:, (unit - 9) * PAIR:(unit - 8) * PAIR] = value[:, at:at + PAIR]

    vector_copies = []

    def vector_step():
        step = len(vector_copies)
        if step:
            vector_copies[-1].wait()
        if step == 1:
            vec_ref[0] = vec_ref[0] + vin_ref[BITS]
        elif step == BITS + 1:
            vec_out[...] = vec_ref[BITS - 1] + vin_ref[BITS - 1]
            return
        elif step:
            vec_ref[step - 1] = vec_ref[step - 2] + vin_ref[step - 2]
        if step == 0:
            src, slot, device = vsend_ref, BITS, red.partner
        else:
            src, slot, device = vec_ref.at[step - 1], step - 1, red.links[step - 1][1]
        vector_copies.append(remote(src, vin_ref.at[slot], vs_sem.at[slot], vr_sem.at[slot], device))
        vector_copies[-1].start()

    def tick(name):
        for n in PLAN.get(name, ()):
            if n == VECTORS:
                vector_step()
            elif red.stage[n] == BITS:
                finish(n)
            else:
                red.move(n)

    loads.need("df")
    for c in range(chunks):
        cols = slice(c * chunk, (c + 1) * chunk)
        units = (2 * c, 2 * c + 1)
        loads.need(f"g0{c}")
        weight_grad([(send_ref, u % SENDS) for u in units], df_ref[...], g_ref[0, :, cols])
        if c == 0:
            red.meet()
        red.swap(units[0] % SENDS, units[0])
        fetch(*(("g01", "g11"), ("w10",))[c])
        tick(f"A{c}0")
        loads.need(f"g1{c}")
        fetch(*(("h", "w00"), ("w01",))[c])
        weight_grad([(sums_ref, u) for u in units], df_ref[...], g_ref[1, :, cols])
        tick(f"A{c}1")

    bias_sums = [[], []]
    loads.need("h")
    for c in range(chunks):
        cols = slice(c * chunk, (c + 1) * chunk)
        units = (4 + 2 * c, 5 + 2 * c)
        for k, out_ref in enumerate((send_ref, sums_ref)):
            loads.need(f"w{k}{c}")
            fetch(*{(0, 0): ("w11",), (0, 1): ("i0", "r"), (1, 0): ("i1", "dr"), (1, 1): ("norm", "lse")}[c, k])
            for n in range(c * chunk, (c + 1) * chunk, 256):
                part = slice(n, n + 256)
                slope = slope_ref[k, :, part].astype(F32)
                du = (dot_nt(df_ref[...], w2_ref[k, part, :]) * slope).astype(BF)
                slope_ref[k, :, part] = du
                bias_sums[k].append(column_sum(du.astype(F32)))
            tick(f"B{c}{k}u")
            places = [(out_ref, u if k else u % SENDS) for u in units]
            weight_grad(places, h_ref[...], slope_ref[k, :, cols])
            if k == 0:
                red.swap(units[0] % SENDS, units[0])
            tick(f"B{c}{k}w")
    a_ref, da_ref = h_ref, df_ref
    loads("heads", a_hbm, a_ref)
    for k in range(2):
        for p in range(pairs):
            loads("last", wc_hbm.at[k, :, p * 384:(p + 1) * 384],
                  w2_ref.at[p // 2, p % 2 * 768:(p % 2 + 1) * 768, k * 384:(k + 1) * 384])

    def wc(p):
        return w2_ref[p // 2, p % 2 * 768:(p % 2 + 1) * 768, :]

    def dqkv(p):
        return p // 2, slice(p % 2 * 768, (p % 2 + 1) * 768)

    loads.need("dr", "norm")
    grad_ref[...] = jnp.zeros_like(grad_ref)
    gain = gain_ref[...].reshape(1, -1)

    def first_norm(rows):
        e, normed = dx_ref[rows, :], n1_ref[rows, :]
        dr = norm_back(e, normed, r1_ref[rows, 0:1], gain)
        low = dr.astype(BF)
        dx_ref[rows, :] = dr
        low_ref[rows, :] = low
        grad_ref[0:1, :] += column_sum(low.astype(F32))
        grad_ref[1:2, :] += column_sum(e * normed)
        grad_ref[2:3, :] += column_sum(e)

    parts = [slice(i * rows_all // 2, (i + 1) * rows_all // 2) for i in range(2)]
    for i, rows in enumerate(parts):
        dx_ref[rows, :] += dot_nt(slope_ref[0, rows, :], w1_ref[0]) + dot_nt(slope_ref[1, rows, :], w1_ref[1])
        first_norm(rows)
        tick(f"C{i}")
    fetch("x")
    for k, wo_hbm in enumerate((wop_hbm, woo_hbm)):
        loads("wo", wo_hbm, w1_ref.at[0, k * inner:(k + 1) * inner, 0:d])
        loads("qkv", qkv_hbm.at[k], slope_ref.at[k, :, 0:3 * inner])
    loads.need("heads")
    weight_grad([(send_ref, 0), (sums_ref, 8)], low_ref[...], a_ref[...])
    red.swap(0, 8)
    tick("E")
    loads.need("wo")
    da_ref[...] = dot_nt(low_ref[...], w1_ref[0, :, 0:d]).astype(BF)
    tick("E2")
    loads.need("qkv", "x")

    slots = [slot_parts(kind, lengths) for kind in range(2)]

    def attention(p, k):
        at = k * inner + p * PAIR
        q_cols, k_cols, v_cols = (slice(p * 384 + j * 128, p * 384 + (j + 1) * 128) for j in range(3))

        def scores(kind, h):
            s, dp = [], []
            for rows, scale, key_bias in slots[kind]:
                q = slope_ref[k, rows, q_cols] * scale
                s.append(dot_nt(keep(half == h, q), slope_ref[k, rows, k_cols]) + key_bias)
                dp.append(dot_nt(keep(half == h, da_ref[rows, at:at + PAIR]), slope_ref[k, rows, v_cols]))
            return stack(s), stack(dp)

        def grads(kind, h, prob, ds):
            dq, dk, dv = [], [], []
            for i, (rows, scale, _) in enumerate(slots[kind]):
                count = rows.stop - rows.start
                part = slice(i * count, (i + 1) * count)
                dv.append(dot_tn(prob[part], keep(half == h, da_ref[rows, at:at + PAIR])))
                dk.append(dot_tn(ds[part], keep(half == h, slope_ref[k, rows, q_cols] * scale)))
                dq.append(dot(ds[part], keep(half == h, slope_ref[k, rows, k_cols] * scale)))
            return stack(dq), stack(dk), stack(dv)

        tasks = [(kind, h) for kind in range(2) for h in range(2)]
        ahead = scores(*tasks[0])
        held = None
        for i, (kind, h) in enumerate(tasks):
            s, dp = ahead
            if i + 1 < len(tasks):
                ahead = scores(*tasks[i + 1])
            rows = slice(slots[kind][0][0].start, slots[kind][-1][0].stop)
            product = da_ref[rows, at:at + PAIR].astype(F32) * a_ref[rows, at:at + PAIR].astype(F32)
            delta = jnp.sum(keep(half == h, product), axis=1, keepdims=True)
            lane = h * HEAD_DIM + p
            prob = jnp.exp(s - lse_ref[k, rows, lane:lane + 1])
            value = grads(kind, h, prob.astype(BF), (prob * (dp - delta)).astype(BF))
            if h == 0:
                held = value
                continue
            slot, cols = dqkv(p)
            for j in range(3):
                at_col = cols.start + k * 384 + j * 128
                g_ref[slot, rows, at_col:at_col + 128] = (held[j] + value[j]).astype(BF)

    for p in range(pairs):
        for k in range(2):
            attention(p, k)
            tick(f"F{p}{k}")
        slot, cols = dqkv(p)
        weight_grad([(send_ref, 1 + p), (sums_ref, 9 + p)], x_ref[...], g_ref[slot, :, cols])
        red.swap(1 + p, 9 + p)
        tick(f"F{p}w")

    for k, ref in enumerate((vsend_ref, vec_ref.at[0])):
        ref[...] = jnp.zeros(ref.shape, F32)
        ref[0:3, :] = grad_ref[0:3, :]
        ref[3:6, :] = grad2_ref[0:3, :]
        for n, sums in enumerate(bias_sums[k]):
            ref[6 + n // 3:7 + n // 3, n % 3 * 256:(n % 3 + 1) * 256] = sums
        for p in range(pairs):
            slot, cols = dqkv(p)
            sums = column_sum(g_ref[slot, :, cols.start + k * 384:cols.start + (k + 1) * 384].astype(F32))
            ref[8:9, p * PAIR:(p + 1) * PAIR] = sums[:, 0:128]
            ref[8:9, inner + p * PAIR:inner + (p + 1) * PAIR] = sums[:, 256:384]
    vector_step()
    loads.need("last")
    tick("vec")
    tile = 256
    span = rows_all // 2
    outs = []
    for i in range(rows_all // tile):
        rows = slice(i * tile, (i + 1) * tile)
        dx_ref[rows, :] += sum(dot_nt(g_ref[dqkv(p)[0], rows, dqkv(p)[1]], wc(p)) for p in range(pairs))
        if i * tile % span == span - tile:
            g = i * tile // span
            here = dx_ref.at[pl.ds(g * span, span)]
            there = dx_out.at[pl.ds(pl.multiple_of((2 * g + tensor) * span, span), span)]
            loads("dx", here, there)
            outs.append(remote(here, there, swap_sem.at[0, g], swap_sem.at[1, g], red.partner))
            outs[-1].start()
        tick(f"G{i}")
    tick("end")
    for copy in outs:
        copy.wait()
    loads.drain()


def backward(sub, slots, tokens, df, h, dr, g, slope, n1, r1, qkv, a, lse, wc, w1, w2, wo, gain, grad2):
    rows, d = df.shape
    inner = a.shape[1] // 2
    ff = w1[0].shape[1]
    units = 2 * ff // UNIT + 1 + 3 * inner // UNIT
    pieces = [(slice(unit, unit + n), slice(first, last), order) for unit, n, first, last, order in PIECES]
    shape, vmem, dma = jax.ShapeDtypeStruct, pltpu.VMEM, pltpu.SemaphoreType.DMA
    return pl.pallas_call(
        functools.partial(backward_kernel, sub, pieces),
        out_shape=(
            shape((48, ff), F32), shape((48, ff), F32), shape((48, inner), F32), shape((48, inner), F32),
            shape((48, inner), F32), shape((48, inner), F32), shape((2 * rows, d), F32), shape((16, d), F32),
        ),
        in_specs=[SM, SM, SM] + [ANY] * 18 + [VM] * 2,
        out_specs=(VM, VM, VM, VM, VM, VM, ANY, VM),
        scratch_shapes=[
            vmem((rows, d), BF), vmem((rows, d), BF), vmem((2, rows, ff), BF), vmem((2, rows, ff), BF),
            vmem((2, d, ff), BF), vmem((2, ff, d), BF), vmem((rows, d), F32), vmem((rows, d), F32),
            vmem((rows, 128), F32), vmem((rows, d), BF), vmem((2, rows, PAIR), F32), vmem((rows, d), BF),
            vmem((8, d), F32), vmem((16, d), F32), vmem((BITS, 16, d), F32), vmem((BITS + 1, 16, d), F32),
            vmem((units, 2, 2, 2, 2, 48, UNIT), BF), vmem((SENDS, 2, 2, 2, 2, 48, UNIT), BF),
            *halving_scratch(units, len(pieces)), dma((BITS + 1,)), dma((BITS + 1,)), dma((48,)), dma((2, 2)),
        ],
        compiler_params=params(collective_id=1, has_side_effects=True),
        name="backward",
    )(*slots, tokens, df, h, dr, g, slope, n1, r1, qkv, a, lse, wc, *w1, *w2, *wo, gain, grad2)


def deliver_kernel(
    share, short_half, own_hbm, other_hbm, pool_own_ref, pool_other_ref, dx_hbm, total_ref, *refs,
):
    grads = refs[:6]
    result_out, pooled_out, dx_out = refs[6:9]
    grad_outs = refs[9:15]
    moved_out, bq_out, bv_out, b1_out, dx_ref, result_ref, sem = refs[15:]
    tensor = lax.axis_index("tensor")
    loads = Loads(sem)
    half = own_hbm.shape[0] // 2
    parts = 4 * half // 256
    moves = []
    for n in range(parts):
        rows = pl.ds(n * 256, 256)
        moves.append((dx_hbm.at[rows], dx_ref.at[rows], dx_out.at[rows]))
    for n, (hbm, place) in enumerate(((own_hbm, tensor), (other_hbm, 1 - tensor))):
        for k in range(2):
            here = pl.ds((2 * n + k) * half, half)
            moves.append((hbm.at[pl.ds(k * half, half)], result_ref.at[here],
                          result_out.at[pl.ds(pl.multiple_of((2 * k + place) * half, half), half)]))
    for n, (src, here, _) in enumerate(moves):
        loads(n, src, here)
    for src, dst in zip(grads, grad_outs):
        dst[...] = src[...]
    first = jnp.where(tensor == 0, pool_own_ref[...], pool_other_ref[...])
    second = jnp.where(tensor == 0, pool_other_ref[...], pool_own_ref[...])
    pooled_out[0:1, :] = first[0:1]
    pooled_out[1:2, :] = second[0:1]
    pooled_out[2:2 + short_half, :] = first[1:1 + short_half]
    pooled_out[2 + short_half:2 + 2 * short_half, :] = second[1:1 + short_half]
    total = total_ref[...]
    d = total.shape[1]
    start = lax.axis_index("dp") * share
    moved_out[...] = pltpu.roll(total[0:8, :], (d - start) % d, 1)
    inner = bq_out.shape[0]
    bq_out[...] = total[8, 0:inner]
    bv_out[...] = total[8, inner:2 * inner]
    b1_out[0:d] = total[6]
    b1_out[d:2 * d] = total[7]
    for n, (_, here, dst) in enumerate(moves):
        loads.need(n)
        loads("out", here, dst)
    loads.drain()


def deliver(own, other, pool_own, pool_other, dx, total, grads, share, inner, short_half):
    rows, d = own.shape
    shape = jax.ShapeDtypeStruct
    return pl.pallas_call(
        functools.partial(deliver_kernel, share, short_half),
        out_shape=(
            shape((2 * rows, d), BF), shape((2 + 2 * short_half, d), F32), shape((2 * rows, d), F32),
            *(shape(g.shape, F32) for g in grads), shape((8, d), F32),
            shape((inner,), F32), shape((inner,), F32), shape((2 * d,), F32),
        ),
        in_specs=[ANY, ANY, VM, VM, ANY, VM] + [VM] * 6,
        out_specs=(ANY, VM, ANY) + (VM,) * 10,
        scratch_shapes=[pltpu.VMEM(dx.shape, F32), pltpu.VMEM((2 * rows, d), BF), pltpu.SemaphoreType.DMA((32,))],
        compiler_params=params(),
        name="deliver",
    )(own, other, pool_own, pool_other, dx, total, *grads)


def per_device(
    dp_size, tokens, cotangent, long_lengths, short_lengths, live_counts, query_weight, query_bias, key_weight,
    value_weight, value_bias, output_weight, output_bias, attn_gain, attn_shift, inner_weight, inner_bias,
    outer_weight, outer_bias, ffn_gain, ffn_shift,
):
    d = tokens.shape[1]
    sub = dp_size // GROUPS
    slots = (long_lengths, short_lengths, live_counts)

    def swap(a):
        return lax.ppermute(a, "tensor", [(0, 1), (1, 0)])

    (qkv, a, lse, wc, wo_other, w1_other, w2_other, result, n1, r1, h, g, slope, df, dr, pooled, grad2) = forward(
        slots, tokens, cotangent,
        (query_weight, key_weight, value_weight, output_weight, inner_weight, outer_weight),
        (query_bias, value_bias, inner_bias),
        (output_bias, attn_gain, attn_shift, outer_bias, ffn_gain, ffn_shift))
    wo, w1, w2 = (wo_other, output_weight), (w1_other, inner_weight), (w2_other, outer_weight)
    result_other, pooled_other = swap(result), swap(pooled)
    *grads, dx, total = backward(
        sub, slots, tokens, df, h, dr, g, slope, n1, r1, qkv, a, lse, wc, w1, w2, wo, attn_gain, grad2)
    if sub > 1:
        groups = [[g * sub + i for i in range(sub)] for g in range(GROUPS)]
        grads = [lax.psum_scatter(g, "dp", scatter_dimension=0, axis_index_groups=groups, tiled=True) for g in grads]
        total = lax.psum(total, "dp", axis_index_groups=groups)
    (result_all, pooled_all, dx_all, d_outer, d_inner, d_q, d_k, d_v, d_output, moved, d_bq, d_bv, d_b1) = deliver(
        result, result_other, pooled, pooled_other, dx, total, grads, d // dp_size, query_weight.shape[1],
        short_lengths.shape[0] // 2)
    shards = [moved[k, :d // dp_size] for k in range(6)]
    return (
        result_all, pooled_all, dx_all, d_q, d_bq, d_k, d_v, d_bv, d_output.T, *shards[:3], d_inner, d_b1, d_outer.T,
        *shards[3:],
    )


def solution(mesh):
    in_specs = (
        P("dp", None), P("dp", None), P("dp"), P("dp"), P("dp", None), P(None, "tensor"), P("tensor"),
        P(None, "tensor"), P(None, "tensor"), P("tensor"), P("tensor", None), P(), P(), P(), P(None, "tensor"),
        P("tensor"), P("tensor", None), P(), P(), P(),
    )
    out_specs = (
        P("dp", None), P("dp", None), P("dp", None), P("dp", "tensor"), P("tensor"), P("dp", "tensor"),
        P("dp", "tensor"), P("tensor"), P("tensor", "dp"), P("dp"), P("dp"), P("dp"), P("dp", "tensor"),
        P("tensor"), P("tensor", "dp"), P("dp"), P("dp"), P("dp"),
    )
    return jax.shard_map(
        functools.partial(per_device, mesh.shape["dp"]), mesh=mesh, in_specs=in_specs, out_specs=out_specs,
        check_vma=False)
```
